32 devices in a mesh: mp: 4 (over z), dp: 8 (over y, x, core).
Axes of the slice: x: 2, y: 2, z: 4, core: 2. Of those that a mesh axis runs over, the one named last changes fastest.
Arguments:
- tokens: bfloat16 [32768, 768], P(('mp', 'dp')), may hold values from -6 to 6
- segment_ids: int32 [32768], P(('mp', 'dp')), may hold values from 0 to 64, as said below
- cotangent: float32 [32768, 768], P(('mp', 'dp')), may hold values from -6 to 6
- gain_one: bfloat16 [768], replicated, may hold values from 0.25 to 1.75
- w_qkv: bfloat16 [768, 2304], P('mp', 'dp'), may hold values from -0.21875 to 0.21875
- w_out: bfloat16 [768, 768], P('mp', 'dp'), may hold values from -0.875 to 0.875
- rel_table: bfloat16 [32, 12], replicated, may hold values from -4 to 4
- gain_two: bfloat16 [768], replicated, may hold values from 0.25 to 1.75
- w_in: bfloat16 [768, 3072], P('mp', 'dp'), may hold values from -0.21875 to 0.21875
- w_back: bfloat16 [768, 3072], P('mp', 'dp'), may hold values from -0.109375 to 0.109375
Outputs:
- layer_out: bfloat16 [32768, 768], P(('mp', 'dp'))
- tokens_grad: float32 [32768, 768], P(('mp', 'dp'))
- gain_one_grad: float32 [768], replicated
- w_qkv_grad: float32 [768, 2304], P('mp', 'dp')
- w_out_grad: float32 [768, 768], P('mp', 'dp')
- rel_table_grad: float32 [32, 12], replicated
- gain_two_grad: float32 [768], replicated
- w_in_grad: float32 [768, 3072], P('mp', 'dp')
- w_back_grad: float32 [768, 3072], P('mp', 'dp')
The draws below stay inside these ranges and needn't reach their ends.
Inputs may be any that keep to these rules, and one draw needn't show every extreme that they name: `segment_ids`: in each packed sequence of 512 tokens the ids start at 1 on its first token and never fall; a document is a run of equal nonzero ids; 0 marks padding, which fills the last tokens of every sequence, at least one of them.
All inputs are finite; a program needn't handle non-finite values.
Results may differ from the reference program's by a relative error of at most 0.013.
Values may be sent and summed in bfloat16 or wider, within the bound.
A program may use at most 192 MiB of HBM per device.

```python
import math
import jax
import jax.numpy as jnp
from jax import lax

D = 768
H = 12
HD = 64
FF = 3072
BUCKETS = 32
SEQ = 512
TOKENS = 32768


def draw_segment_ids(key, part):
    key = jax.random.fold_in(key, 7)
    start_key, padding_key, chosen_key = jax.random.split(key, 3)
    sequences = TOKENS // SEQ
    starts = (jax.random.randint(start_key, (sequences, SEQ), 0, 48) == 0).astype(jnp.int32)
    places = lax.broadcasted_iota(jnp.int32, (sequences, SEQ), 1)
    which = lax.broadcasted_iota(jnp.int32, (sequences, SEQ), 0)
    chosen = jax.random.randint(chosen_key, (), 0, sequences)
    forced = (which == chosen) & (places < SEQ // 8)
    starts = jnp.where(forced, 1, starts)
    starts = jnp.where(places == 0, 1, starts)
    numbers = jnp.minimum(jnp.cumsum(starts, axis=1), SEQ // 8)
    padding = jax.random.randint(padding_key, (sequences, 1), 1, SEQ // 2 + 1)
    live = places < SEQ - padding
    return jnp.where(live, numbers, 0).reshape(TOKENS).astype(jnp.int32)


def block_levels(rng, shape, shards, least, top_value):
    loudness = 1.0
    for axis_at, blocks in shards:
        heights = jax.random.uniform(jax.random.fold_in(jax.random.fold_in(rng, 6), axis_at), (blocks,), jnp.float32, least / len(shards), top_value / len(shards))
        loudness = loudness * jnp.repeat(jnp.exp(heights), shape[axis_at] // blocks).reshape((-1,) + (1,) * (len(shape) - 1 - axis_at))
    return loudness


def normal_values(rng, shape, deviation, most, cuts=(), dtype=jnp.bfloat16):
    array = jax.random.normal(rng, shape, jnp.float32) * deviation
    if len(cuts) > 0:
        array = block_levels(rng, shape, cuts, -0.22, 0.18) * array
    return jnp.clip(array, min=-most, max=most).astype(dtype)


def setup_inputs(seed: int = 0) -> dict:
    key_list = jax.random.split(jax.random.key(seed), 11)
    tokens = normal_values(key_list[0], (TOKENS, D), 1.0, 6.0, ((0, 32),))
    segment_ids = draw_segment_ids(jax.random.fold_in(key_list[10], 71), 0)
    cotangent = normal_values(key_list[2], (TOKENS, D), 1.0, 6.0, ((0, 32),), jnp.float32)
    gain_one = jnp.clip(1.0 + 0.15 * jax.random.normal(key_list[3], (D,), jnp.float32), 0.25, 1.75).astype(jnp.bfloat16)
    w_qkv = normal_values(key_list[4], (D, 3 * H * HD), D ** -0.5, 0.21875, ((0, 4), (1, 8)))
    w_out = normal_values(key_list[5], (D, H * HD), (H * HD // 16) ** -0.5, 0.875, ((0, 4), (1, 8)))
    rel_table = normal_values(key_list[6], (BUCKETS, H), 1.0, 4.0)
    gain_two = jnp.clip(1.0 + 0.15 * jax.random.normal(key_list[7], (D,), jnp.float32), 0.25, 1.75).astype(jnp.bfloat16)
    w_in = normal_values(key_list[8], (D, FF), D ** -0.5, 0.21875, ((0, 4), (1, 8)))
    w_back = normal_values(key_list[9], (D, FF), FF ** -0.5, 0.109375, ((0, 4), (1, 8)))
    return dict(tokens=tokens, segment_ids=segment_ids, cotangent=cotangent, gain_one=gain_one, w_qkv=w_qkv, w_out=w_out, rel_table=rel_table, gain_two=gain_two, w_in=w_in, w_back=w_back)


@jax.custom_vjp
def low(v):
    return lax.optimization_barrier(v.astype(jnp.bfloat16)).astype(jnp.float32)

@jax.custom_vjp
def low_back(v):
    return v

def low_keep(v):
    return (low(v), None)

def low_pass(kept, grad):
    return (grad,)

def back_keep(v):
    return (v, None)

def back_low(kept, grad):
    return (low(grad),)
low.defvjp(low_keep, low_pass)
low_back.defvjp(back_keep, back_low)
EPSILON = 1e-06
NEGATIVE = -1e+30
SCALING = 0.125
THRESHOLDS = (12, 16, 23, 32, 46, 64, 91)
HIGHEST = lax.Precision.HIGHEST

def rms_norm(values, gain):
    return values * lax.rsqrt(lax.optimization_barrier(jnp.mean(values * values, axis=-1, keepdims=True)) + EPSILON) * gain

def bucket_table(length):
    offsets = lax.broadcasted_iota(jnp.int32, (length, length), 1) - lax.broadcasted_iota(jnp.int32, (length, length), 0)
    distance = jnp.abs(offsets)
    larger = jnp.zeros_like(distance)
    for edge_value in THRESHOLDS:
        larger = larger + (distance >= edge_value).astype(jnp.int32)
    inside = jnp.where(distance < 8, distance, 8 + larger)
    return inside + BUCKETS // 2 * (offsets > 0).astype(jnp.int32)

def allowed_mask(segments):
    same = (segments[:, None] == segments[None, :]) & (segments[None, :] > 0)
    diagonal = lax.broadcasted_iota(jnp.int32, same.shape, 0) == lax.broadcasted_iota(jnp.int32, same.shape, 1)
    return same | diagonal

def block_forward(values, gain_one, w_qkv, w_out, table, gain_two, w_in, w_back, segments):
    count = values.shape[0] // SEQ
    inner = H * HD
    normed = low(rms_norm(values, gain_one))
    mixed = low_back(low(jnp.dot(normed, w_qkv, precision=HIGHEST)))
    queries = mixed[:, :inner].reshape(count, SEQ, H, HD)
    key_rows = mixed[:, inner:2 * inner].reshape(count, SEQ, H, HD)
    value_rows = mixed[:, 2 * inner:].reshape(count, SEQ, H, HD)
    raw = low_back(jnp.einsum('sqhd,skhd->shqk', queries, key_rows, precision=HIGHEST))
    bias = jnp.moveaxis(table[bucket_table(SEQ)], 2, 0)
    allowed = jax.vmap(allowed_mask)(segments.reshape(count, SEQ))
    scores = jnp.where(allowed[:, None], raw * SCALING + bias[None], NEGATIVE)
    probs = low(jax.nn.softmax(scores, axis=-1))
    context = jnp.einsum('shqk,skhd->sqhd', probs, value_rows, precision=HIGHEST).reshape(count * SEQ, inner)
    context = low_back(low(context))
    attended = low_back(jnp.dot(context, w_out.T, precision=HIGHEST))
    residual = values + attended
    second = low(rms_norm(residual, gain_two))
    hidden = low_back(jnp.dot(second, w_in, precision=HIGHEST))
    active = low(jax.nn.gelu(hidden))
    return residual + low_back(jnp.dot(active, w_back.T, precision=HIGHEST))

def reference(tokens, segment_ids, cotangent, gain_one, w_qkv, w_out, rel_table, gain_two, w_in, w_back):
    weights = tuple((w.astype(jnp.float32) for w in (gain_one, w_qkv, w_out, rel_table, gain_two, w_in, w_back)))
    group_size = math.gcd(TOKENS // SEQ, max(1, 4096 // SEQ))
    blocks = TOKENS // (group_size * SEQ)
    width_rows = group_size * SEQ
    inputs_all = tokens.astype(jnp.float32).reshape(blocks, width_rows, D)
    segments_all = segment_ids.astype(jnp.int32).reshape(blocks, width_rows)
    cotangent_all = cotangent.astype(jnp.float32).reshape(blocks, width_rows, D)

    def visit(totals, pieces):
        input_part, segment_part, cotangent_part = pieces

        def forward(values, *params):
            return block_forward(values, *params, segment_part)
        result, pullback = jax.vjp(forward, input_part, *weights)
        gradients = pullback(cotangent_part)
        totals = tuple((before + added for before, added in zip(totals, gradients[1:])))
        return (totals, (result, gradients[0]))
    initial = tuple((jnp.zeros_like(w) for w in weights))
    totals, (results, input_grads) = lax.scan(visit, initial, (inputs_all, segments_all, cotangent_all))
    return (results.reshape(TOKENS, D).astype(jnp.bfloat16), input_grads.reshape(TOKENS, D), totals[0], totals[1], totals[2], totals[3], totals[4], totals[5], totals[6])
```

```python
import functools

import jax
import jax.numpy as jnp
from jax import lax
from jax.experimental import pallas as pl
from jax.experimental.pallas import tpu as pltpu
from jax.sharding import PartitionSpec as P

H = 12
HD = 64
BUCKETS = 32
SEQ = 512


EPSILON = 1e-06
NEGATIVE = -1e30
SCALING = 0.125
THRESHOLDS = (12, 16, 23, 32, 46, 64, 91)
HIGHEST = lax.Precision.HIGHEST


def rms_norm(values, gain):
    return values * lax.rsqrt(jnp.mean(values * values, axis=-1, keepdims=True) + EPSILON) * gain


def bucket_table(length):
    offsets = lax.broadcasted_iota(jnp.int32, (length, length), 1) - lax.broadcasted_iota(
        jnp.int32, (length, length), 0
    )
    distance = jnp.abs(offsets)
    larger = jnp.zeros_like(distance)
    for edge_value in THRESHOLDS:
        larger = larger + (distance >= edge_value).astype(jnp.int32)
    inside = jnp.where(distance < 8, distance, 8 + larger)
    return inside + BUCKETS // 2 * (offsets > 0).astype(jnp.int32)


def allowed_mask(segments):
    same = (segments[:, None] == segments[None, :]) & (segments[None, :] > 0)
    diagonal = lax.broadcasted_iota(jnp.int32, same.shape, 0) == lax.broadcasted_iota(
        jnp.int32, same.shape, 1
    )
    return same | diagonal


def score_block(query_seq, key_seq, segment_seq, bias):
    raw = jnp.einsum("qhd,khd->hqk", query_seq, key_seq, preferred_element_type=jnp.float32)
    return jnp.where(allowed_mask(segment_seq)[None], raw * SCALING + bias, NEGATIVE)


MESH = pl.DeviceIdType.MESH

class Place:
    def __init__(self):
        self.z = lax.axis_index("mp"); self.d = lax.axis_index("dp")
        d = self.d
        self.c = lax.rem(d, 2); self.x = lax.rem(d // 2, 2); self.y = d // 4
        self.xd = d + 2 - 4 * self.x
        self.yd = d + 4 - 8 * self.y
        self.cd = d + 1 - 2 * self.c
        self.gd = self.xd + 4 - 8 * self.y
    def barrier(self, levels):
        bar = pltpu.get_barrier_semaphore()
        for t in (self.xd, self.yd, self.cd):
            pl.semaphore_signal(bar, inc=1, device_id=(self.z, t), device_id_type=MESH)
        @pl.when(self.z > 0)
        def _():
            pl.semaphore_signal(bar, inc=1, device_id=(self.z - 1, self.d), device_id_type=MESH)
        @pl.when(self.z < levels - 1)
        def _():
            pl.semaphore_signal(bar, inc=1, device_id=(self.z + 1, self.d), device_id_type=MESH)
        peers = 3 + jnp.minimum(self.z, 1) + jnp.minimum(levels - 1 - self.z, 1)
        pl.semaphore_wait(bar, peers)

class Gather:
    def __init__(self, me, levels, piece, full, zs, zr, xs, xr, cs, cr):
        self.me, self.levels, self.piece, self.full = me, levels, piece, full
        self.zs, self.zr, self.xs, self.xr, self.cs, self.cr = zs, zr, xs, xr, cs, cr
        self.rows, self.cols = piece.shape[1], piece.shape[2]
    def blk(self, u, z, d, r0=0, nr=None):
        nr = self.rows if nr is None else nr
        return self.full.at[u, pl.ds(pl.multiple_of(z * self.rows + r0, 16), nr), pl.ds(pl.multiple_of(d * self.cols, 128), self.cols)]
    def col(self, u, d):
        return self.full.at[u, :, pl.ds(pl.multiple_of(d * self.cols, 128), self.cols)]
    def cp(self, src, dst, ss, rs, dev):
        return pltpu.make_async_remote_copy(src_ref=src, dst_ref=dst, send_sem=ss, recv_sem=rs, device_id=dev, device_id_type=MESH)
    def zcopy(self, u, up, k, z, src=None):
        b = self.blk(u, z, self.me.d)
        t = self.me.z + (1 if up else -1)
        return self.cp(b if src is None else src, b, self.zs.at[u, 0 if up else 1, k], self.zr.at[u, 0 if up else 1, k], (t, self.me.d))
    def xcopy(self, u, z, d, src=None):
        b = self.blk(u, z, d)
        return self.cp(b if src is None else src, b, self.xs.at[u, 0, z], self.xr.at[u, 0, z], (self.me.z, self.me.xd))
    def ycopy(self, u, z, d, src=None):
        b = self.blk(u, z, d)
        return self.cp(b if src is None else src, b, self.xs.at[u, 1, z], self.xr.at[u, 1, z], (self.me.z, self.me.yd))
    def half(self, u, z, d, way):
        h = self.rows // 2
        b = self.blk(u, z, d, way * h, h)
        return self.cp(b, b, self.xs.at[u, 2 + way, z], self.xr.at[u, 2 + way, z], (self.me.z, self.me.yd if way == 0 else self.me.xd))
    def ccopy(self, u, which, d):
        b = self.col(u, d)
        return self.cp(b, b, self.cs.at[u, which], self.cr.at[u, which], (self.me.z, self.me.cd))
    def zstep(self, u, k):
        me = self.me
        if k == 0:
            src = self.piece.at[u]
            self.xcopy(u, me.z, me.d, src).start()
            self.ycopy(u, me.z, me.d, src).start()
            @pl.when(me.z < self.levels - 1)
            def _():
                self.zcopy(u, True, 0, me.z, src).start()
            @pl.when(me.z > 0)
            def _():
                self.zcopy(u, False, 0, me.z, src).start()
            self.blk(u, me.z, me.d)[...] = self.piece[u]
            return
        @pl.when(me.z - k >= 0)
        def _():
            z = me.z - k
            self.zcopy(u, True, k - 1, z).wait_recv()
            if k < self.levels - 1:
                @pl.when(me.z < self.levels - 1)
                def _():
                    self.zcopy(u, True, k, z).start()
            self.xcopy(u, z, me.d).start()
            self.ycopy(u, z, me.d).start()
        @pl.when(me.z + k < self.levels)
        def _():
            z = me.z + k
            self.zcopy(u, False, k - 1, z).wait_recv()
            if k < self.levels - 1:
                @pl.when(me.z > 0)
                def _():
                    self.zcopy(u, False, k, z).start()
            self.xcopy(u, z, me.d).start()
            self.ycopy(u, z, me.d).start()
    def xystep(self, u, k):
        me = self.me
        def one(z):
            self.xcopy(u, z, me.xd).wait_recv()
            self.half(u, z, me.xd, 0).start()
            self.ycopy(u, z, me.yd).wait_recv()
            self.half(u, z, me.yd, 1).start()
        if k == 0:
            one(me.z)
            return
        @pl.when(me.z - k >= 0)
        def _():
            one(me.z - k)
        @pl.when(me.z + k < self.levels)
        def _():
            one(me.z + k)
    def corestep(self, u, which):
        me = self.me
        self.ccopy(u, which, (me.d, me.xd, me.yd, me.gd)[which]).start()
    def diagstep(self, u):
        me = self.me
        for z in range(self.levels):
            self.half(u, z, me.gd, 0).wait_recv()
            self.half(u, z, me.gd, 1).wait_recv()
    def corewait(self, u):
        me = self.me
        for which in range(4):
            self.ccopy(u, which, (me.cd, me.cd + me.xd - me.d, me.cd + me.yd - me.d, me.cd + me.gd - me.d)[which]).wait_recv()
    def sendwait(self, u):
        me = self.me
        for k in range(self.levels - 1):
            @pl.when((me.z < self.levels - 1) & (me.z - k >= 0))
            def _():
                self.zcopy(u, True, k, me.z - k).wait_send()
            @pl.when((me.z > 0) & (me.z + k < self.levels))
            def _():
                self.zcopy(u, False, k, me.z + k).wait_send()
        for z in range(self.levels):
            self.xcopy(u, z, me.d).wait_send()
            self.ycopy(u, z, me.d).wait_send()
            self.half(u, z, me.xd, 0).wait_send()
            self.half(u, z, me.yd, 1).wait_send()
        for which in range(4):
            self.ccopy(u, which, me.d).wait_send()
    def events(self, units):
        L = self.levels
        out = []
        n = units * L
        for s in range(n + 3):
            step = []
            u, k = divmod(s, L)
            if s < n:
                step.append(functools.partial(self.zstep, u, k))
                if k == L - 1:
                    step.append(functools.partial(self.corestep, u, 0))
            t = s - 1
            if 0 <= t < n:
                u, k = divmod(t, L)
                step.append(functools.partial(self.xystep, u, k))
                if k == L - 1:
                    step.append(functools.partial(self.corestep, u, 1))
                    step.append(functools.partial(self.corestep, u, 2))
            t = s - 2
            if 0 <= t < n:
                u, k = divmod(t, L)
                if k == L - 1:
                    step.append(functools.partial(self.diagstep, u))
                    step.append(functools.partial(self.corestep, u, 3))
            t = s - 3
            if 0 <= t < n:
                u, k = divmod(t, L)
                if k == L - 1:
                    step.append(functools.partial(self.corewait, u))
            out.append(step)
        return out

def gather_sems(units, levels):
    return [pltpu.SemaphoreType.DMA((units, 2, levels - 1))] * 2 + [pltpu.SemaphoreType.DMA((units, 4, levels))] * 2 + [pltpu.SemaphoreType.DMA((units, 4))] * 2

def gather_kernel(levels, piece, full, *sems):
    me = Place()
    me.barrier(levels)
    g = Gather(me, levels, piece, full, *sems)
    for step in g.events(piece.shape[0]):
        for call in step: call()
    for u in range(piece.shape[0]): g.sendwait(u)

def gather(piece, levels, width):
    u, r, c = piece.shape
    return pl.pallas_call(functools.partial(gather_kernel, levels),
        out_shape=jax.ShapeDtypeStruct((u, r * levels, c * width), piece.dtype),
        in_specs=[pl.BlockSpec(memory_space=pltpu.VMEM)], out_specs=pl.BlockSpec(memory_space=pltpu.VMEM),
        scratch_shapes=gather_sems(u, levels),
        compiler_params=pltpu.CompilerParams(collective_id=0, has_side_effects=True, vmem_limit_bytes=50 << 20), name="gather")(piece)


def collect_weights(matrices):
    levels, width = lax.axis_size("mp"), lax.axis_size("dp")
    qkv, out, inn, back = matrices
    packed = qkv.shape[1] + out.shape[1]
    if width != 8 or packed != inn.shape[1] or packed % 128 != 0 or qkv.shape[0] % 32 != 0:
        full = [lax.all_gather(lax.all_gather(m, "mp", axis=0, tiled=True), "dp", axis=1, tiled=True) for m in matrices]
        return tuple(full)
    piece = jnp.stack([jnp.concatenate([qkv, out], axis=1), inn, back])
    full = gather(piece, levels, width)
    rows = full.shape[1]
    blocks = full[0].reshape(rows, width, packed)
    return (
        blocks[:, :, : qkv.shape[1]].reshape(rows, width * qkv.shape[1]),
        blocks[:, :, qkv.shape[1] :].reshape(rows, width * out.shape[1]),
        full[1],
        full[2],
    )


def spread_grads(gradients):
    row_share = (
        lax.psum_scatter(
            gradients[0].astype(jnp.bfloat16), "mp", scatter_dimension=0, tiled=True
        ).astype(jnp.float32),
        lax.psum_scatter(
            gradients[1].astype(jnp.bfloat16), "mp", scatter_dimension=0, tiled=True
        ).astype(jnp.float32),
        lax.psum_scatter(
            gradients[2].astype(jnp.bfloat16), "mp", scatter_dimension=0, tiled=True
        ).astype(jnp.float32),
        lax.psum_scatter(
            gradients[3].astype(jnp.bfloat16), "mp", scatter_dimension=0, tiled=True
        ).astype(jnp.float32),
    )
    return (
        lax.psum_scatter(row_share[0], "dp", scatter_dimension=1, tiled=True),
        lax.psum_scatter(row_share[1], "dp", scatter_dimension=1, tiled=True),
        lax.psum_scatter(row_share[2], "dp", scatter_dimension=1, tiled=True),
        lax.psum_scatter(row_share[3], "dp", scatter_dimension=1, tiled=True),
    )


def body(tokens, segment_ids, cotangent, gain_one, w_qkv, w_out, rel_table, gain_two, w_in, w_back):
    rows = tokens.shape[0]
    count = rows // SEQ
    inner = H * HD
    qkv_full, out_full, in_full, back_full = collect_weights((w_qkv, w_out, w_in, w_back))
    values = tokens.astype(jnp.float32)
    gain_first = gain_one.astype(jnp.float32)
    gain_second = gain_two.astype(jnp.float32)
    table = rel_table.astype(jnp.float32)
    buckets = bucket_table(SEQ).reshape(SEQ * SEQ)
    one_hot = (buckets[:, None] == lax.broadcasted_iota(jnp.int32, (1, BUCKETS), 1)).astype(
        jnp.float32
    )
    bias = jnp.dot(one_hot, table, precision=HIGHEST).T.reshape(H, SEQ, SEQ)
    normed_low = rms_norm(values, gain_first).astype(jnp.bfloat16)
    mixed = jnp.dot(normed_low, qkv_full, preferred_element_type=jnp.float32).astype(jnp.bfloat16)
    queries = mixed[:, :inner].reshape(count, SEQ, H, HD)
    key_rows = mixed[:, inner : 2 * inner].reshape(count, SEQ, H, HD)
    value_rows = mixed[:, 2 * inner :].reshape(count, SEQ, H, HD)
    segments = segment_ids.reshape(count, SEQ)

    def attend(pieces):
        query_seq, key_seq, value_seq, segment_seq = pieces
        scores = score_block(query_seq, key_seq, segment_seq, bias)
        highest = jnp.max(scores, axis=-1, keepdims=True)
        log_total = highest + jnp.log(jnp.sum(jnp.exp(scores - highest), axis=-1, keepdims=True))
        probs = jnp.exp(scores - log_total).astype(jnp.bfloat16)
        context_seq = jnp.einsum(
            "hqk,khd->qhd", probs, value_seq, preferred_element_type=jnp.float32
        )
        return (context_seq.astype(jnp.bfloat16), log_total)

    context, log_totals = lax.map(attend, (queries, key_rows, value_rows, segments))
    context = context.reshape(rows, inner)
    attended = jnp.einsum("ti,di->td", context, out_full, preferred_element_type=jnp.float32)
    residual = values + attended
    second_low = rms_norm(residual, gain_second).astype(jnp.bfloat16)
    hidden = jnp.einsum("td,df->tf", second_low, in_full, preferred_element_type=jnp.float32)
    active = jax.nn.gelu(hidden).astype(jnp.bfloat16)
    result = residual + jnp.einsum(
        "tf,df->td", active, back_full, preferred_element_type=jnp.float32
    )
    layer_out = result.astype(jnp.bfloat16)
    out_low = cotangent.astype(jnp.bfloat16)
    grad_back = jnp.einsum("td,tf->df", out_low, active, preferred_element_type=jnp.float32)
    active_grad = jnp.einsum("td,df->tf", out_low, back_full, preferred_element_type=jnp.float32)
    hidden_low = jax.vjp(jax.nn.gelu, hidden)[1](active_grad)[0].astype(jnp.bfloat16)
    grad_in = jnp.einsum("td,tf->df", second_low, hidden_low, preferred_element_type=jnp.float32)
    second_grad = jnp.einsum("tf,df->td", hidden_low, in_full, preferred_element_type=jnp.float32)
    residual_part, gain_second_grad = jax.vjp(rms_norm, residual, gain_second)[1](second_grad)
    residual_grad = cotangent + residual_part
    attended_low = residual_grad.astype(jnp.bfloat16)
    grad_out = jnp.einsum("td,ti->di", attended_low, context, preferred_element_type=jnp.float32)
    context_low = jnp.einsum(
        "td,di->ti", attended_low, out_full, preferred_element_type=jnp.float32
    )
    context_low = context_low.astype(jnp.bfloat16).reshape(count, SEQ, H, HD)

    def attend_back(pieces):
        query_seq, key_seq, value_seq, segment_seq, log_total, context_seq = pieces
        scores = score_block(query_seq, key_seq, segment_seq, bias)
        probs = jnp.exp(scores - log_total)
        probs_low = probs.astype(jnp.bfloat16)
        value_grad = jnp.einsum(
            "hqk,qhd->khd", probs_low, context_seq, preferred_element_type=jnp.float32
        )
        probs_grad = jnp.einsum(
            "qhd,khd->hqk", context_seq, value_seq, preferred_element_type=jnp.float32
        )
        score_grad = probs * (probs_grad - jnp.sum(probs_grad * probs, axis=-1, keepdims=True))
        raw_low = (score_grad * SCALING).astype(jnp.bfloat16)
        query_grad = jnp.einsum(
            "hqk,khd->qhd", raw_low, key_seq, preferred_element_type=jnp.float32
        )
        key_grad = jnp.einsum(
            "hqk,qhd->khd", raw_low, query_seq, preferred_element_type=jnp.float32
        )
        table_part = jnp.dot(one_hot.T, score_grad.reshape(H, SEQ * SEQ).T, precision=HIGHEST)
        joined = jnp.concatenate(
            [
                query_grad.reshape(SEQ, inner),
                key_grad.reshape(SEQ, inner),
                value_grad.reshape(SEQ, inner),
            ],
            axis=1,
        )
        return (joined.astype(jnp.bfloat16), table_part)

    mixed_low, table_parts = lax.map(
        attend_back, (queries, key_rows, value_rows, segments, log_totals, context_low)
    )
    mixed_low = mixed_low.reshape(rows, 3 * inner)
    table_grad = jnp.sum(table_parts, axis=0)
    grad_qkv = jnp.einsum("td,tj->dj", normed_low, mixed_low, preferred_element_type=jnp.float32)
    normed_grad = jnp.einsum("tj,dj->td", mixed_low, qkv_full, preferred_element_type=jnp.float32)
    tokens_part, gain_first_grad = jax.vjp(rms_norm, values, gain_first)[1](normed_grad)
    tokens_grad = residual_grad + tokens_part
    first_total, second_total, table_total = lax.psum(
        (gain_first_grad, gain_second_grad, table_grad), ("mp", "dp")
    )
    qkv_share, out_share, in_share, back_share = spread_grads(
        (grad_qkv, grad_out, grad_in, grad_back)
    )
    return (
        layer_out,
        tokens_grad,
        first_total,
        qkv_share,
        out_share,
        table_total,
        second_total,
        in_share,
        back_share,
    )


def solution(mesh):
    placed = (
        P(("mp", "dp"), None),
        P(("mp", "dp")),
        P(("mp", "dp"), None),
        P(),
        P("mp", "dp"),
        P("mp", "dp"),
        P(),
        P(),
        P("mp", "dp"),
        P("mp", "dp"),
    )
    return jax.shard_map(
        body,
        mesh=mesh,
        in_specs=placed,
        out_specs=(
            P(("mp", "dp"), None),
            P(("mp", "dp"), None),
            P(),
            P("mp", "dp"),
            P("mp", "dp"),
            P(),
            P(),
            P("mp", "dp"),
            P("mp", "dp"),
        ),
        check_vma=False,
    )
```

```python
import functools

import jax
import jax.numpy as jnp
from jax import lax
from jax.experimental import pallas as pl
from jax.experimental.pallas import tpu as pltpu
from jax.sharding import PartitionSpec as P

MESH = pl.DeviceIdType.MESH

class Place:
    def __init__(self):
        self.z = lax.axis_index("mp"); self.d = lax.axis_index("dp")
        d = self.d
        self.c = lax.rem(d, 2); self.x = lax.rem(d // 2, 2); self.y = d // 4
        self.xd = d + 2 - 4 * self.x
        self.yd = d + 4 - 8 * self.y
        self.cd = d + 1 - 2 * self.c
        self.gd = self.xd + 4 - 8 * self.y
    def barrier(self, levels):
        bar = pltpu.get_barrier_semaphore()
        for t in (self.xd, self.yd, self.cd):
            pl.semaphore_signal(bar, inc=1, device_id=(self.z, t), device_id_type=MESH)
        @pl.when(self.z > 0)
        def _():
            pl.semaphore_signal(bar, inc=1, device_id=(self.z - 1, self.d), device_id_type=MESH)
        @pl.when(self.z < levels - 1)
        def _():
            pl.semaphore_signal(bar, inc=1, device_id=(self.z + 1, self.d), device_id_type=MESH)
        peers = 3 + jnp.minimum(self.z, 1) + jnp.minimum(levels - 1 - self.z, 1)
        pl.semaphore_wait(bar, peers)

class Gather:
    def __init__(self, me, levels, piece, full, zs, zr, xs, xr, cs, cr):
        self.me, self.levels, self.piece, self.full = me, levels, piece, full
        self.zs, self.zr, self.xs, self.xr, self.cs, self.cr = zs, zr, xs, xr, cs, cr
        self.rows, self.cols = piece.shape[1], piece.shape[2]
    def blk(self, u, z, d, r0=0, nr=None):
        nr = self.rows if nr is None else nr
        return self.full.at[u, pl.ds(pl.multiple_of(z * self.rows + r0, 16), nr), pl.ds(pl.multiple_of(d * self.cols, 128), self.cols)]
    def col(self, u, d):
        return self.full.at[u, :, pl.ds(pl.multiple_of(d * self.cols, 128), self.cols)]
    def cp(self, src, dst, ss, rs, dev):
        return pltpu.make_async_remote_copy(src_ref=src, dst_ref=dst, send_sem=ss, recv_sem=rs, device_id=dev, device_id_type=MESH)
    def zcopy(self, u, up, k, z, src=None):
        b = self.blk(u, z, self.me.d)
        t = self.me.z + (1 if up else -1)
        return self.cp(b if src is None else src, b, self.zs.at[u, 0 if up else 1, k], self.zr.at[u, 0 if up else 1, k], (t, self.me.d))
    def xcopy(self, u, z, d, src=None):
        b = self.blk(u, z, d)
        return self.cp(b if src is None else src, b, self.xs.at[u, 0, z], self.xr.at[u, 0, z], (self.me.z, self.me.xd))
    def ycopy(self, u, z, d, src=None):
        b = self.blk(u, z, d)
        return self.cp(b if src is None else src, b, self.xs.at[u, 1, z], self.xr.at[u, 1, z], (self.me.z, self.me.yd))
    def half(self, u, z, d, way):
        h = self.rows // 2
        b = self.blk(u, z, d, way * h, h)
        return self.cp(b, b, self.xs.at[u, 2 + way, z], self.xr.at[u, 2 + way, z], (self.me.z, self.me.yd if way == 0 else self.me.xd))
    def ccopy(self, u, which, d):
        b = self.col(u, d)
        return self.cp(b, b, self.cs.at[u, which], self.cr.at[u, which], (self.me.z, self.me.cd))
    def zstep(self, u, k):
        me = self.me
        if k == 0:
            src = self.piece.at[u]
            self.xcopy(u, me.z, me.d, src).start()
            self.ycopy(u, me.z, me.d, src).start()
            @pl.when(me.z < self.levels - 1)
            def _():
                self.zcopy(u, True, 0, me.z, src).start()
            @pl.when(me.z > 0)
            def _():
                self.zcopy(u, False, 0, me.z, src).start()
            self.blk(u, me.z, me.d)[...] = self.piece[u]
            return
        @pl.when(me.z - k >= 0)
        def _():
            z = me.z - k
            self.zcopy(u, True, k - 1, z).wait_recv()
            if k < self.levels - 1:
                @pl.when(me.z < self.levels - 1)
                def _():
                    self.zcopy(u, True, k, z).start()
            self.xcopy(u, z, me.d).start()
            self.ycopy(u, z, me.d).start()
        @pl.when(me.z + k < self.levels)
        def _():
            z = me.z + k
            self.zcopy(u, False, k - 1, z).wait_recv()
            if k < self.levels - 1:
                @pl.when(me.z > 0)
                def _():
                    self.zcopy(u, False, k, z).start()
            self.xcopy(u, z, me.d).start()
            self.ycopy(u, z, me.d).start()
    def xystep(self, u, k):
        me = self.me
        def one(z):
            self.xcopy(u, z, me.xd).wait_recv()
            self.half(u, z, me.xd, 0).start()
            self.ycopy(u, z, me.yd).wait_recv()
            self.half(u, z, me.yd, 1).start()
        if k == 0:
            one(me.z)
            return
        @pl.when(me.z - k >= 0)
        def _():
            one(me.z - k)
        @pl.when(me.z + k < self.levels)
        def _():
            one(me.z + k)
    def corestep(self, u, which):
        me = self.me
        self.ccopy(u, which, (me.d, me.xd, me.yd, me.gd)[which]).start()
    def diagstep(self, u):
        me = self.me
        for z in range(self.levels):
            self.half(u, z, me.gd, 0).wait_recv()
            self.half(u, z, me.gd, 1).wait_recv()
    def corewait(self, u):
        me = self.me
        for which in range(4):
            self.ccopy(u, which, (me.cd, me.cd + me.xd - me.d, me.cd + me.yd - me.d, me.cd + me.gd - me.d)[which]).wait_recv()
    def sendwait(self, u):
        me = self.me
        for k in range(self.levels - 1):
            @pl.when((me.z < self.levels - 1) & (me.z - k >= 0))
            def _():
                self.zcopy(u, True, k, me.z - k).wait_send()
            @pl.when((me.z > 0) & (me.z + k < self.levels))
            def _():
                self.zcopy(u, False, k, me.z + k).wait_send()
        for z in range(self.levels):
            self.xcopy(u, z, me.d).wait_send()
            self.ycopy(u, z, me.d).wait_send()
            self.half(u, z, me.xd, 0).wait_send()
            self.half(u, z, me.yd, 1).wait_send()
        for which in range(4):
            self.ccopy(u, which, me.d).wait_send()
    def events(self, units):
        L = self.levels
        out = []
        n = units * L
        for s in range(n + 3):
            step = []
            u, k = divmod(s, L)
            if s < n:
                step.append(functools.partial(self.zstep, u, k))
                if k == L - 1:
                    step.append(functools.partial(self.corestep, u, 0))
            t = s - 1
            if 0 <= t < n:
                u, k = divmod(t, L)
                step.append(functools.partial(self.xystep, u, k))
                if k == L - 1:
                    step.append(functools.partial(self.corestep, u, 1))
                    step.append(functools.partial(self.corestep, u, 2))
            t = s - 2
            if 0 <= t < n:
                u, k = divmod(t, L)
                if k == L - 1:
                    step.append(functools.partial(self.diagstep, u))
                    step.append(functools.partial(self.corestep, u, 3))
            t = s - 3
            if 0 <= t < n:
                u, k = divmod(t, L)
                if k == L - 1:
                    step.append(functools.partial(self.corewait, u))
            out.append(step)
        return out

def gather_sems(units, levels):
    return [pltpu.SemaphoreType.DMA((units, 2, levels - 1))] * 2 + [pltpu.SemaphoreType.DMA((units, 4, levels))] * 2 + [pltpu.SemaphoreType.DMA((units, 4))] * 2

def greet_all(me, levels):
    bar = pltpu.get_barrier_semaphore()
    for t in (me.xd, me.yd, me.cd):
        pl.semaphore_signal(bar, inc=1, device_id=(me.z, t), device_id_type=MESH)
    for k in range(1, levels):
        pl.semaphore_signal(bar, inc=1, device_id=(lax.rem(me.z + k, levels), me.d), device_id_type=MESH)
    pl.semaphore_wait(bar, 2 + levels)

class Scatter:
    def __init__(self, me, levels, rows, cols, own, staged, matrix, core, cross, line, cs, cr, xs, xr, zs, zr):
        self.me, self.levels, self.rows, self.cols = me, levels, rows, cols
        self.grads, self.staged, self.matrix = own, staged, matrix
        self.core, self.cross, self.line = core, cross, line
        self.cs, self.cr, self.xs, self.xr, self.zs, self.zr = cs, cr, xs, xr, zs, zr
        self.order = (me.gd, me.xd, me.yd, me.d)
        self.half_rows = rows * levels // 2
    def cp(self, src, dst, ss, rs, dev):
        return pltpu.make_async_remote_copy(src_ref=src, dst_ref=dst, send_sem=ss, recv_sem=rs, device_id=dev, device_id_type=MESH)
    def add(self, dst, src):
        n = dst.shape[0]
        step = 96 if n % 96 == 0 else 16
        def one(i, _):
            at = pl.ds(pl.multiple_of(i * step, 16), step)
            dst[at, :] = dst[at, :] + src[at, :]
            return 0
        lax.fori_loop(0, n // step, one, 0)
    def core_start(self, u, q):
        self.ccopy(u, q).start()
    def index(self, d):
        return [i for i, o in enumerate(self.order) if o is d][0]
    def block(self, u, d, r0, nr):
        at = pl.ds(r0 if isinstance(r0, int) else pl.multiple_of(r0, 16), nr)
        if u < 2:
            return self.grads.at[u, self.index(d), at]
        return self.matrix.at[at, pl.ds(pl.multiple_of(d * self.cols, 128), self.cols)]
    def slot(self, u):
        return 0 if u == 2 else u
    def ccopy(self, u, q):
        s = self.slot(u)
        if u < 2:
            src = self.staged.at[u, q % 2]
        else:
            src = self.block(u, self.order[q] + self.me.cd - self.me.d, 0, self.rows * self.levels)
        return self.cp(src, self.core.at[s, q], self.cs.at[u, q], self.cr.at[u, q], (self.me.z, self.me.cd))
    def core_add(self, u, q):
        self.ccopy(u, q).wait_recv()
        self.add(self.block(u, self.order[q], 0, self.rows * self.levels), self.core.at[self.slot(u), q])
        if q == 0:
            self.xcopy(u, 0).start()
            self.ycopy(u, 0).start()
        if q == 1:
            self.xcopy(u, 1).start()
        if q == 2:
            self.ycopy(u, 1).start()
    def xcopy(self, u, slot):
        d = (self.me.gd, self.me.xd, self.me.xd)[slot]
        r0 = (0, 0, self.half_rows)[slot]
        return self.cp(self.block(u, d, r0, self.half_rows), self.cross.at[self.slot(u), 0, slot], self.xs.at[u, 0, slot], self.xr.at[u, 0, slot], (self.me.z, self.me.xd))
    def ycopy(self, u, slot):
        d = (self.me.gd, self.me.yd, self.me.yd)[slot]
        r0 = (self.half_rows, self.half_rows, 0)[slot]
        return self.cp(self.block(u, d, r0, self.half_rows), self.cross.at[self.slot(u), 1, slot], self.xs.at[u, 1, slot], self.xr.at[u, 1, slot], (self.me.z, self.me.yd))
    def zcopy(self, u, way, target):
        slot = target - 1 if way == 0 else target
        t = self.me.z + (1 if way == 0 else -1)
        return self.cp(self.block(u, self.me.d, target * self.rows, self.rows), self.line.at[self.slot(u), way, slot], self.zs.at[u, way, slot], self.zr.at[u, way, slot], (t, self.me.d))
    def cross_one(self, u):
        me, h, s = self.me, self.half_rows, self.slot(u)
        self.xcopy(u, 0).wait_recv()
        self.add(self.block(u, me.yd, 0, h), self.cross.at[s, 0, 0])
        self.ycopy(u, 2).start()
        self.ycopy(u, 0).wait_recv()
        self.add(self.block(u, me.xd, h, h), self.cross.at[s, 1, 0])
        self.xcopy(u, 2).start()
    def cross_two(self, u):
        me, h, s = self.me, self.half_rows, self.slot(u)
        self.xcopy(u, 1).wait_recv()
        self.add(self.block(u, me.d, 0, h), self.cross.at[s, 0, 1])
        self.ycopy(u, 1).wait_recv()
        self.add(self.block(u, me.d, h, h), self.cross.at[s, 1, 1])
    def cross_three(self, u):
        me, h, s = self.me, self.half_rows, self.slot(u)
        self.ycopy(u, 2).wait_recv()
        self.add(self.block(u, me.d, 0, h), self.cross.at[s, 1, 2])
        self.xcopy(u, 2).wait_recv()
        self.add(self.block(u, me.d, h, h), self.cross.at[s, 0, 2])
    def line_step(self, u, i):
        me, last, s = self.me, self.levels - 1, self.slot(u)
        up, down = last - i, i
        @pl.when((me.z > 0) & (me.z <= up))
        def _():
            self.zcopy(u, 0, up).wait_recv()
            @pl.when(me.z < up)
            def _():
                self.add(self.block(u, me.d, up * self.rows, self.rows), self.line.at[s, 0, up - 1])
        @pl.when(me.z < up)
        def _():
            self.zcopy(u, 0, up).start()
        @pl.when((me.z < last) & (me.z >= down))
        def _():
            self.zcopy(u, 1, down).wait_recv()
            @pl.when(me.z > down)
            def _():
                self.add(self.block(u, me.d, down * self.rows, self.rows), self.line.at[s, 1, down])
        @pl.when(me.z > down)
        def _():
            self.zcopy(u, 1, down).start()
    def finish(self, u):
        me, last, s = self.me, self.levels - 1, self.slot(u)
        own = self.block(u, me.d, me.z * self.rows, self.rows)[...].astype(F32)
        below = self.line[s, 0, jnp.maximum(me.z - 1, 0)].astype(F32)
        above = self.line[s, 1, jnp.minimum(me.z, last - 1)].astype(F32)
        return own + jnp.where(me.z > 0, below, 0.0) + jnp.where(me.z < last, above, 0.0)
    def release(self, free):
        me, last = self.me, self.levels - 1
        for t in (me.xd, me.yd, me.cd):
            pl.semaphore_signal(free, inc=1, device_id=(me.z, t), device_id_type=MESH)
        @pl.when(me.z > 0)
        def _():
            pl.semaphore_signal(free, inc=1, device_id=(me.z - 1, me.d), device_id_type=MESH)
        @pl.when(me.z < last)
        def _():
            pl.semaphore_signal(free, inc=1, device_id=(me.z + 1, me.d), device_id_type=MESH)
    def acquire(self, free):
        me, last = self.me, self.levels - 1
        pl.semaphore_wait(free, 3 + jnp.minimum(me.z, 1) + jnp.minimum(last - me.z, 1))
    def sendwait(self, u):
        me, last = self.me, self.levels - 1
        for q in range(4):
            if u == 2 or q >= 2: self.ccopy(u, q).wait_send()
        for slot in range(3):
            self.xcopy(u, slot).wait_send()
            self.ycopy(u, slot).wait_send()
        for i in range(last):
            @pl.when(me.z < last - i)
            def _():
                self.zcopy(u, 0, last - i).wait_send()
            @pl.when(me.z > i)
            def _():
                self.zcopy(u, 1, i).wait_send()

class Small:
    def __init__(self, me, levels, mine, swap, slots, ss, rs):
        self.me, self.levels, self.mine, self.swap, self.slots, self.ss, self.rs = me, levels, mine, swap, slots, ss, rs
    def pair(self, i):
        t = (self.me.cd, self.me.xd, self.me.yd)[i]
        return pltpu.make_async_remote_copy(src_ref=self.mine.at[i], dst_ref=self.swap.at[i], send_sem=self.ss.at[i], recv_sem=self.rs.at[i], device_id=(self.me.z, t), device_id_type=MESH)
    def start(self, i):
        self.pair(i).start()
    def add(self, i):
        self.pair(i).wait_recv()
        self.mine[i + 1] = self.mine[i] + self.swap[i]
    def level(self, k):
        t = lax.rem(self.me.z + k, self.levels)
        return pltpu.make_async_remote_copy(src_ref=self.mine.at[3], dst_ref=self.slots.at[k - 1], send_sem=self.ss.at[2 + k], recv_sem=self.rs.at[2 + k], device_id=(t, self.me.d), device_id_type=MESH)
    def spread(self):
        for k in range(1, self.levels):
            self.level(k).start()
    def total(self):
        for k in range(1, self.levels):
            self.level(k).wait_recv()
        def at(level):
            k = lax.rem(self.me.z - level + self.levels, self.levels)
            held = self.slots[jnp.maximum(k - 1, 0)]
            return jnp.where(k == 0, self.mine[3], held)
        out = at(0)
        for level in range(1, self.levels):
            out = out + at(level)
        return out
    def sendwait(self):
        for i in range(3):
            self.pair(i).wait_send()
        for k in range(1, self.levels):
            self.level(k).wait_send()

def small_scratch(levels, shape):
    return [pltpu.VMEM((4, *shape), jnp.float32), pltpu.VMEM((3, *shape), jnp.float32), pltpu.VMEM((levels - 1, *shape), jnp.float32),
            *[pltpu.SemaphoreType.DMA((2 + levels,))] * 2]

SEQ, HD, BUCKETS = 512, 64, 32
EPSILON = 1e-06
NEGATIVE = -1e30
SCALING = 0.125
THRESHOLDS = (12, 16, 23, 32, 46, 64, 91)
F32, BF16 = jnp.float32, jnp.bfloat16
EDGE = 128
NT = (((1,), (1,)), ((), ()))
NN = (((1,), (0,)), ((), ()))

def mm(a, b, dims=NN):
    return lax.dot_general(a, b, dims, preferred_element_type=F32)

def bucket_of(offset):
    distance = jnp.abs(offset)
    larger = jnp.zeros_like(distance)
    for edge in THRESHOLDS:
        larger = larger + (distance >= edge).astype(jnp.int32)
    inside = jnp.where(distance < 8, distance, 8 + larger)
    return inside + BUCKETS // 2 * (offset > 0).astype(jnp.int32)

def build_bias(table_t, skew):
    heads, edge, width = skew.shape
    span = 1024
    c = lax.broadcasted_iota(jnp.int32, (BUCKETS, span), 1)
    c = jnp.where(c >= span - EDGE, c - span, c)
    hot = (bucket_of((SEQ - EDGE) - c) == lax.broadcasted_iota(jnp.int32, (BUCKETS, span), 0)).astype(BF16)
    flat = mm(table_t, hot)
    for h in range(heads):
        rows = jnp.broadcast_to(flat[h : h + 1, :], (edge, span))
        skew[h] = pltpu.roll(rows, 0, 1, stride=1, stride_axis=0)[:, :width]

def build_mask(seg, mask):
    wide = jnp.broadcast_to(seg, (EDGE, SEQ))
    for b in range(SEQ // EDGE):
        col = wide[:, b * EDGE : (b + 1) * EDGE].T
        tall = jnp.concatenate([col] * (SEQ // EDGE), axis=1)
        same = (tall == wide) & (wide > 0.0)
        k = lax.broadcasted_iota(jnp.int32, (EDGE, SEQ), 0) + b * EDGE
        q = lax.broadcasted_iota(jnp.int32, (EDGE, SEQ), 1)
        mask[b * EDGE : (b + 1) * EDGE, :] = jnp.where(same | (k == q), 0.0, NEGATIVE)

def transpose(x):
    return x.T

GELU_C = 0.7978845608028654
def gelu_both(x):
    x2 = x * x
    t = jnp.tanh(x * (GELU_C + (GELU_C * 0.044715) * x2))
    half = 0.5 * x
    one = 0.5 + 0.5 * t
    act = x * one
    grad = one + (half * (1.0 - t * t)) * (GELU_C + (3.0 * 0.044715 * GELU_C) * x2)
    return act, grad

def forward_kernel(levels, comm, schedule, tok, seg, gain1, table_t, gain2, *rest):
    if comm:
        piece, rest = rest[0], rest[1:]
    else:
        weights, rest = rest[:4], rest[4:]
    (out, proj_o, in_o, back_o, mixed_o, e_o, rl_o, ctx_o, ctxt_o, res_o, act_o, gp_o), rest = rest[:12], rest[12:]
    (w, proj, normed, mixed, skew, mask, e, ctx, ctxt, act, gp, second, load, store, estore, gstore), sems = rest[:16], rest[16:]
    rows, width = tok.shape
    inner = width
    heads = skew.shape[0]
    pairs = heads // 2
    seqs = rows // SEQ
    hidden = act.shape[1]
    if comm:
        me = Place()
        me.barrier(levels)
        g = Gather(me, levels, piece, w, *sems)
        steps = g.events(3)
    else:
        steps = []
    def run(t):
        if t < len(steps):
            for call in steps[t]: call()
    if not comm:
        loads = [pltpu.make_async_copy(weights[0], proj.at[:, : 3 * inner], load.at[0]), pltpu.make_async_copy(weights[1], proj.at[:, 3 * inner :], load.at[1]),
                 pltpu.make_async_copy(weights[2], w.at[1], load.at[2]), pltpu.make_async_copy(weights[3], w.at[2], load.at[3])]
        for l in loads: l.start()
        for l in loads: l.wait()
    run(0)
    def norm_one(i, _):
        at = pl.ds(pl.multiple_of(i * 128, 128), 128)
        v = tok[at, :].astype(F32)
        r = lax.rsqrt(jnp.mean(v * v, axis=1, keepdims=True) + EPSILON)
        normed[at, :] = (v * r * gain1[...]).astype(BF16)
        return 0
    lax.fori_loop(0, rows // 128, norm_one, 0)
    run(1)
    build_bias(table_t[...], skew)
    run(2)
    for s in range(seqs):
        build_mask(seg[s : s + 1, :], mask.at[s])
    for t in range(3, levels + 3): run(t)
    if comm:
        packed = piece.shape[2]
        part = packed * 3 // 4
        blocks = hidden // packed
        def unpack(i, _):
            at = pl.ds(pl.multiple_of(i * 64, 64), 64)
            t = w[0, at, :]
            proj[at, :] = jnp.concatenate([t[:, d * packed : d * packed + part] for d in range(blocks)] + [t[:, d * packed + part : (d + 1) * packed] for d in range(blocks)], axis=1)
            return 0
        lax.fori_loop(0, width // 64, unpack, 0)
    proj_copy = pltpu.make_async_copy(proj, proj_o, store.at[0])
    proj_copy.start()
    def project(i, _):
        r = pl.ds(pl.multiple_of((i // 3) * 256, 256), 256)
        c = pl.ds(pl.multiple_of((i % 3) * inner, 128), inner)
        mixed[r, c] = mm(normed[r, :], proj[:, c]).astype(BF16)
        return 0
    lax.fori_loop(0, rows // 256 * 3, project, 0)
    mixed_copy = pltpu.make_async_copy(mixed, mixed_o, store.at[1])
    mixed_copy.start()
    low_lanes = lax.broadcasted_iota(jnp.int32, (256, 128), 1) < HD
    def attend(i, _):
        s, p = i // pairs, i % pairs
        slot = i % 2
        for t, at in schedule:
            @pl.when(i == at)
            def _():
                run(t)
        ecopy = pltpu.make_async_copy(e.at[slot], e_o.at[i], estore.at[slot])
        @pl.when(i >= 2)
        def _():
            ecopy.wait()
        row = pl.ds(pl.multiple_of(s * SEQ, SEQ), SEQ)
        off = pl.multiple_of(p * 128, 128)
        k = mixed[row, pl.ds(inner + off, 128)]
        v_t = transpose(mixed[row, pl.ds(2 * inner + off, 128)])
        for j in range(SEQ // 256):
            qrow = pl.ds(pl.multiple_of(s * SEQ + j * 256, 256), 256)
            q = mixed[qrow, pl.ds(off, 128)] * jnp.asarray(SCALING, BF16)
            tops = []
            for a in range(2):
                qa = jnp.where(low_lanes == (a == 0), q, jnp.zeros_like(q))
                h = 2 * p + a
                parts = []
                for b in range(SEQ // EDGE):
                    sc = mm(k[b * EDGE : (b + 1) * EDGE], qa, NT)
                    lo = SEQ - EDGE - b * EDGE + j * 256
                    parts.append(sc + (skew[h, :, lo : lo + 256] + mask[s, b * EDGE : (b + 1) * EDGE, j * 256 : (j + 1) * 256]))
                score = jnp.concatenate(parts, axis=0)
                top = jnp.max(score, axis=0, keepdims=True)
                ex = jnp.exp(score - top)
                rl = 1.0 / jnp.sum(ex, axis=0, keepdims=True)
                low = ex.astype(BF16)
                e[slot, a, :, j * 256 : (j + 1) * 256] = low
                rl_o[s * heads + h, :, j * 256 : (j + 1) * 256] = jnp.broadcast_to(rl, (8, 256))
                tops.append((mm(v_t[a * HD : (a + 1) * HD], low) * rl).astype(BF16))
            both = jnp.concatenate(tops, axis=0)
            ctxt[pl.ds(off, 128), qrow] = both
            ctx[qrow, pl.ds(off, 128)] = transpose(both)
        ecopy.start()
        return 0
    n = seqs * pairs
    lax.fori_loop(0, n, attend, 0)
    done = 1 + max([t for t, _ in schedule], default=levels + 2)
    ctx_copies = [pltpu.make_async_copy(ctx, ctx_o, store.at[2]), pltpu.make_async_copy(ctxt, ctxt_o, store.at[3])]
    for c in ctx_copies: c.start()
    def close(i, _):
        r = pl.ds(pl.multiple_of(i * 256, 256), 256)
        res = tok[r, :].astype(F32) + mm(ctx[r, :], proj[:, 3 * inner :], NT)
        res_o[r, :] = res
        scale = lax.rsqrt(jnp.mean(res * res, axis=1, keepdims=True) + EPSILON)
        second[r, :] = (res * scale * gain2[...]).astype(BF16)
        return 0
    lax.fori_loop(0, rows // 256, close, 0)
    for t in range(done, 2 * levels + 3): run(t)
    in_copy = pltpu.make_async_copy(w.at[1], in_o, store.at[4])
    in_copy.start()
    chunk = 512
    per = hidden // chunk
    def widen(i, _):
        slot = i % 2
        r = pl.ds(pl.multiple_of((i // per) * 256, 256), 256)
        c = pl.ds(pl.multiple_of((i % per) * chunk, chunk), chunk)
        gcopy = pltpu.make_async_copy(gp.at[slot], gp_o.at[r, c], gstore.at[slot])
        if comm:
            for t in range(max(done, 2 * levels + 3), len(steps)):
                @pl.when(i == 5 * (t - 2 * levels - 3 + 1))
                def _():
                    run(t)
        @pl.when(i >= 2)
        def _():
            gcopy.wait()
        a, grad = gelu_both(mm(second[r, :], w[1, :, c]))
        act[r, c] = a.astype(BF16)
        gp[slot] = grad.astype(BF16)
        gcopy.start()
        return 0
    lax.fori_loop(0, rows // 256 * per, widen, 0)
    act_copy = pltpu.make_async_copy(act, act_o, store.at[5])
    act_copy.start()
    back_copy = pltpu.make_async_copy(w.at[2], back_o, store.at[6])
    back_copy.start()
    def narrow(i, _):
        r = pl.ds(pl.multiple_of(i * 256, 256), 256)
        out[r, :] = (res_o[r, :] + mm(act[r, :], w[2], NT)).astype(out.dtype)
        return 0
    lax.fori_loop(0, rows // 256, narrow, 0)
    for c in [proj_copy, mixed_copy, *ctx_copies, in_copy, act_copy, back_copy]: c.wait()
    for slot in range(2):
        pltpu.make_async_copy(e.at[slot], e_o.at[0], estore.at[slot]).wait()
        pltpu.make_async_copy(gp.at[slot], gp_o.at[pl.ds(0, 256), pl.ds(0, chunk)], gstore.at[slot]).wait()
    if comm:
        for u in range(3): g.sendwait(u)

def forward(levels, tok, seg, gain1, table, gain2, piece=None, weights=None, schedule=()):
    comm = piece is not None
    rows, width = tok.shape
    heads = table.shape[1]
    inner = heads * HD
    hidden = (piece.shape[2] * 8) if comm else weights[2].shape[1]
    seqs, pairs = rows // SEQ, heads // 2
    sds = jax.ShapeDtypeStruct
    vm, hb = pl.BlockSpec(memory_space=pltpu.VMEM), pl.BlockSpec(memory_space=pl.ANY)
    outs = [(sds((rows, width), BF16), vm), (sds((width, 4 * inner), BF16), hb), (sds((width, hidden), BF16), hb), (sds((width, hidden), BF16), hb),
            (sds((rows, 3 * inner), BF16), hb), (sds((seqs * pairs, 2, SEQ, SEQ), BF16), hb), (sds((seqs * heads, 8, SEQ), F32), vm), (sds((rows, inner), BF16), hb), (sds((inner, rows), BF16), hb),
            (sds((rows, width), F32), vm), (sds((rows, hidden), BF16), hb), (sds((rows, hidden), BF16), hb)]
    scratch = [pltpu.VMEM((3, width, hidden), BF16), pltpu.VMEM((width, 4 * inner), BF16), pltpu.VMEM((rows, width), BF16), pltpu.VMEM((rows, 3 * inner), BF16),
               pltpu.VMEM((heads, EDGE, 2 * SEQ - EDGE), F32), pltpu.VMEM((seqs, SEQ, SEQ), F32), pltpu.VMEM((2, 2, SEQ, SEQ), BF16),
               pltpu.VMEM((rows, inner), BF16), pltpu.VMEM((inner, rows), BF16), pltpu.VMEM((rows, hidden), BF16), pltpu.VMEM((2, 256, 512), BF16), pltpu.VMEM((rows, width), BF16),
               pltpu.SemaphoreType.DMA((4,)), pltpu.SemaphoreType.DMA((7,)), pltpu.SemaphoreType.DMA((2,)), pltpu.SemaphoreType.DMA((2,))]
    if comm: scratch += gather_sems(3, levels)
    args = [tok, seg, gain1.astype(F32).reshape(1, width), jnp.pad(table.T, ((0, -heads % 16), (0, 0))), gain2.astype(F32).reshape(1, width)]
    specs = [vm] * 5
    if comm:
        args += [piece]; specs += [vm]
    else:
        args += list(weights); specs += [hb] * 4
    params = dict(collective_id=0, has_side_effects=True) if comm else {}
    return pl.pallas_call(functools.partial(forward_kernel, levels, comm, schedule), out_shape=[o[0] for o in outs], in_specs=specs, out_specs=[o[1] for o in outs],
        scratch_shapes=scratch, compiler_params=pltpu.CompilerParams(vmem_limit_bytes=63 << 20, **params), name="forward")(*args)

def transpose_into(src, dst):
    n, w = src.shape
    def one(i, _):
        r = pl.ds(pl.multiple_of(i * 128, 128), 128)
        for c in range(w // 128):
            dst[c * 128 : (c + 1) * 128, r] = src[r, c * 128 : (c + 1) * 128].T
        return 0
    lax.fori_loop(0, n // 128, one, 0)

def norm_back(v, dy, gain):
    r = lax.rsqrt(jnp.mean(v * v, axis=1, keepdims=True) + EPSILON)
    unit = v * r
    a = dy * gain
    part = r * (a - unit * jnp.mean(a * unit, axis=1, keepdims=True))
    return part, jnp.sum(dy * unit, axis=0, keepdims=True), unit

def backward_kernel(levels, comm, plan, gain1, gain2, rl, tok_h, cot_h, proj_h, in_h, back_h, mixed_h, e_h, ctx_h, ctxt_h, res_h, act_h, gp_h, *rest):
    if comm:
        (tg_o, small_o, qkv_o, out_o, gin_o, gback_o), rest = rest[:6], rest[6:]
    else:
        (tg_o, small_o, proj_o, gin_o, gback_o), rest = rest[:5], rest[5:]
    (u1, u2, b, t, f, e, qkv, racc, far, own, staged, load, stream, eload, qload, store), rest = rest[:16], rest[16:]
    rows, width = f.shape[1], f.shape[2]
    hidden = u1.shape[1]
    inner = width
    heads = racc.shape[0]
    pairs, seqs = heads // 2, rows // SEQ
    small, rest = rest[:5], rest[5:]
    def local(src, dst, sem):
        return pltpu.make_async_copy(src, dst, sem)
    loads = {"cot": local(cot_h, f.at[2], load.at[0]), "back": local(back_h, u1, load.at[1]), "res": local(res_h, f.at[0], load.at[2]), "in": local(in_h, u2, load.at[3])}
    chunk = hidden // 4
    if comm:
        cross, free = rest[:9], rest[9]
        me = Place()
        order = (me.gd, me.xd, me.yd, me.d)
        cols = [pl.ds(pl.multiple_of((o // 2) * chunk, chunk), chunk) for o in order]
    else:
        cols = [pl.ds(q * chunk, chunk) for q in range(4)]
    def act_load(q):
        return local(act_h.at[:, cols[q]], b.at[1 + q % 2], stream.at[0, q % 2])
    def gp_load(q):
        return local(gp_h.at[:, cols[q]], b.at[3 + q % 2], stream.at[1, q % 2])
    loads["cot"].start()
    act_load(0).start()
    loads["res"].start()
    loads["back"].start()
    gp_load(0).start()
    act_load(1).start()
    loads["in"].start()
    gp_load(1).start()
    if comm:
        greet_all(me, levels)
        sc = Scatter(me, levels, width // levels, own.shape[3], own, staged, u2, *cross)
        sm = Small(me, levels, *small)
        mine = sm.mine.at[0]
    else:
        mine = small[0].at[0]
    mine[...] = jnp.zeros(mine.shape, F32)
    racc[...] = jnp.zeros(racc.shape, F32)
    far[...] = jnp.zeros(far.shape, F32)
    loads["cot"].wait()
    def lower(i, _):
        r = pl.ds(pl.multiple_of(i * 128, 128), 128)
        b[0, r, :] = f[2, r, :].astype(BF16)
        return 0
    lax.fori_loop(0, rows // 128, lower, 0)
    transpose_into(b.at[0], t.at[0])
    loads["res"].wait()
    def renorm(i, _):
        r = pl.ds(pl.multiple_of(i * 128, 128), 128)
        v = f[0, r, :]
        s = lax.rsqrt(jnp.mean(v * v, axis=1, keepdims=True) + EPSILON)
        b[5, r, :] = (v * s * gain2[...]).astype(BF16)
        return 0
    lax.fori_loop(0, rows // 128, renorm, 0)
    transpose_into(b.at[5], t.at[1])
    half = chunk // 2
    def weight_grad(u, q, left, right):
        def one(i, _):
            r = pl.ds(pl.multiple_of(i * 256, 256), 256)
            g = mm(left[r, :], right[...]).astype(BF16)
            if comm:
                mine_first = me.c == 0
                own[u, q, r, :] = jnp.where(mine_first, g[:, :half], g[:, half:])
                staged[u, q % 2, r, :] = jnp.where(mine_first, g[:, half:], g[:, :half])
            else:
                own[u, q, r, :] = g[:, :half]
                staged[u, q % 2, r, :] = g[:, half:]
            return 0
        if q >= 2:
            if comm:
                sc.ccopy(u, q - 2).wait_send()
            else:
                put(u, q - 2)[1].wait()
        lax.fori_loop(0, width // 256, one, 0)
        if comm:
            sc.core_start(u, q)
        else:
            for c in put(u, q): c.start()
    def put(u, q):
        dst = (gback_o, gin_o)[u]
        return (local(own.at[u, q], dst.at[:, pl.ds(q * chunk, half)], store.at[u, 0, q]), local(staged.at[u, q % 2], dst.at[:, pl.ds(q * chunk + half, half)], store.at[u, 1, q]))
    def event(name, *a):
        if comm: getattr(sc, name)(*a)
    for q in range(4):
        act, gp = b.at[1 + q % 2], b.at[3 + q % 2]
        act_load(q).wait()
        weight_grad(0, q, t.at[0], act)
        if q + 2 < 4: act_load(q + 2).start()
        if q == 0: loads["back"].wait()
        gp_load(q).wait()
        def widen(i, _):
            r = pl.ds(pl.multiple_of(i * 256, 256), 256)
            b[5, r, :] = (mm(b[0, r, :], u1[:, cols[q]]) * gp[r, :].astype(F32)).astype(BF16)
            return 0
        lax.fori_loop(0, rows // 256, widen, 0)
        if q + 2 < 4: gp_load(q + 2).start()
        if q == 3:
            proj_load = local(proj_h, u1, load.at[4])
            proj_load.start()
        event("core_add", 0, q)
        weight_grad(1, q, t.at[1], b.at[5])
        if q == 0: loads["in"].wait()
        def narrow(i, _):
            r = pl.ds(pl.multiple_of(i * 256, 256), 256)
            g = mm(b[5, r, :], u2[:, cols[q]], NT)
            f[1, r, :] = g if q == 0 else f[1, r, :] + g
            return 0
        lax.fori_loop(0, rows // 256, narrow, 0)
        event("core_add", 1, q)
        if q == 2: event("cross_one", 0)
        if q == 3: event("cross_one", 1)
    ctx_loads = [local(ctx_h, b.at[5], load.at[5]), local(ctxt_h, t.at[2], load.at[6])]
    for c in ctx_loads: c.start()
    def norm_two(i, total):
        r = pl.ds(pl.multiple_of(i * 128, 128), 128)
        part, g, _ = norm_back(f[0, r, :], f[1, r, :], gain2[...])
        grad = f[2, r, :] + part
        f[0, r, :] = grad
        b[0, r, :] = grad.astype(BF16)
        return total + g
    mine[1:2, :] = lax.fori_loop(0, rows // 128, norm_two, jnp.zeros((1, width), F32))
    transpose_into(b.at[0], t.at[0])
    proj_load.wait()
    def context_back(i, _):
        r = pl.ds(pl.multiple_of(i * 256, 256), 256)
        b[4, r, :] = mm(b[0, r, :], u1[:, 3 * inner :]).astype(BF16)
        return 0
    lax.fori_loop(0, rows // 256, context_back, 0)
    for c in ctx_loads: c.wait()
    def out_grad(i, _):
        r = pl.ds(pl.multiple_of(i * 256, 256), 256)
        b[6, r, :] = mm(t[0, r, :], b[5]).astype(BF16)
        return 0
    lax.fori_loop(0, width // 256, out_grad, 0)
    tok_load = local(tok_h, b.at[0], load.at[7])
    tok_load.start()
    tok_load.wait()
    def renorm_one(i, _):
        r = pl.ds(pl.multiple_of(i * 128, 128), 128)
        v = b[0, r, :].astype(F32)
        s = lax.rsqrt(jnp.mean(v * v, axis=1, keepdims=True) + EPSILON)
        b[5, r, :] = (v * s * gain1[...]).astype(BF16)
        return 0
    lax.fori_loop(0, rows // 128, renorm_one, 0)
    transpose_into(b.at[5], t.at[1])
    n = seqs * pairs
    def fetch(i, slot):
        s, p = i // pairs, i % pairs
        row = pl.ds(pl.multiple_of(s * SEQ, SEQ), SEQ)
        return [local(e_h.at[i], e.at[slot], eload.at[slot])] + [
            local(mixed_h.at[row, pl.ds(pl.multiple_of(k * inner + p * 128, 128), 128)], qkv.at[slot, k], qload.at[slot, k]) for k in range(3)]
    for c in fetch(0, 0): c.start()
    low_lanes = lax.broadcasted_iota(jnp.int32, (SEQ, 128), 1) < HD
    blocks = SEQ // EDGE
    def attend_back(i, _):
        s, p = i // pairs, i % pairs
        slot = i % 2
        @pl.when(i + 1 < n)
        def _():
            for c in fetch(i + 1, (i + 1) % 2): c.start()
        for at, name, args in plan:
            @pl.when(i == at)
            def _():
                event(name, *args)
        for c in fetch(i, slot): c.wait()
        row = pl.ds(pl.multiple_of(s * SEQ, SEQ), SEQ)
        off = pl.multiple_of(p * 128, 128)
        q, k, v = qkv[slot, 0] * jnp.asarray(SCALING, BF16), qkv[slot, 1], qkv[slot, 2]
        k_t = k.T
        do_t = b[4, row, pl.ds(off, 128)].T.astype(F32)
        o_t = t[2, pl.ds(off, 128), row].astype(F32)
        scaled = []
        for a in range(2):
            part = do_t[a * HD : (a + 1) * HD] * rl[s * heads + 2 * p + a, :1, :]
            scaled.append(part.astype(BF16))
        dos_t = jnp.concatenate(scaled, axis=0)
        dos = dos_t.T
        prod = dos_t.astype(F32) * o_t
        dq, dk, dv = [], [], []
        for a in range(2):
            h = 2 * p + a
            delta = jnp.sum(prod[a * HD : (a + 1) * HD], axis=0, keepdims=True)
            va = jnp.where(low_lanes == (a == 0), v, jnp.zeros_like(v))
            low = []
            sums = [None] * 3
            fars = [None] * 2
            for kb in range(blocks):
                ek = e[slot, a, kb * EDGE : (kb + 1) * EDGE, :]
                ds = ek.astype(F32) * (mm(va[kb * EDGE : (kb + 1) * EDGE], dos_t) - delta)
                low.append(ds.astype(BF16))
                for qb in range(blocks):
                    piece = ds[:, qb * EDGE : (qb + 1) * EDGE]
                    gap = kb - qb
                    if abs(gap) <= 1:
                        sums[gap + 1] = piece if sums[gap + 1] is None else sums[gap + 1] + piece
                    else:
                        w = 1 if gap > 0 else 0
                        piece = jnp.sum(piece.reshape(EDGE // 8, 8, EDGE), axis=0)
                        fars[w] = piece if fars[w] is None else fars[w] + piece
            for w in range(3):
                racc[h, w] += sums[w]
            for w in range(2):
                far[h, w] += fars[w]
            low = jnp.concatenate(low, axis=0)
            dv.append(mm(e[slot, a], dos))
            dk.append(mm(low, q))
            dq.append(mm(k_t[a * HD : (a + 1) * HD], low))
        b[1, row, pl.ds(off, 128)] = (jnp.concatenate(dq, axis=0) * SCALING).astype(BF16).T
        b[2, row, pl.ds(off, 128)] = jnp.where(low_lanes, dk[0], dk[1]).astype(BF16)
        b[3, row, pl.ds(off, 128)] = jnp.where(low_lanes, dv[0], dv[1]).astype(BF16)
        return 0
    lax.fori_loop(0, n, attend_back, 0)
    if comm:
        for u in range(2):
            (gback_o, gin_o)[u][...] = sc.finish(u)
        for u in range(2): sc.sendwait(u)
        sc.release(free)
    part, packed = own.shape[3] * 3 // 4, own.shape[3]
    def proj_grad(i, _):
        r = pl.ds(pl.multiple_of(i * 256, 256), 256)
        left = t[1, r, :]
        g = jnp.concatenate([mm(left, b[1 + k]).astype(BF16) for k in range(3)], axis=1)
        o = b[6, r, :]
        if comm:
            quarter = packed - part
            for d in range(hidden // packed):
                u2[r, d * packed : (d + 1) * packed] = jnp.concatenate([g[:, d * part : (d + 1) * part], o[:, d * quarter : (d + 1) * quarter]], axis=1)
        else:
            u2[r, : 3 * inner] = g
            u2[r, 3 * inner :] = o
        return 0
    lax.fori_loop(0, width // 256, proj_grad, 0)
    if comm:
        sc.acquire(free)
        for q in range(4): sc.core_start(2, q)
    else:
        proj_put = local(u2, proj_o, store.at[0, 0, 4])
        proj_put.start()
    span = 2 * EDGE
    c = lax.broadcasted_iota(jnp.int32, (span, 128), 0)
    offs = EDGE - 1 - c
    bucket_lane = lax.broadcasted_iota(jnp.int32, (span, 128), 1)
    hots = [(bucket_of(offs + EDGE * w) == bucket_lane).astype(F32) for w in (-1, 0, 1)]
    lane = lax.broadcasted_iota(jnp.int32, (1, 128), 1)
    mirror = (lax.broadcasted_iota(jnp.int32, (EDGE, EDGE), 0) + lax.broadcasted_iota(jnp.int32, (EDGE, EDGE), 1) == EDGE - 1).astype(F32)
    at_row = lax.broadcasted_iota(jnp.int32, (16, 128), 0)
    def table_one(h, held):
        total = jnp.zeros((8, 128), F32)
        for w in range(3):
            upended = lax.dot_general(mirror, racc[h, w], NN, precision=lax.Precision.HIGHEST, preferred_element_type=F32)
            wide = jnp.concatenate([upended, jnp.zeros((EDGE, EDGE), F32)], axis=1)
            turned = pltpu.roll(wide, 0, 1, stride=1, stride_axis=0)
            diag = jnp.sum(turned.reshape(EDGE // 8, 8, span), axis=0)
            total = total + lax.dot_general(diag, hots[w], NN, precision=lax.Precision.HIGHEST, preferred_element_type=F32)
        row = jnp.sum(total, axis=0, keepdims=True)
        left = jnp.sum(far[h, 0])
        right = jnp.sum(far[h, 1])
        row = row + jnp.where(lane == BUCKETS // 2 - 1, left, 0.0) + jnp.where(lane == BUCKETS - 1, right, 0.0)
        return held + jnp.where(at_row == 2 + h, row, 0.0)
    mine[:, :128] += lax.fori_loop(0, heads, table_one, jnp.zeros((16, 128), F32))
    if comm:
        for q in range(4): sc.core_add(2, q)
    def norm_one(i, total):
        r = pl.ds(pl.multiple_of(i * 256, 256), 256)
        dy = mm(b[1, r, :], u1[:, :inner], NT) + mm(b[2, r, :], u1[:, inner : 2 * inner], NT) + mm(b[3, r, :], u1[:, 2 * inner : 3 * inner], NT)
        part, g, _ = norm_back(b[0, r, :].astype(F32), dy, gain1[...])
        f[1, r, :] = f[0, r, :] + part
        return total + g
    mine[0:1, :] = lax.fori_loop(0, rows // 256, norm_one, jnp.zeros((1, width), F32))
    tg_copy = local(f.at[1], tg_o, load.at[8])
    tg_copy.start()
    if comm:
        sm.start(0)
        sc.cross_one(2)
        sm.add(0); sm.start(1)
        sc.cross_two(2)
        sm.add(1); sm.start(2)
        sc.cross_three(2)
        sc.line_step(2, 0)
        sm.add(2); sm.spread()
        for i in range(1, levels - 1): sc.line_step(2, i)
        total = sc.finish(2)
        qkv_o[...] = total[:, :part]
        out_o[...] = total[:, part:]
        small_o[...] = sm.total()
        sc.sendwait(2)
        sm.sendwait()
    else:
        small_o[...] = mine[...]
        for u in range(2):
            for q in range(4):
                x, y = put(u, q)
                x.wait()
                if q >= 2: y.wait()
        proj_put.wait()
    tg_copy.wait()

def backward(levels, comm, plan, gain1, gain2, rl, tok, cot, proj, w_in, w_back, mixed, e, ctx, ctxt, res, act, gp, share=None):
    rows, width = tok.shape
    hidden = w_in.shape[1]
    heads = rl.shape[0] // (rows // SEQ)
    sds = jax.ShapeDtypeStruct
    vm, hb = pl.BlockSpec(memory_space=pltpu.VMEM), pl.BlockSpec(memory_space=pl.ANY)
    shape = (16, width)
    half = hidden // 8
    piece_rows = width // levels
    outs = [(sds((rows, width), F32), hb), (sds(shape, F32), vm)]
    if comm:
        outs += [(sds((piece_rows, half * 3 // 4), F32), vm), (sds((piece_rows, half // 4), F32), vm), (sds((piece_rows, half), F32), vm), (sds((piece_rows, half), F32), vm)]
    else:
        outs += [(sds((width, hidden), BF16), hb)] * 3
    D = pltpu.SemaphoreType.DMA
    scratch = [pltpu.VMEM((width, hidden), BF16), pltpu.VMEM((width, hidden), BF16), pltpu.VMEM((7, rows, width), BF16), pltpu.VMEM((3, width, rows), BF16), pltpu.VMEM((3, rows, width), F32),
               pltpu.VMEM((2, 2, SEQ, SEQ), BF16), pltpu.VMEM((2, 3, SEQ, 128), BF16), pltpu.VMEM((heads, 3, EDGE, EDGE), F32), pltpu.VMEM((heads, 2, 8, EDGE), F32),
               pltpu.VMEM((2, 4, width, half), BF16), pltpu.VMEM((2, 2, width, half), BF16), D((9,)), D((2, 2)), D((2,)), D((2, 3)), D((2, 2, 5))] + small_scratch(levels, shape)
    if comm:
        scratch += [pltpu.VMEM((2, 4, width, half), BF16), pltpu.VMEM((2, 2, 3, width // 2, half), BF16), pltpu.VMEM((2, 2, levels - 1, piece_rows, half), BF16),
                    D((3, 4)), D((3, 4)), D((3, 2, 3)), D((3, 2, 3)), D((3, 2, levels - 1)), D((3, 2, levels - 1)), pltpu.SemaphoreType.REGULAR]
    params = dict(collective_id=1, has_side_effects=True) if comm else {}
    g = lambda x: x.astype(F32).reshape(1, width)
    return pl.pallas_call(functools.partial(backward_kernel, levels, comm, plan), out_shape=[o[0] for o in outs], in_specs=[vm] * 3 + [hb] * 12, out_specs=[o[1] for o in outs],
        scratch_shapes=scratch, compiler_params=pltpu.CompilerParams(vmem_limit_bytes=63 << 20, **params), name="backward")(g(gain1), g(gain2), rl, tok, cot, proj, w_in, w_back, mixed, e, ctx, ctxt, res, act, gp)

def scatter_plain(grad):
    part = lax.psum_scatter(grad, "dp", scatter_dimension=1, tiled=True)
    return lax.psum_scatter(part, "mp", scatter_dimension=0, tiled=True).astype(F32)


FORWARD_PLAN = ((7, 1), (8, 4), (9, 7), (10, 10))
BACKWARD_PLAN = (
    (1, "cross_two", (0,)), (2, "cross_two", (1,)), (4, "cross_three", (0,)), (4, "line_step", (0, 0)), (5, "line_step", (0, 1)),
    (6, "cross_three", (1,)), (6, "line_step", (1, 0)), (7, "line_step", (0, 2)), (8, "line_step", (1, 1)), (10, "line_step", (1, 2)),
)


def body(tokens, segment_ids, cotangent, gain_one, w_qkv, w_out, rel_table, gain_two, w_in, w_back):
    axes = ("mp", "dp")
    levels, width = lax.axis_size("mp"), lax.axis_size("dp")
    heads = rel_table.shape[1]
    inner = heads * HD
    segments = segment_ids.reshape(-1, SEQ).astype(F32)
    packed = w_qkv.shape[1] + w_out.shape[1]
    own = width == 8 and levels == 4 and packed == w_in.shape[1] and packed % 128 == 0
    if own:
        piece = jnp.stack([jnp.concatenate([w_qkv, w_out], axis=1), w_in, w_back])
        held = forward(levels, tokens, segments, gain_one, rel_table, gain_two, piece=piece, schedule=FORWARD_PLAN)
    else:
        whole = [lax.all_gather(lax.all_gather(m, "mp", axis=0, tiled=True), "dp", axis=1, tiled=True) for m in (w_qkv, w_out, w_in, w_back)]
        held = forward(levels, tokens, segments, gain_one, rel_table, gain_two, weights=whole)
    layer_out, proj, full_in, full_back, mixed, e, rl, ctx, ctxt, res, act, gp = held
    grads = backward(levels, own, BACKWARD_PLAN, gain_one, gain_two, rl, tokens, cotangent, proj, full_in, full_back, mixed, e, ctx, ctxt, res, act, gp)
    if own:
        tokens_grad, small, qkv_grad, out_grad, in_grad, back_grad = grads
    else:
        tokens_grad, small, proj_grad, in_grad, back_grad = grads
        small = lax.psum(small, axes)
        qkv_grad, out_grad = scatter_plain(proj_grad[:, : 3 * inner]), scatter_plain(proj_grad[:, 3 * inner :])
        in_grad, back_grad = scatter_plain(in_grad), scatter_plain(back_grad)
    table_grad = small[2 : 2 + heads, :BUCKETS].T
    return layer_out, tokens_grad, small[0], qkv_grad, out_grad, table_grad, small[1], in_grad, back_grad


def solution(mesh):
    both = ("mp", "dp")
    weight = P("mp", "dp")
    return jax.shard_map(
        body,
        mesh=mesh,
        in_specs=(P(both, None), P(both), P(both, None), P(), weight, weight, P(), P(), weight, weight),
        out_specs=(P(both, None), P(both, None), P(), weight, weight, P(), P(), weight, weight),
        check_vma=False,
    )
```

```python
import functools

import jax
import jax.numpy as jnp
from jax import lax
from jax.experimental import pallas as pl
from jax.experimental.pallas import tpu as pltpu
from jax.sharding import PartitionSpec as P

MESH = pl.DeviceIdType.MESH

class Place:
    def __init__(self):
        self.z = lax.axis_index("mp"); self.d = lax.axis_index("dp")
        d = self.d
        self.c = lax.rem(d, 2); self.x = lax.rem(d // 2, 2); self.y = d // 4
        self.xd = d + 2 - 4 * self.x
        self.yd = d + 4 - 8 * self.y
        self.cd = d + 1 - 2 * self.c
        self.gd = self.xd + 4 - 8 * self.y
    def barrier(self, levels):
        bar = pltpu.get_barrier_semaphore()
        for t in (self.xd, self.yd, self.cd):
            pl.semaphore_signal(bar, inc=1, device_id=(self.z, t), device_id_type=MESH)
        @pl.when(self.z > 0)
        def _():
            pl.semaphore_signal(bar, inc=1, device_id=(self.z - 1, self.d), device_id_type=MESH)
        @pl.when(self.z < levels - 1)
        def _():
            pl.semaphore_signal(bar, inc=1, device_id=(self.z + 1, self.d), device_id_type=MESH)
        peers = 3 + jnp.minimum(self.z, 1) + jnp.minimum(levels - 1 - self.z, 1)
        pl.semaphore_wait(bar, peers)

class Gather:
    def __init__(self, me, levels, piece, full, zs, zr, xs, xr, cs, cr):
        self.me, self.levels, self.piece, self.full = me, levels, piece, full
        self.zs, self.zr, self.xs, self.xr, self.cs, self.cr = zs, zr, xs, xr, cs, cr
        self.rows, self.cols = piece.shape[1], piece.shape[2]
    def blk(self, u, z, d, r0=0, nr=None):
        nr = self.rows if nr is None else nr
        return self.full.at[u, pl.ds(pl.multiple_of(z * self.rows + r0, 16), nr), pl.ds(pl.multiple_of(d * self.cols, 128), self.cols)]
    def col(self, u, d):
        return self.full.at[u, :, pl.ds(pl.multiple_of(d * self.cols, 128), self.cols)]
    def cp(self, src, dst, ss, rs, dev):
        return pltpu.make_async_remote_copy(src_ref=src, dst_ref=dst, send_sem=ss, recv_sem=rs, device_id=dev, device_id_type=MESH)
    def zcopy(self, u, up, k, z, src=None):
        b = self.blk(u, z, self.me.d)
        t = self.me.z + (1 if up else -1)
        return self.cp(b if src is None else src, b, self.zs.at[u, 0 if up else 1, k], self.zr.at[u, 0 if up else 1, k], (t, self.me.d))
    def xcopy(self, u, z, d, src=None):
        b = self.blk(u, z, d)
        return self.cp(b if src is None else src, b, self.xs.at[u, 0, z], self.xr.at[u, 0, z], (self.me.z, self.me.xd))
    def ycopy(self, u, z, d, src=None):
        b = self.blk(u, z, d)
        return self.cp(b if src is None else src, b, self.xs.at[u, 1, z], self.xr.at[u, 1, z], (self.me.z, self.me.yd))
    def half(self, u, z, d, way):
        h = self.rows // 2
        b = self.blk(u, z, d, way * h, h)
        return self.cp(b, b, self.xs.at[u, 2 + way, z], self.xr.at[u, 2 + way, z], (self.me.z, self.me.yd if way == 0 else self.me.xd))
    def ccopy(self, u, which, d):
        b = self.col(u, d)
        return self.cp(b, b, self.cs.at[u, which], self.cr.at[u, which], (self.me.z, self.me.cd))
    def zstep(self, u, k):
        me = self.me
        if k == 0:
            src = self.piece.at[u]
            self.xcopy(u, me.z, me.d, src).start()
            self.ycopy(u, me.z, me.d, src).start()
            @pl.when(me.z < self.levels - 1)
            def _():
                self.zcopy(u, True, 0, me.z, src).start()
            @pl.when(me.z > 0)
            def _():
                self.zcopy(u, False, 0, me.z, src).start()
            self.blk(u, me.z, me.d)[...] = self.piece[u]
            return
        @pl.when(me.z - k >= 0)
        def _():
            z = me.z - k
            self.zcopy(u, True, k - 1, z).wait_recv()
            if k < self.levels - 1:
                @pl.when(me.z < self.levels - 1)
                def _():
                    self.zcopy(u, True, k, z).start()
            self.xcopy(u, z, me.d).start()
            self.ycopy(u, z, me.d).start()
        @pl.when(me.z + k < self.levels)
        def _():
            z = me.z + k
            self.zcopy(u, False, k - 1, z).wait_recv()
            if k < self.levels - 1:
                @pl.when(me.z > 0)
                def _():
                    self.zcopy(u, False, k, z).start()
            self.xcopy(u, z, me.d).start()
            self.ycopy(u, z, me.d).start()
    def xystep(self, u, k):
        me = self.me
        def one(z):
            self.xcopy(u, z, me.xd).wait_recv()
            self.half(u, z, me.xd, 0).start()
            self.ycopy(u, z, me.yd).wait_recv()
            self.half(u, z, me.yd, 1).start()
        if k == 0:
            one(me.z)
            return
        @pl.when(me.z - k >= 0)
        def _():
            one(me.z - k)
        @pl.when(me.z + k < self.levels)
        def _():
            one(me.z + k)
    def corestep(self, u, which):
        me = self.me
        self.ccopy(u, which, (me.d, me.xd, me.yd, me.gd)[which]).start()
    def diagstep(self, u):
        me = self.me
        for z in range(self.levels):
            self.half(u, z, me.gd, 0).wait_recv()
            self.half(u, z, me.gd, 1).wait_recv()
    def corewait(self, u):
        me = self.me
        for which in range(4):
            self.ccopy(u, which, (me.cd, me.cd + me.xd - me.d, me.cd + me.yd - me.d, me.cd + me.gd - me.d)[which]).wait_recv()
    def sendwait(self, u):
        me = self.me
        for k in range(self.levels - 1):
            @pl.when((me.z < self.levels - 1) & (me.z - k >= 0))
            def _():
                self.zcopy(u, True, k, me.z - k).wait_send()
            @pl.when((me.z > 0) & (me.z + k < self.levels))
            def _():
                self.zcopy(u, False, k, me.z + k).wait_send()
        for z in range(self.levels):
            self.xcopy(u, z, me.d).wait_send()
            self.ycopy(u, z, me.d).wait_send()
            self.half(u, z, me.xd, 0).wait_send()
            self.half(u, z, me.yd, 1).wait_send()
        for which in range(4):
            self.ccopy(u, which, me.d).wait_send()
    def events(self, units):
        L = self.levels
        out = []
        n = units * L
        for s in range(n + 3):
            step = []
            u, k = divmod(s, L)
            if s < n:
                step.append(functools.partial(self.zstep, u, k))
                if k == L - 1:
                    step.append(functools.partial(self.corestep, u, 0))
            t = s - 1
            if 0 <= t < n:
                u, k = divmod(t, L)
                step.append(functools.partial(self.xystep, u, k))
                if k == L - 1:
                    step.append(functools.partial(self.corestep, u, 1))
                    step.append(functools.partial(self.corestep, u, 2))
            t = s - 2
            if 0 <= t < n:
                u, k = divmod(t, L)
                if k == L - 1:
                    step.append(functools.partial(self.diagstep, u))
                    step.append(functools.partial(self.corestep, u, 3))
            t = s - 3
            if 0 <= t < n:
                u, k = divmod(t, L)
                if k == L - 1:
                    step.append(functools.partial(self.corewait, u))
            out.append(step)
        return out

def gather_sems(units, levels):
    return [pltpu.SemaphoreType.DMA((units, 2, levels - 1))] * 2 + [pltpu.SemaphoreType.DMA((units, 4, levels))] * 2 + [pltpu.SemaphoreType.DMA((units, 4))] * 2

def greet_all(me, levels):
    bar = pltpu.get_barrier_semaphore()
    for t in (me.xd, me.yd, me.cd):
        pl.semaphore_signal(bar, inc=1, device_id=(me.z, t), device_id_type=MESH)
    for k in range(1, levels):
        pl.semaphore_signal(bar, inc=1, device_id=(lax.rem(me.z + k, levels), me.d), device_id_type=MESH)
    pl.semaphore_wait(bar, 2 + levels)

class Scatter:
    def __init__(self, me, levels, rows, cols, own, staged, matrix, core, cross, line, cs, cr, xs, xr, zs, zr):
        self.me, self.levels, self.rows, self.cols = me, levels, rows, cols
        self.grads, self.staged, self.matrix = own, staged, matrix
        self.core, self.cross, self.line = core, cross, line
        self.cs, self.cr, self.xs, self.xr, self.zs, self.zr = cs, cr, xs, xr, zs, zr
        self.order = (me.gd, me.xd, me.yd, me.d)
        self.half_rows = rows * levels // 2
    def cp(self, src, dst, ss, rs, dev):
        return pltpu.make_async_remote_copy(src_ref=src, dst_ref=dst, send_sem=ss, recv_sem=rs, device_id=dev, device_id_type=MESH)
    def add(self, dst, src):
        n = dst.shape[0]
        step = 96 if n % 96 == 0 else 16
        def one(i, _):
            at = pl.ds(pl.multiple_of(i * step, 16), step)
            dst[at, :] = dst[at, :] + src[at, :]
            return 0
        lax.fori_loop(0, n // step, one, 0)
    def core_start(self, u, q):
        self.ccopy(u, q).start()
    def index(self, d):
        return [i for i, o in enumerate(self.order) if o is d][0]
    def block(self, u, d, r0, nr):
        at = pl.ds(r0 if isinstance(r0, int) else pl.multiple_of(r0, 16), nr)
        if u < 2:
            return self.grads.at[u, self.index(d), at]
        return self.matrix.at[at, pl.ds(pl.multiple_of(d * self.cols, 128), self.cols)]
    def slot(self, u):
        return 0 if u == 2 else u
    def ccopy(self, u, q):
        s = self.slot(u)
        if u < 2:
            src = self.staged.at[u, q % 2]
        else:
            src = self.block(u, self.order[q] + self.me.cd - self.me.d, 0, self.rows * self.levels)
        return self.cp(src, self.core.at[s, q], self.cs.at[u, q], self.cr.at[u, q], (self.me.z, self.me.cd))
    def core_add(self, u, q):
        self.ccopy(u, q).wait_recv()
        self.add(self.block(u, self.order[q], 0, self.rows * self.levels), self.core.at[self.slot(u), q])
        if q == 0:
            self.xcopy(u, 0).start()
            self.ycopy(u, 0).start()
        if q == 1:
            self.xcopy(u, 1).start()
        if q == 2:
            self.ycopy(u, 1).start()
    def xcopy(self, u, slot):
        d = (self.me.gd, self.me.xd, self.me.xd)[slot]
        r0 = (0, 0, self.half_rows)[slot]
        return self.cp(self.block(u, d, r0, self.half_rows), self.cross.at[self.slot(u), 0, slot], self.xs.at[u, 0, slot], self.xr.at[u, 0, slot], (self.me.z, self.me.xd))
    def ycopy(self, u, slot):
        d = (self.me.gd, self.me.yd, self.me.yd)[slot]
        r0 = (self.half_rows, self.half_rows, 0)[slot]
        return self.cp(self.block(u, d, r0, self.half_rows), self.cross.at[self.slot(u), 1, slot], self.xs.at[u, 1, slot], self.xr.at[u, 1, slot], (self.me.z, self.me.yd))
    def zcopy(self, u, way, target):
        slot = target - 1 if way == 0 else target
        t = self.me.z + (1 if way == 0 else -1)
        return self.cp(self.block(u, self.me.d, target * self.rows, self.rows), self.line.at[self.slot(u), way, slot], self.zs.at[u, way, slot], self.zr.at[u, way, slot], (t, self.me.d))
    def cross_one(self, u):
        me, h, s = self.me, self.half_rows, self.slot(u)
        self.xcopy(u, 0).wait_recv()
        self.add(self.block(u, me.yd, 0, h), self.cross.at[s, 0, 0])
        self.ycopy(u, 2).start()
        self.ycopy(u, 0).wait_recv()
        self.add(self.block(u, me.xd, h, h), self.cross.at[s, 1, 0])
        self.xcopy(u, 2).start()
    def cross_two(self, u):
        me, h, s = self.me, self.half_rows, self.slot(u)
        self.xcopy(u, 1).wait_recv()
        self.add(self.block(u, me.d, 0, h), self.cross.at[s, 0, 1])
        self.ycopy(u, 1).wait_recv()
        self.add(self.block(u, me.d, h, h), self.cross.at[s, 1, 1])
    def cross_three(self, u):
        me, h, s = self.me, self.half_rows, self.slot(u)
        self.ycopy(u, 2).wait_recv()
        self.add(self.block(u, me.d, 0, h), self.cross.at[s, 1, 2])
        self.xcopy(u, 2).wait_recv()
        self.add(self.block(u, me.d, h, h), self.cross.at[s, 0, 2])
    def line_open(self, u):
        me, last = self.me, self.levels - 1
        @pl.when(me.z == 0)
        def _():
            for i in range(last):
                self.zcopy(u, 0, last - i).start()
        @pl.when(me.z == last)
        def _():
            for i in range(last):
                self.zcopy(u, 1, i).start()
    def line_step(self, u, k):
        me, last, s = self.me, self.levels - 1, self.slot(u)
        def take(way, target):
            self.zcopy(u, way, target).wait_recv()
            if k < last:
                at = target - 1 if way == 0 else target
                self.add(self.block(u, me.d, target * self.rows, self.rows), self.line.at[s, way, at])
                self.zcopy(u, way, target).start()
        @pl.when((me.z >= 1) & (me.z <= k))
        def _():
            take(0, last - k + me.z)
        @pl.when((me.z <= last - 1) & (me.z >= last - k))
        def _():
            take(1, k - last + me.z)
    def finish(self, u):
        me, last, s = self.me, self.levels - 1, self.slot(u)
        own = self.block(u, me.d, me.z * self.rows, self.rows)[...].astype(F32)
        below = self.line[s, 0, jnp.maximum(me.z - 1, 0)].astype(F32)
        above = self.line[s, 1, jnp.minimum(me.z, last - 1)].astype(F32)
        return own + jnp.where(me.z > 0, below, 0.0) + jnp.where(me.z < last, above, 0.0)
    def release(self, free):
        me, last = self.me, self.levels - 1
        for t in (me.xd, me.yd, me.cd):
            pl.semaphore_signal(free, inc=1, device_id=(me.z, t), device_id_type=MESH)
        @pl.when(me.z > 0)
        def _():
            pl.semaphore_signal(free, inc=1, device_id=(me.z - 1, me.d), device_id_type=MESH)
        @pl.when(me.z < last)
        def _():
            pl.semaphore_signal(free, inc=1, device_id=(me.z + 1, me.d), device_id_type=MESH)
    def acquire(self, free):
        me, last = self.me, self.levels - 1
        pl.semaphore_wait(free, 3 + jnp.minimum(me.z, 1) + jnp.minimum(last - me.z, 1))
    def sendwait(self, u):
        me, last = self.me, self.levels - 1
        for q in range(4):
            if u == 2 or q >= 2: self.ccopy(u, q).wait_send()
        for slot in range(3):
            self.xcopy(u, slot).wait_send()
            self.ycopy(u, slot).wait_send()
        for i in range(last):
            @pl.when(me.z < last - i)
            def _():
                self.zcopy(u, 0, last - i).wait_send()
            @pl.when(me.z > i)
            def _():
                self.zcopy(u, 1, i).wait_send()

class Small:
    def __init__(self, me, levels, mine, swap, slots, ss, rs):
        self.me, self.levels, self.mine, self.swap, self.slots, self.ss, self.rs = me, levels, mine, swap, slots, ss, rs
    def pair(self, i):
        t = (self.me.cd, self.me.xd, self.me.yd)[i]
        return pltpu.make_async_remote_copy(src_ref=self.mine.at[i], dst_ref=self.swap.at[i], send_sem=self.ss.at[i], recv_sem=self.rs.at[i], device_id=(self.me.z, t), device_id_type=MESH)
    def start(self, i):
        self.pair(i).start()
    def add(self, i):
        self.pair(i).wait_recv()
        self.mine[i + 1] = self.mine[i] + self.swap[i]
    def level(self, k):
        t = lax.rem(self.me.z + k, self.levels)
        return pltpu.make_async_remote_copy(src_ref=self.mine.at[3], dst_ref=self.slots.at[k - 1], send_sem=self.ss.at[2 + k], recv_sem=self.rs.at[2 + k], device_id=(t, self.me.d), device_id_type=MESH)
    def spread(self):
        for k in range(1, self.levels):
            self.level(k).start()
    def total(self):
        for k in range(1, self.levels):
            self.level(k).wait_recv()
        def at(level):
            k = lax.rem(self.me.z - level + self.levels, self.levels)
            held = self.slots[jnp.maximum(k - 1, 0)]
            return jnp.where(k == 0, self.mine[3], held)
        out = at(0)
        for level in range(1, self.levels):
            out = out + at(level)
        return out
    def sendwait(self):
        for i in range(3):
            self.pair(i).wait_send()
        for k in range(1, self.levels):
            self.level(k).wait_send()

def small_scratch(levels, shape):
    return [pltpu.VMEM((4, *shape), jnp.float32), pltpu.VMEM((3, *shape), jnp.float32), pltpu.VMEM((levels - 1, *shape), jnp.float32),
            *[pltpu.SemaphoreType.DMA((2 + levels,))] * 2]

SEQ, HD, BUCKETS = 512, 64, 32
EPSILON = 1e-06
NEGATIVE = -1e30
SCALING = 0.125
THRESHOLDS = (12, 16, 23, 32, 46, 64, 91)
F32, BF16 = jnp.float32, jnp.bfloat16
EDGE = 128
NT = (((1,), (1,)), ((), ()))
NN = (((1,), (0,)), ((), ()))

def mm(a, b, dims=NN):
    return lax.dot_general(a, b, dims, preferred_element_type=F32)

def bucket_of(offset):
    distance = jnp.abs(offset)
    larger = jnp.zeros_like(distance)
    for edge in THRESHOLDS:
        larger = larger + (distance >= edge).astype(jnp.int32)
    inside = jnp.where(distance < 8, distance, 8 + larger)
    return inside + BUCKETS // 2 * (offset > 0).astype(jnp.int32)

def build_bias(table_t, skew):
    heads, edge, width = skew.shape
    span = 1024
    c = lax.broadcasted_iota(jnp.int32, (BUCKETS, span), 1)
    c = jnp.where(c >= span - EDGE, c - span, c)
    hot = (bucket_of((SEQ - EDGE) - c) == lax.broadcasted_iota(jnp.int32, (BUCKETS, span), 0)).astype(BF16)
    flat = mm(table_t, hot)
    for h in range(heads):
        rows = jnp.broadcast_to(flat[h : h + 1, :], (edge, span))
        skew[h] = pltpu.roll(rows, 0, 1, stride=1, stride_axis=0)[:, :width]

def build_mask(seg, mask):
    wide = jnp.broadcast_to(seg, (EDGE, SEQ))
    for b in range(SEQ // EDGE):
        col = wide[:, b * EDGE : (b + 1) * EDGE].T
        tall = jnp.concatenate([col] * (SEQ // EDGE), axis=1)
        same = (tall == wide) & (wide > 0.0)
        k = lax.broadcasted_iota(jnp.int32, (EDGE, SEQ), 0) + b * EDGE
        q = lax.broadcasted_iota(jnp.int32, (EDGE, SEQ), 1)
        mask[b * EDGE : (b + 1) * EDGE, :] = jnp.where(same | (k == q), 0.0, NEGATIVE)

def transpose(x):
    return x.T

GELU_C = 0.7978845608028654
def gelu_both(x):
    x2 = x * x
    t = jnp.tanh(x * (GELU_C + (GELU_C * 0.044715) * x2))
    half = 0.5 * x
    one = 0.5 + 0.5 * t
    act = x * one
    grad = one + (half * (1.0 - t * t)) * (GELU_C + (3.0 * 0.044715 * GELU_C) * x2)
    return act, grad

def forward_kernel(levels, comm, schedule, tok, seg, gain1, table_t, gain2, *rest):
    if comm:
        piece, rest = rest[0], rest[1:]
    else:
        weights, rest = rest[:4], rest[4:]
    (out, proj_o, in_o, back_o, mixed_o, e_o, rl_o, ctx_o, ctxt_o, res_o, act_o, gp_o), rest = rest[:12], rest[12:]
    (w, proj, normed, mixed, skew, mask, e, ctx, ctxt, act, gp, second, load, store, estore, gstore), sems = rest[:16], rest[16:]
    rows, width = tok.shape
    inner = width
    heads = skew.shape[0]
    pairs = heads // 2
    seqs = rows // SEQ
    hidden = act.shape[1]
    if comm:
        me = Place()
        me.barrier(levels)
        g = Gather(me, levels, piece, w, *sems)
        steps = g.events(3)
    else:
        steps = []
    def run(t):
        if t < len(steps):
            for call in steps[t]: call()
    if not comm:
        loads = [pltpu.make_async_copy(weights[0], proj.at[:, : 3 * inner], load.at[0]), pltpu.make_async_copy(weights[1], proj.at[:, 3 * inner :], load.at[1]),
                 pltpu.make_async_copy(weights[2], w.at[1], load.at[2]), pltpu.make_async_copy(weights[3], w.at[2], load.at[3])]
        for l in loads: l.start()
        for l in loads: l.wait()
    run(0)
    def norm_one(i, _):
        at = pl.ds(pl.multiple_of(i * 128, 128), 128)
        v = tok[at, :].astype(F32)
        r = lax.rsqrt(jnp.mean(v * v, axis=1, keepdims=True) + EPSILON)
        normed[at, :] = (v * r * gain1[...]).astype(BF16)
        return 0
    lax.fori_loop(0, rows // 128, norm_one, 0)
    run(1)
    build_bias(table_t[...], skew)
    run(2)
    for s in range(seqs):
        build_mask(seg[s : s + 1, :], mask.at[s])
    for t in range(3, levels + 3): run(t)
    if comm:
        packed = piece.shape[2]
        part = packed * 3 // 4
        blocks = hidden // packed
        def unpack(i, _):
            at = pl.ds(pl.multiple_of(i * 64, 64), 64)
            t = w[0, at, :]
            proj[at, :] = jnp.concatenate([t[:, d * packed : d * packed + part] for d in range(blocks)] + [t[:, d * packed + part : (d + 1) * packed] for d in range(blocks)], axis=1)
            return 0
        lax.fori_loop(0, width // 64, unpack, 0)
    proj_copy = pltpu.make_async_copy(proj, proj_o, store.at[0])
    proj_copy.start()
    def project(i, _):
        r = pl.ds(pl.multiple_of((i // 3) * 256, 256), 256)
        c = pl.ds(pl.multiple_of((i % 3) * inner, 128), inner)
        mixed[r, c] = mm(normed[r, :], proj[:, c]).astype(BF16)
        return 0
    lax.fori_loop(0, rows // 256 * 3, project, 0)
    mixed_copy = pltpu.make_async_copy(mixed, mixed_o, store.at[1])
    mixed_copy.start()
    low_lanes = lax.broadcasted_iota(jnp.int32, (256, 128), 1) < HD
    def attend(i, _):
        s, p = i // pairs, i % pairs
        slot = i % 2
        for t, at in schedule:
            @pl.when(i == at)
            def _():
                run(t)
        ecopy = pltpu.make_async_copy(e.at[slot], e_o.at[i], estore.at[slot])
        @pl.when(i >= 2)
        def _():
            ecopy.wait()
        row = pl.ds(pl.multiple_of(s * SEQ, SEQ), SEQ)
        off = pl.multiple_of(p * 128, 128)
        k = mixed[row, pl.ds(inner + off, 128)]
        v_t = transpose(mixed[row, pl.ds(2 * inner + off, 128)])
        for j in range(SEQ // 256):
            qrow = pl.ds(pl.multiple_of(s * SEQ + j * 256, 256), 256)
            q = mixed[qrow, pl.ds(off, 128)] * jnp.asarray(SCALING, BF16)
            tops = []
            for a in range(2):
                qa = jnp.where(low_lanes == (a == 0), q, jnp.zeros_like(q))
                h = 2 * p + a
                parts = []
                for b in range(SEQ // EDGE):
                    sc = mm(k[b * EDGE : (b + 1) * EDGE], qa, NT)
                    lo = SEQ - EDGE - b * EDGE + j * 256
                    parts.append(sc + (skew[h, :, lo : lo + 256] + mask[s, b * EDGE : (b + 1) * EDGE, j * 256 : (j + 1) * 256]))
                score = jnp.concatenate(parts, axis=0)
                top = jnp.max(score, axis=0, keepdims=True)
                ex = jnp.exp(score - top)
                rl = 1.0 / jnp.sum(ex, axis=0, keepdims=True)
                low = ex.astype(BF16)
                e[slot, a, :, j * 256 : (j + 1) * 256] = low
                rl_o[s * heads + h, :, j * 256 : (j + 1) * 256] = jnp.broadcast_to(rl, (8, 256))
                tops.append((mm(v_t[a * HD : (a + 1) * HD], low) * rl).astype(BF16))
            both = jnp.concatenate(tops, axis=0)
            ctxt[pl.ds(off, 128), qrow] = both
            ctx[qrow, pl.ds(off, 128)] = transpose(both)
        ecopy.start()
        return 0
    n = seqs * pairs
    lax.fori_loop(0, n, attend, 0)
    done = 1 + max([t for t, _ in schedule], default=levels + 2)
    ctx_copies = [pltpu.make_async_copy(ctx, ctx_o, store.at[2]), pltpu.make_async_copy(ctxt, ctxt_o, store.at[3])]
    for c in ctx_copies: c.start()
    def close(i, _):
        r = pl.ds(pl.multiple_of(i * 256, 256), 256)
        res = tok[r, :].astype(F32) + mm(ctx[r, :], proj[:, 3 * inner :], NT)
        res_o[r, :] = res
        scale = lax.rsqrt(jnp.mean(res * res, axis=1, keepdims=True) + EPSILON)
        second[r, :] = (res * scale * gain2[...]).astype(BF16)
        return 0
    lax.fori_loop(0, rows // 256, close, 0)
    for t in range(done, 2 * levels + 3): run(t)
    in_copy = pltpu.make_async_copy(w.at[1], in_o, store.at[4])
    in_copy.start()
    chunk = 512
    per = hidden // chunk
    def widen(i, _):
        slot = i % 2
        r = pl.ds(pl.multiple_of((i // per) * 256, 256), 256)
        c = pl.ds(pl.multiple_of((i % per) * chunk, chunk), chunk)
        gcopy = pltpu.make_async_copy(gp.at[slot], gp_o.at[r, c], gstore.at[slot])
        if comm:
            for t in range(max(done, 2 * levels + 3), len(steps)):
                @pl.when(i == 5 * (t - 2 * levels - 3 + 1))
                def _():
                    run(t)
        @pl.when(i >= 2)
        def _():
            gcopy.wait()
        a, grad = gelu_both(mm(second[r, :], w[1, :, c]))
        act[r, c] = a.astype(BF16)
        gp[slot] = grad.astype(BF16)
        gcopy.start()
        return 0
    lax.fori_loop(0, rows // 256 * per, widen, 0)
    act_copy = pltpu.make_async_copy(act, act_o, store.at[5])
    act_copy.start()
    back_copy = pltpu.make_async_copy(w.at[2], back_o, store.at[6])
    back_copy.start()
    def narrow(i, _):
        r = pl.ds(pl.multiple_of(i * 256, 256), 256)
        out[r, :] = (res_o[r, :] + mm(act[r, :], w[2], NT)).astype(out.dtype)
        return 0
    lax.fori_loop(0, rows // 256, narrow, 0)
    for c in [proj_copy, mixed_copy, *ctx_copies, in_copy, act_copy, back_copy]: c.wait()
    for slot in range(2):
        pltpu.make_async_copy(e.at[slot], e_o.at[0], estore.at[slot]).wait()
        pltpu.make_async_copy(gp.at[slot], gp_o.at[pl.ds(0, 256), pl.ds(0, chunk)], gstore.at[slot]).wait()
    if comm:
        for u in range(3): g.sendwait(u)

def forward(levels, tok, seg, gain1, table, gain2, piece=None, weights=None, schedule=()):
    comm = piece is not None
    rows, width = tok.shape
    heads = table.shape[1]
    inner = heads * HD
    hidden = (piece.shape[2] * 8) if comm else weights[2].shape[1]
    seqs, pairs = rows // SEQ, heads // 2
    sds = jax.ShapeDtypeStruct
    vm, hb = pl.BlockSpec(memory_space=pltpu.VMEM), pl.BlockSpec(memory_space=pl.ANY)
    outs = [(sds((rows, width), BF16), vm), (sds((width, 4 * inner), BF16), hb), (sds((width, hidden), BF16), hb), (sds((width, hidden), BF16), hb),
            (sds((rows, 3 * inner), BF16), hb), (sds((seqs * pairs, 2, SEQ, SEQ), BF16), hb), (sds((seqs * heads, 8, SEQ), F32), vm), (sds((rows, inner), BF16), hb), (sds((inner, rows), BF16), hb),
            (sds((rows, width), F32), vm), (sds((rows, hidden), BF16), hb), (sds((rows, hidden), BF16), hb)]
    scratch = [pltpu.VMEM((3, width, hidden), BF16), pltpu.VMEM((width, 4 * inner), BF16), pltpu.VMEM((rows, width), BF16), pltpu.VMEM((rows, 3 * inner), BF16),
               pltpu.VMEM((heads, EDGE, 2 * SEQ - EDGE), F32), pltpu.VMEM((seqs, SEQ, SEQ), F32), pltpu.VMEM((2, 2, SEQ, SEQ), BF16),
               pltpu.VMEM((rows, inner), BF16), pltpu.VMEM((inner, rows), BF16), pltpu.VMEM((rows, hidden), BF16), pltpu.VMEM((2, 256, 512), BF16), pltpu.VMEM((rows, width), BF16),
               pltpu.SemaphoreType.DMA((4,)), pltpu.SemaphoreType.DMA((7,)), pltpu.SemaphoreType.DMA((2,)), pltpu.SemaphoreType.DMA((2,))]
    if comm: scratch += gather_sems(3, levels)
    args = [tok, seg, gain1.astype(F32).reshape(1, width), jnp.pad(table.T, ((0, -heads % 16), (0, 0))), gain2.astype(F32).reshape(1, width)]
    specs = [vm] * 5
    if comm:
        args += [piece]; specs += [vm]
    else:
        args += list(weights); specs += [hb] * 4
    params = dict(collective_id=0, has_side_effects=True) if comm else {}
    return pl.pallas_call(functools.partial(forward_kernel, levels, comm, schedule), out_shape=[o[0] for o in outs], in_specs=specs, out_specs=[o[1] for o in outs],
        scratch_shapes=scratch, compiler_params=pltpu.CompilerParams(vmem_limit_bytes=63 << 20, **params), name="forward")(*args)

def transpose_into(src, dst):
    n, w = src.shape
    def one(i, _):
        r = pl.ds(pl.multiple_of(i * 128, 128), 128)
        for c in range(w // 128):
            dst[c * 128 : (c + 1) * 128, r] = src[r, c * 128 : (c + 1) * 128].T
        return 0
    lax.fori_loop(0, n // 128, one, 0)

def norm_back(v, dy, gain):
    r = lax.rsqrt(jnp.mean(v * v, axis=1, keepdims=True) + EPSILON)
    unit = v * r
    a = dy * gain
    part = r * (a - unit * jnp.mean(a * unit, axis=1, keepdims=True))
    return part, jnp.sum(dy * unit, axis=0, keepdims=True), unit

def backward_kernel(levels, comm, plan, gain1, gain2, rl, tok_h, cot_h, proj_h, in_h, back_h, mixed_h, e_h, ctx_h, ctxt_h, res_h, act_h, gp_h, *rest):
    if comm:
        (tg_o, small_o, qkv_o, out_o, gin_o, gback_o), rest = rest[:6], rest[6:]
    else:
        (tg_o, small_o, proj_o, gin_o, gback_o), rest = rest[:5], rest[5:]
    (u1, u2, b, t, f, e, qkv, racc, far, own, staged, load, stream, eload, qload, store), rest = rest[:16], rest[16:]
    rows, width = f.shape[1], f.shape[2]
    hidden = u1.shape[1]
    inner = width
    heads = racc.shape[0]
    pairs, seqs = heads // 2, rows // SEQ
    small, rest = rest[:5], rest[5:]
    def local(src, dst, sem):
        return pltpu.make_async_copy(src, dst, sem)
    loads = {"cot": local(cot_h, f.at[2], load.at[0]), "back": local(back_h, u1, load.at[1]), "res": local(res_h, f.at[0], load.at[2]), "in": local(in_h, u2, load.at[3])}
    chunk = hidden // 4
    if comm:
        cross, free = rest[:9], rest[9]
        me = Place()
        order = (me.gd, me.xd, me.yd, me.d)
        cols = [pl.ds(pl.multiple_of((o // 2) * chunk, chunk), chunk) for o in order]
    else:
        cols = [pl.ds(q * chunk, chunk) for q in range(4)]
    def act_load(q):
        return local(act_h.at[:, cols[q]], b.at[1 + q % 2], stream.at[0, q % 2])
    def gp_load(q):
        return local(gp_h.at[:, cols[q]], b.at[3 + q % 2], stream.at[1, q % 2])
    loads["cot"].start()
    act_load(0).start()
    loads["res"].start()
    loads["back"].start()
    gp_load(0).start()
    act_load(1).start()
    loads["in"].start()
    gp_load(1).start()
    if comm:
        greet_all(me, levels)
        sc = Scatter(me, levels, width // levels, own.shape[3], own, staged, u2, *cross)
        sm = Small(me, levels, *small)
        mine = sm.mine.at[0]
    else:
        mine = small[0].at[0]
    mine[...] = jnp.zeros(mine.shape, F32)
    racc[...] = jnp.zeros(racc.shape, F32)
    far[...] = jnp.zeros(far.shape, F32)
    loads["cot"].wait()
    def lower(i, _):
        r = pl.ds(pl.multiple_of(i * 128, 128), 128)
        b[0, r, :] = f[2, r, :].astype(BF16)
        return 0
    lax.fori_loop(0, rows // 128, lower, 0)
    transpose_into(b.at[0], t.at[0])
    loads["res"].wait()
    def renorm(i, _):
        r = pl.ds(pl.multiple_of(i * 128, 128), 128)
        v = f[0, r, :]
        s = lax.rsqrt(jnp.mean(v * v, axis=1, keepdims=True) + EPSILON)
        b[5, r, :] = (v * s * gain2[...]).astype(BF16)
        return 0
    lax.fori_loop(0, rows // 128, renorm, 0)
    transpose_into(b.at[5], t.at[1])
    half = chunk // 2
    def weight_grad(u, q, left, right):
        def one(i, _):
            r = pl.ds(pl.multiple_of(i * 256, 256), 256)
            g = mm(left[r, :], right[...]).astype(BF16)
            if comm:
                mine_first = me.c == 0
                own[u, q, r, :] = jnp.where(mine_first, g[:, :half], g[:, half:])
                staged[u, q % 2, r, :] = jnp.where(mine_first, g[:, half:], g[:, :half])
            else:
                own[u, q, r, :] = g[:, :half]
                staged[u, q % 2, r, :] = g[:, half:]
            return 0
        if q >= 2:
            if comm:
                sc.ccopy(u, q - 2).wait_send()
            else:
                put(u, q - 2)[1].wait()
        lax.fori_loop(0, width // 256, one, 0)
        if comm:
            sc.core_start(u, q)
        else:
            for c in put(u, q): c.start()
    def put(u, q):
        dst = (gback_o, gin_o)[u]
        return (local(own.at[u, q], dst.at[:, pl.ds(q * chunk, half)], store.at[u, 0, q]), local(staged.at[u, q % 2], dst.at[:, pl.ds(q * chunk + half, half)], store.at[u, 1, q]))
    def event(name, *a):
        if comm: getattr(sc, name)(*a)
    for q in range(4):
        act, gp = b.at[1 + q % 2], b.at[3 + q % 2]
        act_load(q).wait()
        weight_grad(0, q, t.at[0], act)
        if q + 2 < 4: act_load(q + 2).start()
        if q == 0: loads["back"].wait()
        gp_load(q).wait()
        def widen(i, _):
            r = pl.ds(pl.multiple_of(i * 256, 256), 256)
            b[5, r, :] = (mm(b[0, r, :], u1[:, cols[q]]) * gp[r, :].astype(F32)).astype(BF16)
            return 0
        lax.fori_loop(0, rows // 256, widen, 0)
        if q + 2 < 4: gp_load(q + 2).start()
        if q == 3:
            proj_load = local(proj_h, u1, load.at[4])
            proj_load.start()
        event("core_add", 0, q)
        weight_grad(1, q, t.at[1], b.at[5])
        if q == 0: loads["in"].wait()
        def narrow(i, _):
            r = pl.ds(pl.multiple_of(i * 256, 256), 256)
            g = mm(b[5, r, :], u2[:, cols[q]], NT)
            f[1, r, :] = g if q == 0 else f[1, r, :] + g
            return 0
        lax.fori_loop(0, rows // 256, narrow, 0)
        event("core_add", 1, q)
        if q == 2: event("cross_one", 0)
        if q == 3: event("cross_one", 1)
    ctx_loads = [local(ctx_h, b.at[5], load.at[5]), local(ctxt_h, t.at[2], load.at[6])]
    for c in ctx_loads: c.start()
    def norm_two(i, total):
        r = pl.ds(pl.multiple_of(i * 128, 128), 128)
        part, g, _ = norm_back(f[0, r, :], f[1, r, :], gain2[...])
        grad = f[2, r, :] + part
        f[0, r, :] = grad
        b[0, r, :] = grad.astype(BF16)
        return total + g
    mine[1:2, :] = lax.fori_loop(0, rows // 128, norm_two, jnp.zeros((1, width), F32))
    transpose_into(b.at[0], t.at[0])
    proj_load.wait()
    def context_back(i, _):
        r = pl.ds(pl.multiple_of(i * 256, 256), 256)
        b[4, r, :] = mm(b[0, r, :], u1[:, 3 * inner :]).astype(BF16)
        return 0
    lax.fori_loop(0, rows // 256, context_back, 0)
    for c in ctx_loads: c.wait()
    def out_grad(i, _):
        r = pl.ds(pl.multiple_of(i * 256, 256), 256)
        b[6, r, :] = mm(t[0, r, :], b[5]).astype(BF16)
        return 0
    lax.fori_loop(0, width // 256, out_grad, 0)
    tok_load = local(tok_h, b.at[0], load.at[7])
    tok_load.start()
    tok_load.wait()
    def renorm_one(i, _):
        r = pl.ds(pl.multiple_of(i * 128, 128), 128)
        v = b[0, r, :].astype(F32)
        s = lax.rsqrt(jnp.mean(v * v, axis=1, keepdims=True) + EPSILON)
        b[5, r, :] = (v * s * gain1[...]).astype(BF16)
        return 0
    lax.fori_loop(0, rows // 128, renorm_one, 0)
    transpose_into(b.at[5], t.at[1])
    n = seqs * pairs
    def fetch(i, slot):
        s, p = i // pairs, i % pairs
        row = pl.ds(pl.multiple_of(s * SEQ, SEQ), SEQ)
        return [local(e_h.at[i], e.at[slot], eload.at[slot])] + [
            local(mixed_h.at[row, pl.ds(pl.multiple_of(k * inner + p * 128, 128), 128)], qkv.at[slot, k], qload.at[slot, k]) for k in range(3)]
    for c in fetch(0, 0): c.start()
    low_lanes = lax.broadcasted_iota(jnp.int32, (SEQ, 128), 1) < HD
    blocks = SEQ // EDGE
    def attend_back(i, _):
        s, p = i // pairs, i % pairs
        slot = i % 2
        @pl.when(i + 1 < n)
        def _():
            for c in fetch(i + 1, (i + 1) % 2): c.start()
        for at, name, args in plan:
            @pl.when(i == at)
            def _():
                event(name, *args)
        for c in fetch(i, slot): c.wait()
        row = pl.ds(pl.multiple_of(s * SEQ, SEQ), SEQ)
        off = pl.multiple_of(p * 128, 128)
        q, k, v = qkv[slot, 0] * jnp.asarray(SCALING, BF16), qkv[slot, 1], qkv[slot, 2]
        k_t = k.T
        do_t = b[4, row, pl.ds(off, 128)].T.astype(F32)
        o_t = t[2, pl.ds(off, 128), row].astype(F32)
        scaled = []
        for a in range(2):
            part = do_t[a * HD : (a + 1) * HD] * rl[s * heads + 2 * p + a, :1, :]
            scaled.append(part.astype(BF16))
        dos_t = jnp.concatenate(scaled, axis=0)
        dos = dos_t.T
        prod = dos_t.astype(F32) * o_t
        dq, dk, dv = [], [], []
        for a in range(2):
            h = 2 * p + a
            delta = jnp.sum(prod[a * HD : (a + 1) * HD], axis=0, keepdims=True)
            va = jnp.where(low_lanes == (a == 0), v, jnp.zeros_like(v))
            low = []
            sums = [None] * 3
            fars = [None] * 2
            for kb in range(blocks):
                ek = e[slot, a, kb * EDGE : (kb + 1) * EDGE, :]
                ds = ek.astype(F32) * (mm(va[kb * EDGE : (kb + 1) * EDGE], dos_t) - delta)
                low.append(ds.astype(BF16))
                for qb in range(blocks):
                    piece = ds[:, qb * EDGE : (qb + 1) * EDGE]
                    gap = kb - qb
                    if abs(gap) <= 1:
                        sums[gap + 1] = piece if sums[gap + 1] is None else sums[gap + 1] + piece
                    else:
                        w = 1 if gap > 0 else 0
                        piece = jnp.sum(piece.reshape(EDGE // 8, 8, EDGE), axis=0)
                        fars[w] = piece if fars[w] is None else fars[w] + piece
            for w in range(3):
                racc[h, w] += sums[w]
            for w in range(2):
                far[h, w] += fars[w]
            low = jnp.concatenate(low, axis=0)
            dv.append(mm(e[slot, a], dos))
            dk.append(mm(low, q))
            dq.append(mm(k_t[a * HD : (a + 1) * HD], low))
        b[1, row, pl.ds(off, 128)] = (jnp.concatenate(dq, axis=0) * SCALING).astype(BF16).T
        b[2, row, pl.ds(off, 128)] = jnp.where(low_lanes, dk[0], dk[1]).astype(BF16)
        b[3, row, pl.ds(off, 128)] = jnp.where(low_lanes, dv[0], dv[1]).astype(BF16)
        return 0
    lax.fori_loop(0, n, attend_back, 0)
    if comm:
        for u in range(2):
            (gback_o, gin_o)[u][...] = sc.finish(u)
        for u in range(2): sc.sendwait(u)
        sc.release(free)
    part, packed = own.shape[3] * 3 // 4, own.shape[3]
    def proj_grad(i, _):
        r = pl.ds(pl.multiple_of(i * 256, 256), 256)
        left = t[1, r, :]
        g = jnp.concatenate([mm(left, b[1 + k]).astype(BF16) for k in range(3)], axis=1)
        o = b[6, r, :]
        if comm:
            quarter = packed - part
            for d in range(hidden // packed):
                u2[r, d * packed : (d + 1) * packed] = jnp.concatenate([g[:, d * part : (d + 1) * part], o[:, d * quarter : (d + 1) * quarter]], axis=1)
        else:
            u2[r, : 3 * inner] = g
            u2[r, 3 * inner :] = o
        return 0
    lax.fori_loop(0, width // 256, proj_grad, 0)
    if comm:
        sc.acquire(free)
        for q in range(4): sc.core_start(2, q)
    else:
        proj_put = local(u2, proj_o, store.at[0, 0, 4])
        proj_put.start()
    span = 2 * EDGE
    c = lax.broadcasted_iota(jnp.int32, (span, 128), 0)
    offs = EDGE - 1 - c
    bucket_lane = lax.broadcasted_iota(jnp.int32, (span, 128), 1)
    hots = [(bucket_of(offs + EDGE * w) == bucket_lane).astype(F32) for w in (-1, 0, 1)]
    lane = lax.broadcasted_iota(jnp.int32, (1, 128), 1)
    mirror = (lax.broadcasted_iota(jnp.int32, (EDGE, EDGE), 0) + lax.broadcasted_iota(jnp.int32, (EDGE, EDGE), 1) == EDGE - 1).astype(F32)
    at_row = lax.broadcasted_iota(jnp.int32, (16, 128), 0)
    def table_one(h, held):
        total = jnp.zeros((8, 128), F32)
        for w in range(3):
            upended = lax.dot_general(mirror, racc[h, w], NN, precision=lax.Precision.HIGHEST, preferred_element_type=F32)
            wide = jnp.concatenate([upended, jnp.zeros((EDGE, EDGE), F32)], axis=1)
            turned = pltpu.roll(wide, 0, 1, stride=1, stride_axis=0)
            diag = jnp.sum(turned.reshape(EDGE // 8, 8, span), axis=0)
            total = total + lax.dot_general(diag, hots[w], NN, precision=lax.Precision.HIGHEST, preferred_element_type=F32)
        row = jnp.sum(total, axis=0, keepdims=True)
        left = jnp.sum(far[h, 0])
        right = jnp.sum(far[h, 1])
        row = row + jnp.where(lane == BUCKETS // 2 - 1, left, 0.0) + jnp.where(lane == BUCKETS - 1, right, 0.0)
        return held + jnp.where(at_row == 2 + h, row, 0.0)
    mine[:, :128] += lax.fori_loop(0, heads, table_one, jnp.zeros((16, 128), F32))
    if comm:
        for q in range(4): sc.core_add(2, q)
    def norm_one(i, total):
        r = pl.ds(pl.multiple_of(i * 256, 256), 256)
        dy = mm(b[1, r, :], u1[:, :inner], NT) + mm(b[2, r, :], u1[:, inner : 2 * inner], NT) + mm(b[3, r, :], u1[:, 2 * inner : 3 * inner], NT)
        part, g, _ = norm_back(b[0, r, :].astype(F32), dy, gain1[...])
        f[1, r, :] = f[0, r, :] + part
        return total + g
    mine[0:1, :] = lax.fori_loop(0, rows // 256, norm_one, jnp.zeros((1, width), F32))
    tg_copy = local(f.at[1], tg_o, load.at[8])
    tg_copy.start()
    if comm:
        sm.start(0)
        sc.cross_one(2)
        sm.add(0); sm.start(1)
        sc.cross_two(2)
        sm.add(1); sm.start(2)
        sc.cross_three(2)
        sc.line_open(2)
        sm.add(2); sm.spread()
        for k in range(1, levels): sc.line_step(2, k)
        total = sc.finish(2)
        qkv_o[...] = total[:, :part]
        out_o[...] = total[:, part:]
        small_o[...] = sm.total()
        sc.sendwait(2)
        sm.sendwait()
    else:
        small_o[...] = mine[...]
        for u in range(2):
            for q in range(4):
                x, y = put(u, q)
                x.wait()
                if q >= 2: y.wait()
        proj_put.wait()
    tg_copy.wait()

def backward(levels, comm, plan, gain1, gain2, rl, tok, cot, proj, w_in, w_back, mixed, e, ctx, ctxt, res, act, gp, share=None):
    rows, width = tok.shape
    hidden = w_in.shape[1]
    heads = rl.shape[0] // (rows // SEQ)
    sds = jax.ShapeDtypeStruct
    vm, hb = pl.BlockSpec(memory_space=pltpu.VMEM), pl.BlockSpec(memory_space=pl.ANY)
    shape = (16, width)
    half = hidden // 8
    piece_rows = width // levels
    outs = [(sds((rows, width), F32), hb), (sds(shape, F32), vm)]
    if comm:
        outs += [(sds((piece_rows, half * 3 // 4), F32), vm), (sds((piece_rows, half // 4), F32), vm), (sds((piece_rows, half), F32), vm), (sds((piece_rows, half), F32), vm)]
    else:
        outs += [(sds((width, hidden), BF16), hb)] * 3
    D = pltpu.SemaphoreType.DMA
    scratch = [pltpu.VMEM((width, hidden), BF16), pltpu.VMEM((width, hidden), BF16), pltpu.VMEM((7, rows, width), BF16), pltpu.VMEM((3, width, rows), BF16), pltpu.VMEM((3, rows, width), F32),
               pltpu.VMEM((2, 2, SEQ, SEQ), BF16), pltpu.VMEM((2, 3, SEQ, 128), BF16), pltpu.VMEM((heads, 3, EDGE, EDGE), F32), pltpu.VMEM((heads, 2, 8, EDGE), F32),
               pltpu.VMEM((2, 4, width, half), BF16), pltpu.VMEM((2, 2, width, half), BF16), D((9,)), D((2, 2)), D((2,)), D((2, 3)), D((2, 2, 5))] + small_scratch(levels, shape)
    if comm:
        scratch += [pltpu.VMEM((2, 4, width, half), BF16), pltpu.VMEM((2, 2, 3, width // 2, half), BF16), pltpu.VMEM((2, 2, levels - 1, piece_rows, half), BF16),
                    D((3, 4)), D((3, 4)), D((3, 2, 3)), D((3, 2, 3)), D((3, 2, levels - 1)), D((3, 2, levels - 1)), pltpu.SemaphoreType.REGULAR]
    params = dict(collective_id=1, has_side_effects=True) if comm else {}
    g = lambda x: x.astype(F32).reshape(1, width)
    return pl.pallas_call(functools.partial(backward_kernel, levels, comm, plan), out_shape=[o[0] for o in outs], in_specs=[vm] * 3 + [hb] * 12, out_specs=[o[1] for o in outs],
        scratch_shapes=scratch, compiler_params=pltpu.CompilerParams(vmem_limit_bytes=63 << 20, **params), name="backward")(g(gain1), g(gain2), rl, tok, cot, proj, w_in, w_back, mixed, e, ctx, ctxt, res, act, gp)

def scatter_plain(grad):
    part = lax.psum_scatter(grad, "dp", scatter_dimension=1, tiled=True)
    return lax.psum_scatter(part, "mp", scatter_dimension=0, tiled=True).astype(F32)


FORWARD_PLAN = ((7, 1), (8, 4), (9, 7), (10, 10))
BACKWARD_PLAN = (
    (0, "cross_two", (0,)), (1, "cross_two", (1,)), (3, "cross_three", (0,)), (3, "line_open", (0,)), (4, "line_step", (0, 1)),
    (5, "cross_three", (1,)), (5, "line_open", (1,)), (6, "line_step", (0, 2)), (7, "line_step", (1, 1)), (8, "line_step", (0, 3)),
    (9, "line_step", (1, 2)), (11, "line_step", (1, 3)),
)


def body(tokens, segment_ids, cotangent, gain_one, w_qkv, w_out, rel_table, gain_two, w_in, w_back):
    axes = ("mp", "dp")
    levels, width = lax.axis_size("mp"), lax.axis_size("dp")
    heads = rel_table.shape[1]
    inner = heads * HD
    segments = segment_ids.reshape(-1, SEQ).astype(F32)
    packed = w_qkv.shape[1] + w_out.shape[1]
    own = width == 8 and levels == 4 and packed == w_in.shape[1] and packed % 128 == 0
    if own:
        piece = jnp.stack([jnp.concatenate([w_qkv, w_out], axis=1), w_in, w_back])
        held = forward(levels, tokens, segments, gain_one, rel_table, gain_two, piece=piece, schedule=FORWARD_PLAN)
    else:
        whole = [lax.all_gather(lax.all_gather(m, "mp", axis=0, tiled=True), "dp", axis=1, tiled=True) for m in (w_qkv, w_out, w_in, w_back)]
        held = forward(levels, tokens, segments, gain_one, rel_table, gain_two, weights=whole)
    layer_out, proj, full_in, full_back, mixed, e, rl, ctx, ctxt, res, act, gp = held
    grads = backward(levels, own, BACKWARD_PLAN, gain_one, gain_two, rl, tokens, cotangent, proj, full_in, full_back, mixed, e, ctx, ctxt, res, act, gp)
    if own:
        tokens_grad, small, qkv_grad, out_grad, in_grad, back_grad = grads
    else:
        tokens_grad, small, proj_grad, in_grad, back_grad = grads
        small = lax.psum(small, axes)
        qkv_grad, out_grad = scatter_plain(proj_grad[:, : 3 * inner]), scatter_plain(proj_grad[:, 3 * inner :])
        in_grad, back_grad = scatter_plain(in_grad), scatter_plain(back_grad)
    table_grad = small[2 : 2 + heads, :BUCKETS].T
    return layer_out, tokens_grad, small[0], qkv_grad, out_grad, table_grad, small[1], in_grad, back_grad


def solution(mesh):
    both = ("mp", "dp")
    weight = P("mp", "dp")
    return jax.shard_map(
        body,
        mesh=mesh,
        in_specs=(P(both, None), P(both), P(both, None), P(), weight, weight, P(), P(), weight, weight),
        out_specs=(P(both, None), P(both, None), P(), weight, weight, P(), P(), weight, weight),
        check_vma=False,
    )
```

```python
import functools

import jax
import jax.numpy as jnp
from jax import lax
from jax.experimental import pallas as pl
from jax.experimental.pallas import tpu as pltpu
from jax.sharding import PartitionSpec as P

MESH = pl.DeviceIdType.MESH

class Place:
    def __init__(self):
        self.z = lax.axis_index("mp"); self.d = lax.axis_index("dp")
        d = self.d
        self.c = lax.rem(d, 2); self.x = lax.rem(d // 2, 2); self.y = d // 4
        self.xd = d + 2 - 4 * self.x
        self.yd = d + 4 - 8 * self.y
        self.cd = d + 1 - 2 * self.c
        self.gd = self.xd + 4 - 8 * self.y
    def barrier(self, levels):
        bar = pltpu.get_barrier_semaphore()
        for t in (self.xd, self.yd, self.cd):
            pl.semaphore_signal(bar, inc=1, device_id=(self.z, t), device_id_type=MESH)
        @pl.when(self.z > 0)
        def _():
            pl.semaphore_signal(bar, inc=1, device_id=(self.z - 1, self.d), device_id_type=MESH)
        @pl.when(self.z < levels - 1)
        def _():
            pl.semaphore_signal(bar, inc=1, device_id=(self.z + 1, self.d), device_id_type=MESH)
        peers = 3 + jnp.minimum(self.z, 1) + jnp.minimum(levels - 1 - self.z, 1)
        pl.semaphore_wait(bar, peers)

class Gather:
    def __init__(self, me, levels, piece, full, zs, zr, xs, xr, cs, cr):
        self.me, self.levels, self.piece, self.full = me, levels, piece, full
        self.zs, self.zr, self.xs, self.xr, self.cs, self.cr = zs, zr, xs, xr, cs, cr
        self.rows, self.cols = piece.shape[1], piece.shape[2]
    def blk(self, u, z, d, r0=0, nr=None):
        nr = self.rows if nr is None else nr
        return self.full.at[u, pl.ds(pl.multiple_of(z * self.rows + r0, 16), nr), pl.ds(pl.multiple_of(d * self.cols, 128), self.cols)]
    def col(self, u, d):
        return self.full.at[u, :, pl.ds(pl.multiple_of(d * self.cols, 128), self.cols)]
    def cp(self, src, dst, ss, rs, dev):
        return pltpu.make_async_remote_copy(src_ref=src, dst_ref=dst, send_sem=ss, recv_sem=rs, device_id=dev, device_id_type=MESH)
    def zcopy(self, u, up, k, z, src=None):
        b = self.blk(u, z, self.me.d)
        t = self.me.z + (1 if up else -1)
        return self.cp(b if src is None else src, b, self.zs.at[u, 0 if up else 1, k], self.zr.at[u, 0 if up else 1, k], (t, self.me.d))
    def xcopy(self, u, z, d, src=None):
        b = self.blk(u, z, d)
        return self.cp(b if src is None else src, b, self.xs.at[u, 0, z], self.xr.at[u, 0, z], (self.me.z, self.me.xd))
    def ycopy(self, u, z, d, src=None):
        b = self.blk(u, z, d)
        return self.cp(b if src is None else src, b, self.xs.at[u, 1, z], self.xr.at[u, 1, z], (self.me.z, self.me.yd))
    def half(self, u, z, d, way):
        h = self.rows // 2
        b = self.blk(u, z, d, way * h, h)
        return self.cp(b, b, self.xs.at[u, 2 + way, z], self.xr.at[u, 2 + way, z], (self.me.z, self.me.yd if way == 0 else self.me.xd))
    def ccopy(self, u, which, d):
        b = self.col(u, d)
        return self.cp(b, b, self.cs.at[u, which], self.cr.at[u, which], (self.me.z, self.me.cd))
    def zstep(self, u, k):
        me = self.me
        if k == 0:
            src = self.piece.at[u]
            self.xcopy(u, me.z, me.d, src).start()
            self.ycopy(u, me.z, me.d, src).start()
            @pl.when(me.z < self.levels - 1)
            def _():
                self.zcopy(u, True, 0, me.z, src).start()
            @pl.when(me.z > 0)
            def _():
                self.zcopy(u, False, 0, me.z, src).start()
            self.blk(u, me.z, me.d)[...] = self.piece[u]
            return
        @pl.when(me.z - k >= 0)
        def _():
            z = me.z - k
            self.zcopy(u, True, k - 1, z).wait_recv()
            if k < self.levels - 1:
                @pl.when(me.z < self.levels - 1)
                def _():
                    self.zcopy(u, True, k, z).start()
            self.xcopy(u, z, me.d).start()
            self.ycopy(u, z, me.d).start()
        @pl.when(me.z + k < self.levels)
        def _():
            z = me.z + k
            self.zcopy(u, False, k - 1, z).wait_recv()
            if k < self.levels - 1:
                @pl.when(me.z > 0)
                def _():
                    self.zcopy(u, False, k, z).start()
            self.xcopy(u, z, me.d).start()
            self.ycopy(u, z, me.d).start()
    def xystep(self, u, k):
        me = self.me
        def one(z):
            self.xcopy(u, z, me.xd).wait_recv()
            self.half(u, z, me.xd, 0).start()
            self.ycopy(u, z, me.yd).wait_recv()
            self.half(u, z, me.yd, 1).start()
        if k == 0:
            one(me.z)
            return
        @pl.when(me.z - k >= 0)
        def _():
            one(me.z - k)
        @pl.when(me.z + k < self.levels)
        def _():
            one(me.z + k)
    def corestep(self, u, which):
        me = self.me
        self.ccopy(u, which, (me.d, me.xd, me.yd, me.gd)[which]).start()
    def diagstep(self, u):
        me = self.me
        for z in range(self.levels):
            self.half(u, z, me.gd, 0).wait_recv()
            self.half(u, z, me.gd, 1).wait_recv()
    def corewait(self, u):
        me = self.me
        for which in range(4):
            self.ccopy(u, which, (me.cd, me.cd + me.xd - me.d, me.cd + me.yd - me.d, me.cd + me.gd - me.d)[which]).wait_recv()
    def sendwait(self, u):
        me = self.me
        for k in range(self.levels - 1):
            @pl.when((me.z < self.levels - 1) & (me.z - k >= 0))
            def _():
                self.zcopy(u, True, k, me.z - k).wait_send()
            @pl.when((me.z > 0) & (me.z + k < self.levels))
            def _():
                self.zcopy(u, False, k, me.z + k).wait_send()
        for z in range(self.levels):
            self.xcopy(u, z, me.d).wait_send()
            self.ycopy(u, z, me.d).wait_send()
            self.half(u, z, me.xd, 0).wait_send()
            self.half(u, z, me.yd, 1).wait_send()
        for which in range(4):
            self.ccopy(u, which, me.d).wait_send()
    def events(self, units):
        L = self.levels
        def at(t):
            u, k = divmod(t, L + 1)
            return (u, k) if 0 <= t and u < units and k < L else (None, None)
        out = []
        for s in range(units * (L + 1) + 2):
            step = []
            u, k = at(s)
            if u is not None:
                step.append(functools.partial(self.zstep, u, k))
                if k == L - 1:
                    step.append(functools.partial(self.corestep, u, 0))
            u, k = at(s - 1)
            if u is not None:
                step.append(functools.partial(self.xystep, u, k))
                if k == L - 1:
                    step.append(functools.partial(self.corestep, u, 1))
                    step.append(functools.partial(self.corestep, u, 2))
            u, k = at(s - 2)
            if k == L - 1:
                step.append(functools.partial(self.diagstep, u))
                step.append(functools.partial(self.corestep, u, 3))
            u, k = at(s - 3)
            if k == L - 1:
                step.append(functools.partial(self.corewait, u))
            out.append(step)
        return out

def gather_sems(units, levels):
    return [pltpu.SemaphoreType.DMA((units, 2, levels - 1))] * 2 + [pltpu.SemaphoreType.DMA((units, 4, levels))] * 2 + [pltpu.SemaphoreType.DMA((units, 4))] * 2

def greet_all(me, levels):
    bar = pltpu.get_barrier_semaphore()
    for t in (me.xd, me.yd, me.cd):
        pl.semaphore_signal(bar, inc=1, device_id=(me.z, t), device_id_type=MESH)
    for k in range(1, levels):
        pl.semaphore_signal(bar, inc=1, device_id=(lax.rem(me.z + k, levels), me.d), device_id_type=MESH)
    pl.semaphore_wait(bar, 2 + levels)

class Scatter:
    def __init__(self, me, levels, rows, cols, own, staged, matrix, core, cross, line, cs, cr, xs, xr, zs, zr):
        self.me, self.levels, self.rows, self.cols = me, levels, rows, cols
        self.grads, self.staged, self.matrix = own, staged, matrix
        self.core, self.cross, self.line = core, cross, line
        self.cs, self.cr, self.xs, self.xr, self.zs, self.zr = cs, cr, xs, xr, zs, zr
        self.order = (me.gd, me.xd, me.yd, me.d)
        self.half_rows = rows * levels // 2
    def cp(self, src, dst, ss, rs, dev):
        return pltpu.make_async_remote_copy(src_ref=src, dst_ref=dst, send_sem=ss, recv_sem=rs, device_id=dev, device_id_type=MESH)
    def add(self, dst, src):
        n = dst.shape[0]
        step = 96 if n % 96 == 0 else 16
        def one(i, _):
            at = pl.ds(pl.multiple_of(i * step, 16), step)
            dst[at, :] = dst[at, :] + src[at, :]
            return 0
        lax.fori_loop(0, n // step, one, 0)
    def core_start(self, u, q):
        self.ccopy(u, q).start()
    def index(self, d):
        return [i for i, o in enumerate(self.order) if o is d][0]
    def block(self, u, d, r0, nr):
        at = pl.ds(r0 if isinstance(r0, int) else pl.multiple_of(r0, 16), nr)
        if u < 2:
            return self.grads.at[u, self.index(d), at]
        return self.matrix.at[at, pl.ds(pl.multiple_of(d * self.cols, 128), self.cols)]
    def slot(self, u):
        return 0 if u == 2 else u
    def ccopy(self, u, q):
        s = self.slot(u)
        if u < 2:
            src = self.staged.at[u, q % 2]
        else:
            src = self.block(u, self.order[q] + self.me.cd - self.me.d, 0, self.rows * self.levels)
        return self.cp(src, self.core.at[s, q], self.cs.at[u, q], self.cr.at[u, q], (self.me.z, self.me.cd))
    def core_add(self, u, q):
        self.ccopy(u, q).wait_recv()
        self.add(self.block(u, self.order[q], 0, self.rows * self.levels), self.core.at[self.slot(u), q])
        if q == 0:
            self.xcopy(u, 0).start()
            self.ycopy(u, 0).start()
        if q == 1:
            self.xcopy(u, 1).start()
        if q == 2:
            self.ycopy(u, 1).start()
    def xcopy(self, u, slot):
        d = (self.me.gd, self.me.xd, self.me.xd)[slot]
        r0 = (0, 0, self.half_rows)[slot]
        return self.cp(self.block(u, d, r0, self.half_rows), self.cross.at[self.slot(u), 0, slot], self.xs.at[u, 0, slot], self.xr.at[u, 0, slot], (self.me.z, self.me.xd))
    def ycopy(self, u, slot):
        d = (self.me.gd, self.me.yd, self.me.yd)[slot]
        r0 = (self.half_rows, self.half_rows, 0)[slot]
        return self.cp(self.block(u, d, r0, self.half_rows), self.cross.at[self.slot(u), 1, slot], self.xs.at[u, 1, slot], self.xr.at[u, 1, slot], (self.me.z, self.me.yd))
    def zcopy(self, u, way, target):
        slot = target - 1 if way == 0 else target
        t = self.me.z + (1 if way == 0 else -1)
        return self.cp(self.block(u, self.me.d, target * self.rows, self.rows), self.line.at[self.slot(u), way, slot], self.zs.at[u, way, slot], self.zr.at[u, way, slot], (t, self.me.d))
    def cross_one(self, u):
        me, h, s = self.me, self.half_rows, self.slot(u)
        self.xcopy(u, 0).wait_recv()
        self.add(self.block(u, me.yd, 0, h), self.cross.at[s, 0, 0])
        self.ycopy(u, 2).start()
        self.ycopy(u, 0).wait_recv()
        self.add(self.block(u, me.xd, h, h), self.cross.at[s, 1, 0])
        self.xcopy(u, 2).start()
    def cross_two(self, u):
        me, h, s = self.me, self.half_rows, self.slot(u)
        self.xcopy(u, 1).wait_recv()
        self.add(self.block(u, me.d, 0, h), self.cross.at[s, 0, 1])
        self.ycopy(u, 1).wait_recv()
        self.add(self.block(u, me.d, h, h), self.cross.at[s, 1, 1])
    def cross_three(self, u):
        me, h, s = self.me, self.half_rows, self.slot(u)
        self.ycopy(u, 2).wait_recv()
        self.add(self.block(u, me.d, 0, h), self.cross.at[s, 1, 2])
        self.xcopy(u, 2).wait_recv()
        self.add(self.block(u, me.d, h, h), self.cross.at[s, 0, 2])
    def line_open(self, u):
        me, last = self.me, self.levels - 1
        @pl.when(me.z == 0)
        def _():
            for i in range(last):
                self.zcopy(u, 0, last - i).start()
        @pl.when(me.z == last)
        def _():
            for i in range(last):
                self.zcopy(u, 1, i).start()
    def line_step(self, u, k):
        me, last, s = self.me, self.levels - 1, self.slot(u)
        def take(way, target):
            self.zcopy(u, way, target).wait_recv()
            if k < last:
                at = target - 1 if way == 0 else target
                self.add(self.block(u, me.d, target * self.rows, self.rows), self.line.at[s, way, at])
                self.zcopy(u, way, target).start()
        @pl.when((me.z >= 1) & (me.z <= k))
        def _():
            take(0, last - k + me.z)
        @pl.when((me.z <= last - 1) & (me.z >= last - k))
        def _():
            take(1, k - last + me.z)
    def finish(self, u):
        me, last, s = self.me, self.levels - 1, self.slot(u)
        own = self.block(u, me.d, me.z * self.rows, self.rows)[...].astype(F32)
        below = self.line[s, 0, jnp.maximum(me.z - 1, 0)].astype(F32)
        above = self.line[s, 1, jnp.minimum(me.z, last - 1)].astype(F32)
        return own + jnp.where(me.z > 0, below, 0.0) + jnp.where(me.z < last, above, 0.0)
    def release(self, free):
        me, last = self.me, self.levels - 1
        for t in (me.xd, me.yd, me.cd):
            pl.semaphore_signal(free, inc=1, device_id=(me.z, t), device_id_type=MESH)
        @pl.when(me.z > 0)
        def _():
            pl.semaphore_signal(free, inc=1, device_id=(me.z - 1, me.d), device_id_type=MESH)
        @pl.when(me.z < last)
        def _():
            pl.semaphore_signal(free, inc=1, device_id=(me.z + 1, me.d), device_id_type=MESH)
    def acquire(self, free):
        me, last = self.me, self.levels - 1
        pl.semaphore_wait(free, 3 + jnp.minimum(me.z, 1) + jnp.minimum(last - me.z, 1))
    def sendwait(self, u):
        me, last = self.me, self.levels - 1
        for q in range(4):
            if u == 2 or q >= 2: self.ccopy(u, q).wait_send()
        for slot in range(3):
            self.xcopy(u, slot).wait_send()
            self.ycopy(u, slot).wait_send()
        for i in range(last):
            @pl.when(me.z < last - i)
            def _():
                self.zcopy(u, 0, last - i).wait_send()
            @pl.when(me.z > i)
            def _():
                self.zcopy(u, 1, i).wait_send()

class Small:
    def __init__(self, me, levels, mine, swap, slots, ss, rs):
        self.me, self.levels, self.mine, self.swap, self.slots, self.ss, self.rs = me, levels, mine, swap, slots, ss, rs
    def pair(self, i):
        t = (self.me.cd, self.me.xd, self.me.yd)[i]
        return pltpu.make_async_remote_copy(src_ref=self.mine.at[i], dst_ref=self.swap.at[i], send_sem=self.ss.at[i], recv_sem=self.rs.at[i], device_id=(self.me.z, t), device_id_type=MESH)
    def start(self, i):
        self.pair(i).start()
    def add(self, i):
        self.pair(i).wait_recv()
        self.mine[i + 1] = self.mine[i] + self.swap[i]
    def level(self, k):
        t = lax.rem(self.me.z + k, self.levels)
        return pltpu.make_async_remote_copy(src_ref=self.mine.at[3], dst_ref=self.slots.at[k - 1], send_sem=self.ss.at[2 + k], recv_sem=self.rs.at[2 + k], device_id=(t, self.me.d), device_id_type=MESH)
    def spread(self):
        for k in range(1, self.levels):
            self.level(k).start()
    def total(self):
        for k in range(1, self.levels):
            self.level(k).wait_recv()
        def at(level):
            k = lax.rem(self.me.z - level + self.levels, self.levels)
            held = self.slots[jnp.maximum(k - 1, 0)]
            return jnp.where(k == 0, self.mine[3], held)
        out = at(0)
        for level in range(1, self.levels):
            out = out + at(level)
        return out
    def sendwait(self):
        for i in range(3):
            self.pair(i).wait_send()
        for k in range(1, self.levels):
            self.level(k).wait_send()

def small_scratch(levels, shape):
    return [pltpu.VMEM((4, *shape), jnp.float32), pltpu.VMEM((3, *shape), jnp.float32), pltpu.VMEM((levels - 1, *shape), jnp.float32),
            *[pltpu.SemaphoreType.DMA((2 + levels,))] * 2]

SEQ, HD, BUCKETS = 512, 64, 32
EPSILON = 1e-06
NEGATIVE = -1e30
SCALING = 0.125
THRESHOLDS = (12, 16, 23, 32, 46, 64, 91)
F32, BF16 = jnp.float32, jnp.bfloat16
EDGE = 128
NT = (((1,), (1,)), ((), ()))
NN = (((1,), (0,)), ((), ()))

def mm(a, b, dims=NN):
    return lax.dot_general(a, b, dims, preferred_element_type=F32)

def bucket_of(offset):
    distance = jnp.abs(offset)
    larger = jnp.zeros_like(distance)
    for edge in THRESHOLDS:
        larger = larger + (distance >= edge).astype(jnp.int32)
    inside = jnp.where(distance < 8, distance, 8 + larger)
    return inside + BUCKETS // 2 * (offset > 0).astype(jnp.int32)

def build_bias(table_t, skew):
    heads, edge, width = skew.shape
    span = 1024
    c = lax.broadcasted_iota(jnp.int32, (BUCKETS, span), 1)
    c = jnp.where(c >= span - EDGE, c - span, c)
    hot = (bucket_of((SEQ - EDGE) - c) == lax.broadcasted_iota(jnp.int32, (BUCKETS, span), 0)).astype(BF16)
    flat = mm(table_t, hot)
    for h in range(heads):
        rows = jnp.broadcast_to(flat[h : h + 1, :], (edge, span))
        skew[h] = pltpu.roll(rows, 0, 1, stride=1, stride_axis=0)[:, :width]

def build_mask(seg, mask):
    wide = jnp.broadcast_to(seg, (EDGE, SEQ))
    for b in range(SEQ // EDGE):
        col = wide[:, b * EDGE : (b + 1) * EDGE].T
        tall = jnp.concatenate([col] * (SEQ // EDGE), axis=1)
        same = (tall == wide) & (wide > 0.0)
        k = lax.broadcasted_iota(jnp.int32, (EDGE, SEQ), 0) + b * EDGE
        q = lax.broadcasted_iota(jnp.int32, (EDGE, SEQ), 1)
        mask[b * EDGE : (b + 1) * EDGE, :] = jnp.where(same | (k == q), 0.0, NEGATIVE)

def transpose(x):
    return x.T

GELU_C = 0.7978845608028654
def gelu_both(x):
    x2 = x * x
    t = jnp.tanh(x * (GELU_C + (GELU_C * 0.044715) * x2))
    half = 0.5 * x
    one = 0.5 + 0.5 * t
    act = x * one
    grad = one + (half * (1.0 - t * t)) * (GELU_C + (3.0 * 0.044715 * GELU_C) * x2)
    return act, grad

def forward_kernel(levels, comm, schedule, tok, seg, gains, table_t, *rest):
    gain1, gain2 = gains.at[0:1], gains.at[1:2]
    weights, rest = rest[:4], rest[4:]
    if comm:
        piece, rest = rest[-1], rest[:-1]
        piece[0] = jnp.concatenate([weights[0][...], weights[1][...]], axis=1)
        piece[1] = weights[2][...]
        piece[2] = weights[3][...]
    (out, proj_o, in_o, back_o, mixed_o, e_o, rl_o, ctx_o, ctxt_o, res_o, act_o, gp_o), rest = rest[:12], rest[12:]
    (w, proj, normed, mixed, skew, mask, e, ctx, ctxt, act, gp, second, load, store, estore, gstore), sems = rest[:16], rest[16:]
    rows, width = tok.shape
    inner = width
    heads = skew.shape[0]
    pairs = heads // 2
    seqs = rows // SEQ
    hidden = act.shape[1]
    if comm:
        me = Place()
        me.barrier(levels)
        g = Gather(me, levels, piece, w, *sems)
        steps = g.events(3)
    else:
        steps = []
    def run(t):
        if t < len(steps):
            for call in steps[t]: call()
    if not comm:
        loads = [pltpu.make_async_copy(weights[0], proj.at[:, : 3 * inner], load.at[0]), pltpu.make_async_copy(weights[1], proj.at[:, 3 * inner :], load.at[1]),
                 pltpu.make_async_copy(weights[2], w.at[1], load.at[2]), pltpu.make_async_copy(weights[3], w.at[2], load.at[3])]
        for l in loads: l.start()
        for l in loads: l.wait()
    run(0)
    def norm_one(i, _):
        at = pl.ds(pl.multiple_of(i * 128, 128), 128)
        v = tok[at, :].astype(F32)
        r = lax.rsqrt(jnp.mean(v * v, axis=1, keepdims=True) + EPSILON)
        normed[at, :] = (v * r * gain1[...]).astype(BF16)
        return 0
    lax.fori_loop(0, rows // 128, norm_one, 0)
    run(1)
    build_bias(table_t[...], skew)
    run(2)
    for s in range(seqs):
        build_mask(seg[s : s + 1, :], mask.at[s])
    for t in range(3, levels + 3): run(t)
    if comm:
        packed = piece.shape[2]
        part = packed * 3 // 4
        blocks = hidden // packed
        def unpack(i, _):
            at = pl.ds(pl.multiple_of(i * 64, 64), 64)
            t = w[0, at, :]
            proj[at, :] = jnp.concatenate([t[:, d * packed : d * packed + part] for d in range(blocks)] + [t[:, d * packed + part : (d + 1) * packed] for d in range(blocks)], axis=1)
            return 0
        lax.fori_loop(0, width // 64, unpack, 0)
    proj_copy = pltpu.make_async_copy(proj, proj_o, store.at[0])
    proj_copy.start()
    def project(i, _):
        r = pl.ds(pl.multiple_of((i // 3) * 256, 256), 256)
        c = pl.ds(pl.multiple_of((i % 3) * inner, 128), inner)
        mixed[r, c] = mm(normed[r, :], proj[:, c]).astype(BF16)
        return 0
    lax.fori_loop(0, rows // 256 * 3, project, 0)
    mixed_copy = pltpu.make_async_copy(mixed, mixed_o, store.at[1])
    mixed_copy.start()
    low_lanes = lax.broadcasted_iota(jnp.int32, (256, 128), 1) < HD
    def attend(i, _):
        s, p = i // pairs, i % pairs
        slot = i % 2
        for t, at in schedule:
            @pl.when(i == at)
            def _():
                run(t)
        ecopy = pltpu.make_async_copy(e.at[slot], e_o.at[i], estore.at[slot])
        @pl.when(i >= 2)
        def _():
            ecopy.wait()
        row = pl.ds(pl.multiple_of(s * SEQ, SEQ), SEQ)
        off = pl.multiple_of(p * 128, 128)
        k = mixed[row, pl.ds(inner + off, 128)]
        v_t = transpose(mixed[row, pl.ds(2 * inner + off, 128)])
        for j in range(SEQ // 256):
            qrow = pl.ds(pl.multiple_of(s * SEQ + j * 256, 256), 256)
            q = mixed[qrow, pl.ds(off, 128)] * jnp.asarray(SCALING, BF16)
            tops = []
            for a in range(2):
                qa = jnp.where(low_lanes == (a == 0), q, jnp.zeros_like(q))
                h = 2 * p + a
                parts = []
                for b in range(SEQ // EDGE):
                    sc = mm(k[b * EDGE : (b + 1) * EDGE], qa, NT)
                    lo = SEQ - EDGE - b * EDGE + j * 256
                    parts.append(sc + (skew[h, :, lo : lo + 256] + mask[s, b * EDGE : (b + 1) * EDGE, j * 256 : (j + 1) * 256]))
                score = jnp.concatenate(parts, axis=0)
                top = jnp.max(score, axis=0, keepdims=True)
                ex = jnp.exp(score - top)
                rl = 1.0 / jnp.sum(ex, axis=0, keepdims=True)
                low = ex.astype(BF16)
                e[slot, a, :, j * 256 : (j + 1) * 256] = low
                rl_o[s * heads + h, :, j * 256 : (j + 1) * 256] = jnp.broadcast_to(rl, (8, 256))
                tops.append((mm(v_t[a * HD : (a + 1) * HD], low) * rl).astype(BF16))
            both = jnp.concatenate(tops, axis=0)
            ctxt[pl.ds(off, 128), qrow] = both
            ctx[qrow, pl.ds(off, 128)] = transpose(both)
        ecopy.start()
        return 0
    n = seqs * pairs
    lax.fori_loop(0, n, attend, 0)
    done = 1 + max([t for t, _ in schedule], default=levels + 2)
    ctx_copies = [pltpu.make_async_copy(ctx, ctx_o, store.at[2]), pltpu.make_async_copy(ctxt, ctxt_o, store.at[3])]
    for c in ctx_copies: c.start()
    def close(i, _):
        r = pl.ds(pl.multiple_of(i * 256, 256), 256)
        res = tok[r, :].astype(F32) + mm(ctx[r, :], proj[:, 3 * inner :], NT)
        res_o[r, :] = res
        scale = lax.rsqrt(jnp.mean(res * res, axis=1, keepdims=True) + EPSILON)
        second[r, :] = (res * scale * gain2[...]).astype(BF16)
        return 0
    lax.fori_loop(0, rows // 256, close, 0)
    for t in range(done, 2 * levels + 4): run(t)
    in_copy = pltpu.make_async_copy(w.at[1], in_o, store.at[4])
    in_copy.start()
    chunk = 512
    per = hidden // chunk
    def widen(i, _):
        slot = i % 2
        r = pl.ds(pl.multiple_of((i // per) * 256, 256), 256)
        c = pl.ds(pl.multiple_of((i % per) * chunk, chunk), chunk)
        gcopy = pltpu.make_async_copy(gp.at[slot], gp_o.at[r, c], gstore.at[slot])
        if comm:
            for t in range(max(done, 2 * levels + 4), len(steps)):
                @pl.when(i == 4 * (t - 2 * levels - 4 + 1))
                def _():
                    run(t)
        @pl.when(i >= 2)
        def _():
            gcopy.wait()
        a, grad = gelu_both(mm(second[r, :], w[1, :, c]))
        act[r, c] = a.astype(BF16)
        gp[slot] = grad.astype(BF16)
        gcopy.start()
        return 0
    lax.fori_loop(0, rows // 256 * per, widen, 0)
    act_copy = pltpu.make_async_copy(act, act_o, store.at[5])
    act_copy.start()
    back_copy = pltpu.make_async_copy(w.at[2], back_o, store.at[6])
    back_copy.start()
    def narrow(i, _):
        r = pl.ds(pl.multiple_of(i * 256, 256), 256)
        out[r, :] = (res_o[r, :] + mm(act[r, :], w[2], NT)).astype(out.dtype)
        return 0
    lax.fori_loop(0, rows // 256, narrow, 0)
    for c in [proj_copy, mixed_copy, *ctx_copies, in_copy, act_copy, back_copy]: c.wait()
    for slot in range(2):
        pltpu.make_async_copy(e.at[slot], e_o.at[0], estore.at[slot]).wait()
        pltpu.make_async_copy(gp.at[slot], gp_o.at[pl.ds(0, 256), pl.ds(0, chunk)], gstore.at[slot]).wait()
    if comm:
        for u in range(3): g.sendwait(u)

def forward(levels, comm, tok, seg, gains, table, weights, schedule=()):
    rows, width = tok.shape
    heads = table.shape[1]
    inner = heads * HD
    hidden = weights[2].shape[1] * (8 if comm else 1)
    seqs, pairs = rows // SEQ, heads // 2
    sds = jax.ShapeDtypeStruct
    vm, hb = pl.BlockSpec(memory_space=pltpu.VMEM), pl.BlockSpec(memory_space=pl.ANY)
    outs = [(sds((rows, width), BF16), vm), (sds((width, 4 * inner), BF16), hb), (sds((width, hidden), BF16), hb), (sds((width, hidden), BF16), hb),
            (sds((rows, 3 * inner), BF16), hb), (sds((seqs * pairs, 2, SEQ, SEQ), BF16), hb), (sds((seqs * heads, 8, SEQ), F32), vm), (sds((rows, inner), BF16), hb), (sds((inner, rows), BF16), hb),
            (sds((rows, width), F32), vm), (sds((rows, hidden), BF16), hb), (sds((rows, hidden), BF16), hb)]
    scratch = [pltpu.VMEM((3, width, hidden), BF16), pltpu.VMEM((width, 4 * inner), BF16), pltpu.VMEM((rows, width), BF16), pltpu.VMEM((rows, 3 * inner), BF16),
               pltpu.VMEM((heads, EDGE, 2 * SEQ - EDGE), F32), pltpu.VMEM((seqs, SEQ, SEQ), F32), pltpu.VMEM((2, 2, SEQ, SEQ), BF16),
               pltpu.VMEM((rows, inner), BF16), pltpu.VMEM((inner, rows), BF16), pltpu.VMEM((rows, hidden), BF16), pltpu.VMEM((2, 256, 512), BF16), pltpu.VMEM((rows, width), BF16),
               pltpu.SemaphoreType.DMA((4,)), pltpu.SemaphoreType.DMA((7,)), pltpu.SemaphoreType.DMA((2,)), pltpu.SemaphoreType.DMA((2,))]
    if comm:
        scratch += gather_sems(3, levels) + [pltpu.VMEM((3, *weights[2].shape), BF16)]
    args = [tok, seg, gains, jnp.pad(table.T, ((0, -heads % 16), (0, 0))), *weights]
    specs = [vm] * 4 + [vm if comm else hb] * 4
    params = dict(collective_id=0, has_side_effects=True) if comm else {}
    return pl.pallas_call(functools.partial(forward_kernel, levels, comm, schedule), out_shape=[o[0] for o in outs], in_specs=specs, out_specs=[o[1] for o in outs],
        scratch_shapes=scratch, compiler_params=pltpu.CompilerParams(vmem_limit_bytes=63 << 20, **params), name="forward")(*args)

def transpose_into(src, dst):
    n, w = src.shape
    def one(i, _):
        r = pl.ds(pl.multiple_of(i * 128, 128), 128)
        for c in range(w // 128):
            dst[c * 128 : (c + 1) * 128, r] = src[r, c * 128 : (c + 1) * 128].T
        return 0
    lax.fori_loop(0, n // 128, one, 0)

def norm_back(v, dy, gain):
    r = lax.rsqrt(jnp.mean(v * v, axis=1, keepdims=True) + EPSILON)
    unit = v * r
    a = dy * gain
    part = r * (a - unit * jnp.mean(a * unit, axis=1, keepdims=True))
    return part, jnp.sum(dy * unit, axis=0, keepdims=True), unit

def backward_kernel(levels, comm, plan, gains, rl, tok_h, cot_h, proj_h, in_h, back_h, mixed_h, e_h, ctx_h, ctxt_h, res_h, act_h, gp_h, *rest):
    if comm:
        (tg_o, small_o, qkv_o, out_o, gin_o, gback_o), rest = rest[:6], rest[6:]
    else:
        (tg_o, small_o, proj_o, gin_o, gback_o), rest = rest[:5], rest[5:]
    (u1, u2, b, t, f, e, qkv, racc, far, own, staged, load, stream, eload, qload, store), rest = rest[:16], rest[16:]
    gain1, gain2 = gains.at[0:1], gains.at[1:2]
    rows, width = f.shape[1], f.shape[2]
    hidden = u1.shape[1]
    inner = width
    heads = racc.shape[0]
    pairs, seqs = heads // 2, rows // SEQ
    small, rest = rest[:5], rest[5:]
    def local(src, dst, sem):
        return pltpu.make_async_copy(src, dst, sem)
    loads = {"cot": local(cot_h, f.at[2], load.at[0]), "back": local(back_h, u1, load.at[1]), "res": local(res_h, f.at[0], load.at[2]), "in": local(in_h, u2, load.at[3])}
    chunk = hidden // 4
    if comm:
        cross, free = rest[:9], rest[9]
        me = Place()
        order = (me.gd, me.xd, me.yd, me.d)
        cols = [pl.ds(pl.multiple_of((o // 2) * chunk, chunk), chunk) for o in order]
    else:
        cols = [pl.ds(q * chunk, chunk) for q in range(4)]
    def act_load(q):
        return local(act_h.at[:, cols[q]], b.at[1 + q % 2], stream.at[0, q % 2])
    def gp_load(q):
        return local(gp_h.at[:, cols[q]], b.at[3 + q % 2], stream.at[1, q % 2])
    loads["cot"].start()
    act_load(0).start()
    loads["res"].start()
    loads["back"].start()
    gp_load(0).start()
    act_load(1).start()
    loads["in"].start()
    gp_load(1).start()
    if comm:
        greet_all(me, levels)
        sc = Scatter(me, levels, width // levels, own.shape[3], own, staged, u2, *cross)
        sm = Small(me, levels, *small)
        mine = sm.mine.at[0]
    else:
        mine = small[0].at[0]
    mine[...] = jnp.zeros(mine.shape, F32)
    racc[...] = jnp.zeros(racc.shape, F32)
    far[...] = jnp.zeros(far.shape, F32)
    loads["cot"].wait()
    def lower(i, _):
        r = pl.ds(pl.multiple_of(i * 128, 128), 128)
        b[0, r, :] = f[2, r, :].astype(BF16)
        return 0
    lax.fori_loop(0, rows // 128, lower, 0)
    transpose_into(b.at[0], t.at[0])
    loads["res"].wait()
    def renorm(i, _):
        r = pl.ds(pl.multiple_of(i * 128, 128), 128)
        v = f[0, r, :]
        s = lax.rsqrt(jnp.mean(v * v, axis=1, keepdims=True) + EPSILON)
        b[5, r, :] = (v * s * gain2[...]).astype(BF16)
        return 0
    lax.fori_loop(0, rows // 128, renorm, 0)
    transpose_into(b.at[5], t.at[1])
    half = chunk // 2
    def weight_grad(u, q, left, right):
        def one(i, _):
            r = pl.ds(pl.multiple_of(i * 256, 256), 256)
            g = mm(left[r, :], right[...]).astype(BF16)
            if comm:
                mine_first = me.c == 0
                own[u, q, r, :] = jnp.where(mine_first, g[:, :half], g[:, half:])
                staged[u, q % 2, r, :] = jnp.where(mine_first, g[:, half:], g[:, :half])
            else:
                own[u, q, r, :] = g[:, :half]
                staged[u, q % 2, r, :] = g[:, half:]
            return 0
        if q >= 2:
            if comm:
                sc.ccopy(u, q - 2).wait_send()
            else:
                put(u, q - 2)[1].wait()
        lax.fori_loop(0, width // 256, one, 0)
        if comm:
            sc.core_start(u, q)
        else:
            for c in put(u, q): c.start()
    def put(u, q):
        dst = (gback_o, gin_o)[u]
        return (local(own.at[u, q], dst.at[:, pl.ds(q * chunk, half)], store.at[u, 0, q]), local(staged.at[u, q % 2], dst.at[:, pl.ds(q * chunk + half, half)], store.at[u, 1, q]))
    def event(name, *a):
        if comm: getattr(sc, name)(*a)
    for q in range(4):
        act, gp = b.at[1 + q % 2], b.at[3 + q % 2]
        act_load(q).wait()
        weight_grad(0, q, t.at[0], act)
        if q + 2 < 4: act_load(q + 2).start()
        if q == 0: loads["back"].wait()
        gp_load(q).wait()
        def widen(i, _):
            r = pl.ds(pl.multiple_of(i * 256, 256), 256)
            b[5, r, :] = (mm(b[0, r, :], u1[:, cols[q]]) * gp[r, :].astype(F32)).astype(BF16)
            return 0
        lax.fori_loop(0, rows // 256, widen, 0)
        if q + 2 < 4: gp_load(q + 2).start()
        if q == 3:
            proj_load = local(proj_h, u1, load.at[4])
            proj_load.start()
        event("core_add", 0, q)
        weight_grad(1, q, t.at[1], b.at[5])
        if q == 0: loads["in"].wait()
        def narrow(i, _):
            r = pl.ds(pl.multiple_of(i * 256, 256), 256)
            g = mm(b[5, r, :], u2[:, cols[q]], NT)
            f[1, r, :] = g if q == 0 else f[1, r, :] + g
            return 0
        lax.fori_loop(0, rows // 256, narrow, 0)
        event("core_add", 1, q)
        if q == 2: event("cross_one", 0)
        if q == 3: event("cross_one", 1)
    ctx_loads = [local(ctx_h, b.at[5], load.at[5]), local(ctxt_h, t.at[2], load.at[6])]
    for c in ctx_loads: c.start()
    def norm_two(i, total):
        r = pl.ds(pl.multiple_of(i * 128, 128), 128)
        part, g, _ = norm_back(f[0, r, :], f[1, r, :], gain2[...])
        grad = f[2, r, :] + part
        f[0, r, :] = grad
        b[0, r, :] = grad.astype(BF16)
        return total + g
    mine[1:2, :] = lax.fori_loop(0, rows // 128, norm_two, jnp.zeros((1, width), F32))
    transpose_into(b.at[0], t.at[0])
    proj_load.wait()
    def context_back(i, _):
        r = pl.ds(pl.multiple_of(i * 256, 256), 256)
        b[4, r, :] = mm(b[0, r, :], u1[:, 3 * inner :]).astype(BF16)
        return 0
    lax.fori_loop(0, rows // 256, context_back, 0)
    for c in ctx_loads: c.wait()
    def out_grad(i, _):
        r = pl.ds(pl.multiple_of(i * 256, 256), 256)
        b[6, r, :] = mm(t[0, r, :], b[5]).astype(BF16)
        return 0
    lax.fori_loop(0, width // 256, out_grad, 0)
    tok_load = local(tok_h, b.at[0], load.at[7])
    tok_load.start()
    tok_load.wait()
    def renorm_one(i, _):
        r = pl.ds(pl.multiple_of(i * 128, 128), 128)
        v = b[0, r, :].astype(F32)
        s = lax.rsqrt(jnp.mean(v * v, axis=1, keepdims=True) + EPSILON)
        b[5, r, :] = (v * s * gain1[...]).astype(BF16)
        return 0
    lax.fori_loop(0, rows // 128, renorm_one, 0)
    transpose_into(b.at[5], t.at[1])
    n = seqs * pairs
    def fetch(i, slot):
        s, p = i // pairs, i % pairs
        row = pl.ds(pl.multiple_of(s * SEQ, SEQ), SEQ)
        return [local(e_h.at[i], e.at[slot], eload.at[slot])] + [
            local(mixed_h.at[row, pl.ds(pl.multiple_of(k * inner + p * 128, 128), 128)], qkv.at[slot, k], qload.at[slot, k]) for k in range(3)]
    for c in fetch(0, 0): c.start()
    low_lanes = lax.broadcasted_iota(jnp.int32, (SEQ, 128), 1) < HD
    blocks = SEQ // EDGE
    def attend_back(i, _):
        s, p = i // pairs, i % pairs
        slot = i % 2
        @pl.when(i + 1 < n)
        def _():
            for c in fetch(i + 1, (i + 1) % 2): c.start()
        for at, name, args in plan:
            @pl.when(i == at)
            def _():
                event(name, *args)
        for c in fetch(i, slot): c.wait()
        row = pl.ds(pl.multiple_of(s * SEQ, SEQ), SEQ)
        off = pl.multiple_of(p * 128, 128)
        q, k, v = qkv[slot, 0] * jnp.asarray(SCALING, BF16), qkv[slot, 1], qkv[slot, 2]
        k_t = k.T
        do_t = b[4, row, pl.ds(off, 128)].T.astype(F32)
        o_t = t[2, pl.ds(off, 128), row].astype(F32)
        scaled = []
        for a in range(2):
            part = do_t[a * HD : (a + 1) * HD] * rl[s * heads + 2 * p + a, :1, :]
            scaled.append(part.astype(BF16))
        dos_t = jnp.concatenate(scaled, axis=0)
        dos = dos_t.T
        prod = dos_t.astype(F32) * o_t
        dq, dk, dv = [], [], []
        for a in range(2):
            h = 2 * p + a
            delta = jnp.sum(prod[a * HD : (a + 1) * HD], axis=0, keepdims=True)
            va = jnp.where(low_lanes == (a == 0), v, jnp.zeros_like(v))
            low = []
            sums = [None] * 3
            fars = [None] * 2
            for kb in range(blocks):
                ek = e[slot, a, kb * EDGE : (kb + 1) * EDGE, :]
                ds = ek.astype(F32) * (mm(va[kb * EDGE : (kb + 1) * EDGE], dos_t) - delta)
                low.append(ds.astype(BF16))
                for qb in range(blocks):
                    piece = ds[:, qb * EDGE : (qb + 1) * EDGE]
                    gap = kb - qb
                    if abs(gap) <= 1:
                        sums[gap + 1] = piece if sums[gap + 1] is None else sums[gap + 1] + piece
                    else:
                        w = 1 if gap > 0 else 0
                        piece = jnp.sum(piece.reshape(EDGE // 8, 8, EDGE), axis=0)
                        fars[w] = piece if fars[w] is None else fars[w] + piece
            for w in range(3):
                racc[h, w] += sums[w]
            for w in range(2):
                far[h, w] += fars[w]
            low = jnp.concatenate(low, axis=0)
            dv.append(mm(e[slot, a], dos))
            dk.append(mm(low, q))
            dq.append(mm(k_t[a * HD : (a + 1) * HD], low))
        b[1, row, pl.ds(off, 128)] = (jnp.concatenate(dq, axis=0) * SCALING).astype(BF16).T
        b[2, row, pl.ds(off, 128)] = jnp.where(low_lanes, dk[0], dk[1]).astype(BF16)
        b[3, row, pl.ds(off, 128)] = jnp.where(low_lanes, dv[0], dv[1]).astype(BF16)
        return 0
    lax.fori_loop(0, n, attend_back, 0)
    if comm:
        for u in range(2):
            (gback_o, gin_o)[u][...] = sc.finish(u)
        for u in range(2): sc.sendwait(u)
        sc.release(free)
    part, packed = own.shape[3] * 3 // 4, own.shape[3]
    def proj_grad(i, _):
        r = pl.ds(pl.multiple_of(i * 256, 256), 256)
        left = t[1, r, :]
        g = jnp.concatenate([mm(left, b[1 + k]).astype(BF16) for k in range(3)], axis=1)
        o = b[6, r, :]
        if comm:
            quarter = packed - part
            for d in range(hidden // packed):
                u2[r, d * packed : (d + 1) * packed] = jnp.concatenate([g[:, d * part : (d + 1) * part], o[:, d * quarter : (d + 1) * quarter]], axis=1)
        else:
            u2[r, : 3 * inner] = g
            u2[r, 3 * inner :] = o
        return 0
    lax.fori_loop(0, width // 256, proj_grad, 0)
    if comm:
        sc.acquire(free)
        for q in range(4): sc.core_start(2, q)
        for q in range(4): sc.core_add(2, q)
    else:
        proj_put = local(u2, proj_o, store.at[0, 0, 4])
        proj_put.start()
    span = 2 * EDGE
    c = lax.broadcasted_iota(jnp.int32, (span, 128), 0)
    offs = EDGE - 1 - c
    bucket_lane = lax.broadcasted_iota(jnp.int32, (span, 128), 1)
    hots = [(bucket_of(offs + EDGE * w) == bucket_lane).astype(F32) for w in (-1, 0, 1)]
    lane = lax.broadcasted_iota(jnp.int32, (1, 128), 1)
    mirror = (lax.broadcasted_iota(jnp.int32, (EDGE, EDGE), 0) + lax.broadcasted_iota(jnp.int32, (EDGE, EDGE), 1) == EDGE - 1).astype(F32)
    at_row = lax.broadcasted_iota(jnp.int32, (16, 128), 0)
    def table_one(h, held):
        total = jnp.zeros((8, 128), F32)
        for w in range(3):
            upended = lax.dot_general(mirror, racc[h, w], NN, precision=lax.Precision.HIGHEST, preferred_element_type=F32)
            wide = jnp.concatenate([upended, jnp.zeros((EDGE, EDGE), F32)], axis=1)
            turned = pltpu.roll(wide, 0, 1, stride=1, stride_axis=0)
            diag = jnp.sum(turned.reshape(EDGE // 8, 8, span), axis=0)
            total = total + lax.dot_general(diag, hots[w], NN, precision=lax.Precision.HIGHEST, preferred_element_type=F32)
        row = jnp.sum(total, axis=0, keepdims=True)
        left = jnp.sum(far[h, 0])
        right = jnp.sum(far[h, 1])
        row = row + jnp.where(lane == BUCKETS // 2 - 1, left, 0.0) + jnp.where(lane == BUCKETS - 1, right, 0.0)
        return held + jnp.where(at_row == 2 + h, row, 0.0)
    mine[:, :128] += lax.fori_loop(0, heads, table_one, jnp.zeros((16, 128), F32))
    if comm: sc.cross_one(2)
    def norm_one(i, total):
        r = pl.ds(pl.multiple_of(i * 256, 256), 256)
        dy = mm(b[1, r, :], u1[:, :inner], NT) + mm(b[2, r, :], u1[:, inner : 2 * inner], NT) + mm(b[3, r, :], u1[:, 2 * inner : 3 * inner], NT)
        part, g, _ = norm_back(b[0, r, :].astype(F32), dy, gain1[...])
        f[1, r, :] = f[0, r, :] + part
        return total + g
    mine[0:1, :] = lax.fori_loop(0, rows // 256, norm_one, jnp.zeros((1, width), F32))
    tg_copy = local(f.at[1], tg_o, load.at[8])
    tg_copy.start()
    if comm:
        sm.start(0)
        sm.add(0); sm.start(1)
        sc.cross_two(2)
        sm.add(1); sm.start(2)
        sc.cross_three(2)
        sc.line_open(2)
        sm.add(2); sm.spread()
        for k in range(1, levels): sc.line_step(2, k)
        total = sc.finish(2)
        qkv_o[...] = total[:, :part]
        out_o[...] = total[:, part:]
        small_o[...] = sm.total()
        sc.sendwait(2)
        sm.sendwait()
    else:
        small_o[...] = mine[...]
        for u in range(2):
            for q in range(4):
                x, y = put(u, q)
                x.wait()
                if q >= 2: y.wait()
        proj_put.wait()
    tg_copy.wait()

def backward(levels, comm, plan, gains, rl, tok, cot, proj, w_in, w_back, mixed, e, ctx, ctxt, res, act, gp, share=None):
    rows, width = tok.shape
    hidden = w_in.shape[1]
    heads = rl.shape[0] // (rows // SEQ)
    sds = jax.ShapeDtypeStruct
    vm, hb = pl.BlockSpec(memory_space=pltpu.VMEM), pl.BlockSpec(memory_space=pl.ANY)
    shape = (16, width)
    half = hidden // 8
    piece_rows = width // levels
    outs = [(sds((rows, width), F32), hb), (sds(shape, F32), vm)]
    if comm:
        outs += [(sds((piece_rows, half * 3 // 4), F32), vm), (sds((piece_rows, half // 4), F32), vm), (sds((piece_rows, half), F32), vm), (sds((piece_rows, half), F32), vm)]
    else:
        outs += [(sds((width, hidden), BF16), hb)] * 3
    D = pltpu.SemaphoreType.DMA
    scratch = [pltpu.VMEM((width, hidden), BF16), pltpu.VMEM((width, hidden), BF16), pltpu.VMEM((7, rows, width), BF16), pltpu.VMEM((3, width, rows), BF16), pltpu.VMEM((3, rows, width), F32),
               pltpu.VMEM((2, 2, SEQ, SEQ), BF16), pltpu.VMEM((2, 3, SEQ, 128), BF16), pltpu.VMEM((heads, 3, EDGE, EDGE), F32), pltpu.VMEM((heads, 2, 8, EDGE), F32),
               pltpu.VMEM((2, 4, width, half), BF16), pltpu.VMEM((2, 2, width, half), BF16), D((9,)), D((2, 2)), D((2,)), D((2, 3)), D((2, 2, 5))] + small_scratch(levels, shape)
    if comm:
        scratch += [pltpu.VMEM((2, 4, width, half), BF16), pltpu.VMEM((2, 2, 3, width // 2, half), BF16), pltpu.VMEM((2, 2, levels - 1, piece_rows, half), BF16),
                    D((3, 4)), D((3, 4)), D((3, 2, 3)), D((3, 2, 3)), D((3, 2, levels - 1)), D((3, 2, levels - 1)), pltpu.SemaphoreType.REGULAR]
    params = dict(collective_id=1, has_side_effects=True) if comm else {}
    return pl.pallas_call(functools.partial(backward_kernel, levels, comm, plan), out_shape=[o[0] for o in outs], in_specs=[vm] * 2 + [hb] * 12, out_specs=[o[1] for o in outs],
        scratch_shapes=scratch, compiler_params=pltpu.CompilerParams(vmem_limit_bytes=63 << 20, **params), name="backward")(gains, rl, tok, cot, proj, w_in, w_back, mixed, e, ctx, ctxt, res, act, gp)

def scatter_plain(grad):
    part = lax.psum_scatter(grad, "dp", scatter_dimension=1, tiled=True)
    return lax.psum_scatter(part, "mp", scatter_dimension=0, tiled=True).astype(F32)


FORWARD_PLAN = ((7, 1), (8, 4), (9, 7), (10, 10))
BACKWARD_PLAN = (
    (0, "cross_two", (0,)), (1, "cross_two", (1,)), (3, "cross_three", (0,)), (3, "line_open", (0,)), (4, "line_step", (0, 1)),
    (5, "cross_three", (1,)), (5, "line_open", (1,)), (6, "line_step", (0, 2)), (7, "line_step", (1, 1)), (8, "line_step", (0, 3)),
    (9, "line_step", (1, 2)), (11, "line_step", (1, 3)),
)


def body(tokens, segment_ids, cotangent, gain_one, w_qkv, w_out, rel_table, gain_two, w_in, w_back):
    axes = ("mp", "dp")
    levels, width = lax.axis_size("mp"), lax.axis_size("dp")
    heads = rel_table.shape[1]
    inner = heads * HD
    segments = segment_ids.reshape(-1, SEQ).astype(F32)
    packed = w_qkv.shape[1] + w_out.shape[1]
    own = width == 8 and levels == 4 and packed == w_in.shape[1] and packed % 128 == 0
    gains = jnp.stack([gain_one, gain_two]).astype(F32)
    weights = [w_qkv, w_out, w_in, w_back]
    if not own:
        weights = [lax.all_gather(lax.all_gather(m, "mp", axis=0, tiled=True), "dp", axis=1, tiled=True) for m in weights]
    held = forward(levels, own, tokens, segments, gains, rel_table, weights, FORWARD_PLAN)
    layer_out, proj, full_in, full_back, mixed, e, rl, ctx, ctxt, res, act, gp = held
    grads = backward(levels, own, BACKWARD_PLAN, gains, rl, tokens, cotangent, proj, full_in, full_back, mixed, e, ctx, ctxt, res, act, gp)
    if own:
        tokens_grad, small, qkv_grad, out_grad, in_grad, back_grad = grads
    else:
        tokens_grad, small, proj_grad, in_grad, back_grad = grads
        small = lax.psum(small, axes)
        qkv_grad, out_grad = scatter_plain(proj_grad[:, : 3 * inner]), scatter_plain(proj_grad[:, 3 * inner :])
        in_grad, back_grad = scatter_plain(in_grad), scatter_plain(back_grad)
    table_grad = small[2 : 2 + heads, :BUCKETS].T
    return layer_out, tokens_grad, small[0], qkv_grad, out_grad, table_grad, small[1], in_grad, back_grad


def solution(mesh):
    both = ("mp", "dp")
    weight = P("mp", "dp")
    return jax.shard_map(
        body,
        mesh=mesh,
        in_specs=(P(both, None), P(both), P(both, None), P(), weight, weight, P(), P(), weight, weight),
        out_specs=(P(both, None), P(both, None), P(), weight, weight, P(), P(), weight, weight),
        check_vma=False,
    )
```

```python
import functools

import jax
import jax.numpy as jnp
from jax import lax
from jax.experimental import pallas as pl
from jax.experimental.pallas import tpu as pltpu
from jax.sharding import PartitionSpec as P

MESH = pl.DeviceIdType.MESH

class Place:
    def __init__(self):
        self.z = lax.axis_index("mp"); self.d = lax.axis_index("dp")
        d = self.d
        self.c = lax.rem(d, 2); self.x = lax.rem(d // 2, 2); self.y = d // 4
        self.xd = d + 2 - 4 * self.x
        self.yd = d + 4 - 8 * self.y
        self.cd = d + 1 - 2 * self.c
        self.gd = self.xd + 4 - 8 * self.y
    def barrier(self, levels):
        bar = pltpu.get_barrier_semaphore()
        for t in (self.xd, self.yd, self.cd):
            pl.semaphore_signal(bar, inc=1, device_id=(self.z, t), device_id_type=MESH)
        @pl.when(self.z > 0)
        def _():
            pl.semaphore_signal(bar, inc=1, device_id=(self.z - 1, self.d), device_id_type=MESH)
        @pl.when(self.z < levels - 1)
        def _():
            pl.semaphore_signal(bar, inc=1, device_id=(self.z + 1, self.d), device_id_type=MESH)
        peers = 3 + jnp.minimum(self.z, 1) + jnp.minimum(levels - 1 - self.z, 1)
        pl.semaphore_wait(bar, peers)

class Gather:
    def __init__(self, me, levels, piece, full, zs, zr, xs, xr, cs, cr):
        self.me, self.levels, self.piece, self.full = me, levels, piece, full
        self.zs, self.zr, self.xs, self.xr, self.cs, self.cr = zs, zr, xs, xr, cs, cr
        self.rows, self.cols = piece.shape[1], piece.shape[2]
    def blk(self, u, z, d, r0=0, nr=None):
        nr = self.rows if nr is None else nr
        return self.full.at[u, pl.ds(pl.multiple_of(z * self.rows + r0, 16), nr), pl.ds(pl.multiple_of(d * self.cols, 128), self.cols)]
    def col(self, u, d):
        return self.full.at[u, :, pl.ds(pl.multiple_of(d * self.cols, 128), self.cols)]
    def cp(self, src, dst, ss, rs, dev):
        return pltpu.make_async_remote_copy(src_ref=src, dst_ref=dst, send_sem=ss, recv_sem=rs, device_id=dev, device_id_type=MESH)
    def zcopy(self, u, up, k, z, src=None):
        b = self.blk(u, z, self.me.d)
        t = self.me.z + (1 if up else -1)
        return self.cp(b if src is None else src, b, self.zs.at[u, 0 if up else 1, k], self.zr.at[u, 0 if up else 1, k], (t, self.me.d))
    def xcopy(self, u, z, d, src=None):
        b = self.blk(u, z, d)
        return self.cp(b if src is None else src, b, self.xs.at[u, 0, z], self.xr.at[u, 0, z], (self.me.z, self.me.xd))
    def ycopy(self, u, z, d, src=None):
        b = self.blk(u, z, d)
        return self.cp(b if src is None else src, b, self.xs.at[u, 1, z], self.xr.at[u, 1, z], (self.me.z, self.me.yd))
    def half(self, u, z, d, way):
        h = self.rows // 2
        b = self.blk(u, z, d, way * h, h)
        return self.cp(b, b, self.xs.at[u, 2 + way, z], self.xr.at[u, 2 + way, z], (self.me.z, self.me.yd if way == 0 else self.me.xd))
    def ccopy(self, u, which, d):
        b = self.col(u, d)
        return self.cp(b, b, self.cs.at[u, which], self.cr.at[u, which], (self.me.z, self.me.cd))
    def zstep(self, u, k):
        me = self.me
        if k == 0:
            src = self.piece.at[u]
            self.xcopy(u, me.z, me.d, src).start()
            self.ycopy(u, me.z, me.d, src).start()
            @pl.when(me.z < self.levels - 1)
            def _():
                self.zcopy(u, True, 0, me.z, src).start()
            @pl.when(me.z > 0)
            def _():
                self.zcopy(u, False, 0, me.z, src).start()
            self.blk(u, me.z, me.d)[...] = self.piece[u]
            return
        @pl.when(me.z - k >= 0)
        def _():
            z = me.z - k
            self.zcopy(u, True, k - 1, z).wait_recv()
            if k < self.levels - 1:
                @pl.when(me.z < self.levels - 1)
                def _():
                    self.zcopy(u, True, k, z).start()
            self.xcopy(u, z, me.d).start()
            self.ycopy(u, z, me.d).start()
        @pl.when(me.z + k < self.levels)
        def _():
            z = me.z + k
            self.zcopy(u, False, k - 1, z).wait_recv()
            if k < self.levels - 1:
                @pl.when(me.z > 0)
                def _():
                    self.zcopy(u, False, k, z).start()
            self.xcopy(u, z, me.d).start()
            self.ycopy(u, z, me.d).start()
    def xystep(self, u, k):
        me = self.me
        def one(z):
            self.xcopy(u, z, me.xd).wait_recv()
            self.half(u, z, me.xd, 0).start()
            self.ycopy(u, z, me.yd).wait_recv()
            self.half(u, z, me.yd, 1).start()
        if k == 0:
            one(me.z)
            return
        @pl.when(me.z - k >= 0)
        def _():
            one(me.z - k)
        @pl.when(me.z + k < self.levels)
        def _():
            one(me.z + k)
    def corestep(self, u, which):
        me = self.me
        self.ccopy(u, which, (me.d, me.xd, me.yd, me.gd)[which]).start()
    def diagstep(self, u):
        me = self.me
        for z in range(self.levels):
            self.half(u, z, me.gd, 0).wait_recv()
            self.half(u, z, me.gd, 1).wait_recv()
    def corewait(self, u):
        me = self.me
        for which in range(4):
            self.ccopy(u, which, (me.cd, me.cd + me.xd - me.d, me.cd + me.yd - me.d, me.cd + me.gd - me.d)[which]).wait_recv()
    def sendwait(self, u):
        me = self.me
        for k in range(self.levels - 1):
            @pl.when((me.z < self.levels - 1) & (me.z - k >= 0))
            def _():
                self.zcopy(u, True, k, me.z - k).wait_send()
            @pl.when((me.z > 0) & (me.z + k < self.levels))
            def _():
                self.zcopy(u, False, k, me.z + k).wait_send()
        for z in range(self.levels):
            self.xcopy(u, z, me.d).wait_send()
            self.ycopy(u, z, me.d).wait_send()
            self.half(u, z, me.xd, 0).wait_send()
            self.half(u, z, me.yd, 1).wait_send()
        for which in range(4):
            self.ccopy(u, which, me.d).wait_send()
    def events(self, units):
        L = self.levels
        def at(t):
            u, k = divmod(t, L + 1)
            return (u, k) if 0 <= t and u < units and k < L else (None, None)
        out = []
        for s in range(units * (L + 1) + 3):
            step = []
            u, k = at(s)
            if u is not None:
                step.append(functools.partial(self.zstep, u, k))
                if k == L - 1:
                    step.append(functools.partial(self.corestep, u, 0))
            u, k = at(s - 2)
            if u is not None:
                step.append(functools.partial(self.xystep, u, k))
                if k == L - 1:
                    step.append(functools.partial(self.corestep, u, 1))
                    step.append(functools.partial(self.corestep, u, 2))
            u, k = at(s - 3)
            if k == L - 1:
                step.append(functools.partial(self.diagstep, u))
                step.append(functools.partial(self.corestep, u, 3))
            u, k = at(s - 4)
            if k == L - 1:
                step.append(functools.partial(self.corewait, u))
            out.append(step)
        return out

def gather_sems(units, levels):
    return [pltpu.SemaphoreType.DMA((units, 2, levels - 1))] * 2 + [pltpu.SemaphoreType.DMA((units, 4, levels))] * 2 + [pltpu.SemaphoreType.DMA((units, 4))] * 2

def greet_all(me, levels):
    bar = pltpu.get_barrier_semaphore()
    for t in (me.xd, me.yd, me.cd):
        pl.semaphore_signal(bar, inc=1, device_id=(me.z, t), device_id_type=MESH)
    for k in range(1, levels):
        pl.semaphore_signal(bar, inc=1, device_id=(lax.rem(me.z + k, levels), me.d), device_id_type=MESH)
    pl.semaphore_wait(bar, 2 + levels)

class Scatter:
    def __init__(self, me, levels, rows, cols, own, staged, matrix, core, cross, line, cs, cr, xs, xr, zs, zr):
        self.me, self.levels, self.rows, self.cols = me, levels, rows, cols
        self.grads, self.staged, self.matrix = own, staged, matrix
        self.core, self.cross, self.line = core, cross, line
        self.cs, self.cr, self.xs, self.xr, self.zs, self.zr = cs, cr, xs, xr, zs, zr
        self.order = (me.gd, me.xd, me.yd, me.d)
        self.half_rows = rows * levels // 2
    def cp(self, src, dst, ss, rs, dev):
        return pltpu.make_async_remote_copy(src_ref=src, dst_ref=dst, send_sem=ss, recv_sem=rs, device_id=dev, device_id_type=MESH)
    def add(self, dst, src):
        n = dst.shape[0]
        step = 96 if n % 96 == 0 else 16
        def one(i, _):
            at = pl.ds(pl.multiple_of(i * step, 16), step)
            dst[at, :] = dst[at, :] + src[at, :]
            return 0
        lax.fori_loop(0, n // step, one, 0)
    def core_start(self, u, q):
        self.ccopy(u, q).start()
    def index(self, d):
        return [i for i, o in enumerate(self.order) if o is d][0]
    def block(self, u, d, r0, nr):
        at = pl.ds(r0 if isinstance(r0, int) else pl.multiple_of(r0, 16), nr)
        if u < 2:
            return self.grads.at[u, self.index(d), at]
        return self.matrix.at[at, pl.ds(pl.multiple_of(d * self.cols, 128), self.cols)]
    def slot(self, u):
        return 0 if u == 2 else u
    def ccopy(self, u, q):
        s = self.slot(u)
        if u < 2:
            src = self.staged.at[u, q % 2]
        else:
            src = self.block(u, self.order[q] + self.me.cd - self.me.d, 0, self.rows * self.levels)
        return self.cp(src, self.core.at[s, q], self.cs.at[u, q], self.cr.at[u, q], (self.me.z, self.me.cd))
    def core_add(self, u, q):
        self.ccopy(u, q).wait_recv()
        self.add(self.block(u, self.order[q], 0, self.rows * self.levels), self.core.at[self.slot(u), q])
        if q == 0:
            self.xcopy(u, 0).start()
            self.ycopy(u, 0).start()
        if q == 1:
            self.xcopy(u, 1).start()
        if q == 2:
            self.ycopy(u, 1).start()
    def xcopy(self, u, slot):
        d = (self.me.gd, self.me.xd, self.me.xd)[slot]
        r0 = (0, 0, self.half_rows)[slot]
        return self.cp(self.block(u, d, r0, self.half_rows), self.cross.at[self.slot(u), 0, slot], self.xs.at[u, 0, slot], self.xr.at[u, 0, slot], (self.me.z, self.me.xd))
    def ycopy(self, u, slot):
        d = (self.me.gd, self.me.yd, self.me.yd)[slot]
        r0 = (self.half_rows, self.half_rows, 0)[slot]
        return self.cp(self.block(u, d, r0, self.half_rows), self.cross.at[self.slot(u), 1, slot], self.xs.at[u, 1, slot], self.xr.at[u, 1, slot], (self.me.z, self.me.yd))
    def zcopy(self, u, way, target):
        slot = target - 1 if way == 0 else target
        t = self.me.z + (1 if way == 0 else -1)
        return self.cp(self.block(u, self.me.d, target * self.rows, self.rows), self.line.at[self.slot(u), way, slot], self.zs.at[u, way, slot], self.zr.at[u, way, slot], (t, self.me.d))
    def cross_one(self, u):
        me, h, s = self.me, self.half_rows, self.slot(u)
        self.xcopy(u, 0).wait_recv()
        self.add(self.block(u, me.yd, 0, h), self.cross.at[s, 0, 0])
        self.ycopy(u, 2).start()
        self.ycopy(u, 0).wait_recv()
        self.add(self.block(u, me.xd, h, h), self.cross.at[s, 1, 0])
        self.xcopy(u, 2).start()
    def cross_two(self, u):
        me, h, s = self.me, self.half_rows, self.slot(u)
        self.xcopy(u, 1).wait_recv()
        self.add(self.block(u, me.d, 0, h), self.cross.at[s, 0, 1])
        self.ycopy(u, 1).wait_recv()
        self.add(self.block(u, me.d, h, h), self.cross.at[s, 1, 1])
    def cross_three(self, u):
        me, h, s = self.me, self.half_rows, self.slot(u)
        self.ycopy(u, 2).wait_recv()
        self.add(self.block(u, me.d, 0, h), self.cross.at[s, 1, 2])
        self.xcopy(u, 2).wait_recv()
        self.add(self.block(u, me.d, h, h), self.cross.at[s, 0, 2])
    def line_open(self, u):
        me, last = self.me, self.levels - 1
        @pl.when(me.z == 0)
        def _():
            for i in range(last):
                self.zcopy(u, 0, last - i).start()
        @pl.when(me.z == last)
        def _():
            for i in range(last):
                self.zcopy(u, 1, i).start()
    def line_step(self, u, k):
        me, last, s = self.me, self.levels - 1, self.slot(u)
        def take(way, target):
            self.zcopy(u, way, target).wait_recv()
            if k < last:
                at = target - 1 if way == 0 else target
                self.add(self.block(u, me.d, target * self.rows, self.rows), self.line.at[s, way, at])
                self.zcopy(u, way, target).start()
        @pl.when((me.z >= 1) & (me.z <= k))
        def _():
            take(0, last - k + me.z)
        @pl.when((me.z <= last - 1) & (me.z >= last - k))
        def _():
            take(1, k - last + me.z)
    def finish(self, u):
        me, last, s = self.me, self.levels - 1, self.slot(u)
        own = self.block(u, me.d, me.z * self.rows, self.rows)[...].astype(F32)
        below = self.line[s, 0, jnp.maximum(me.z - 1, 0)].astype(F32)
        above = self.line[s, 1, jnp.minimum(me.z, last - 1)].astype(F32)
        return own + jnp.where(me.z > 0, below, 0.0) + jnp.where(me.z < last, above, 0.0)
    def release(self, free):
        me, last = self.me, self.levels - 1
        for t in (me.xd, me.yd, me.cd):
            pl.semaphore_signal(free, inc=1, device_id=(me.z, t), device_id_type=MESH)
        @pl.when(me.z > 0)
        def _():
            pl.semaphore_signal(free, inc=1, device_id=(me.z - 1, me.d), device_id_type=MESH)
        @pl.when(me.z < last)
        def _():
            pl.semaphore_signal(free, inc=1, device_id=(me.z + 1, me.d), device_id_type=MESH)
    def acquire(self, free):
        me, last = self.me, self.levels - 1
        pl.semaphore_wait(free, 3 + jnp.minimum(me.z, 1) + jnp.minimum(last - me.z, 1))
    def sendwait(self, u):
        me, last = self.me, self.levels - 1
        for q in range(4):
            if u == 2 or q >= 2: self.ccopy(u, q).wait_send()
        for slot in range(3):
            self.xcopy(u, slot).wait_send()
            self.ycopy(u, slot).wait_send()
        for i in range(last):
            @pl.when(me.z < last - i)
            def _():
                self.zcopy(u, 0, last - i).wait_send()
            @pl.when(me.z > i)
            def _():
                self.zcopy(u, 1, i).wait_send()

class Small:
    def __init__(self, me, levels, mine, swap, slots, ss, rs):
        self.me, self.levels, self.mine, self.swap, self.slots, self.ss, self.rs = me, levels, mine, swap, slots, ss, rs
    def pair(self, i):
        t = (self.me.cd, self.me.xd, self.me.yd)[i]
        return pltpu.make_async_remote_copy(src_ref=self.mine.at[i], dst_ref=self.swap.at[i], send_sem=self.ss.at[i], recv_sem=self.rs.at[i], device_id=(self.me.z, t), device_id_type=MESH)
    def start(self, i):
        self.pair(i).start()
    def add(self, i):
        self.pair(i).wait_recv()
        self.mine[i + 1] = self.mine[i] + self.swap[i]
    def level(self, k):
        t = lax.rem(self.me.z + k, self.levels)
        return pltpu.make_async_remote_copy(src_ref=self.mine.at[3], dst_ref=self.slots.at[k - 1], send_sem=self.ss.at[2 + k], recv_sem=self.rs.at[2 + k], device_id=(t, self.me.d), device_id_type=MESH)
    def spread(self):
        for k in range(1, self.levels):
            self.level(k).start()
    def total(self):
        for k in range(1, self.levels):
            self.level(k).wait_recv()
        def at(level):
            k = lax.rem(self.me.z - level + self.levels, self.levels)
            held = self.slots[jnp.maximum(k - 1, 0)]
            return jnp.where(k == 0, self.mine[3], held)
        out = at(0)
        for level in range(1, self.levels):
            out = out + at(level)
        return out
    def sendwait(self):
        for i in range(3):
            self.pair(i).wait_send()
        for k in range(1, self.levels):
            self.level(k).wait_send()

def small_scratch(levels, shape):
    return [pltpu.VMEM((4, *shape), jnp.float32), pltpu.VMEM((3, *shape), jnp.float32), pltpu.VMEM((levels - 1, *shape), jnp.float32),
            *[pltpu.SemaphoreType.DMA((2 + levels,))] * 2]

SEQ, HD, BUCKETS = 512, 64, 32
EPSILON = 1e-06
NEGATIVE = -1e30
SCALING = 0.125
THRESHOLDS = (12, 16, 23, 32, 46, 64, 91)
F32, BF16 = jnp.float32, jnp.bfloat16
EDGE = 128
NT = (((1,), (1,)), ((), ()))
NN = (((1,), (0,)), ((), ()))

def mm(a, b, dims=NN):
    return lax.dot_general(a, b, dims, preferred_element_type=F32)

def bucket_of(offset):
    distance = jnp.abs(offset)
    larger = jnp.zeros_like(distance)
    for edge in THRESHOLDS:
        larger = larger + (distance >= edge).astype(jnp.int32)
    inside = jnp.where(distance < 8, distance, 8 + larger)
    return inside + BUCKETS // 2 * (offset > 0).astype(jnp.int32)

def build_bias(table_t, skew):
    heads, edge, width = skew.shape
    span = 1024
    c = lax.broadcasted_iota(jnp.int32, (BUCKETS, span), 1)
    c = jnp.where(c >= span - EDGE, c - span, c)
    hot = (bucket_of((SEQ - EDGE) - c) == lax.broadcasted_iota(jnp.int32, (BUCKETS, span), 0)).astype(BF16)
    flat = mm(table_t, hot)
    for h in range(heads):
        rows = jnp.broadcast_to(flat[h : h + 1, :], (edge, span))
        skew[h] = pltpu.roll(rows, 0, 1, stride=1, stride_axis=0)[:, :width]

def build_mask(seg, mask):
    wide = jnp.broadcast_to(seg, (EDGE, SEQ))
    for b in range(SEQ // EDGE):
        col = wide[:, b * EDGE : (b + 1) * EDGE].T
        tall = jnp.concatenate([col] * (SEQ // EDGE), axis=1)
        same = (tall == wide) & (wide > 0.0)
        k = lax.broadcasted_iota(jnp.int32, (EDGE, SEQ), 0) + b * EDGE
        q = lax.broadcasted_iota(jnp.int32, (EDGE, SEQ), 1)
        mask[b * EDGE : (b + 1) * EDGE, :] = jnp.where(same | (k == q), 0.0, NEGATIVE)

def transpose(x):
    return x.T

GELU_C = 0.7978845608028654
def gelu_both(x):
    x2 = x * x
    t = jnp.tanh(x * (GELU_C + (GELU_C * 0.044715) * x2))
    half = 0.5 * x
    one = 0.5 + 0.5 * t
    act = x * one
    grad = one + (half * (1.0 - t * t)) * (GELU_C + (3.0 * 0.044715 * GELU_C) * x2)
    return act, grad

def forward_kernel(levels, comm, schedule, tok, seg, gains, table_t, *rest):
    gain1, gain2 = gains.at[0:1], gains.at[1:2]
    weights, rest = rest[:4], rest[4:]
    if comm:
        piece, rest = rest[-1], rest[:-1]
        piece[0] = jnp.concatenate([weights[0][...], weights[1][...]], axis=1)
        piece[1] = weights[2][...]
        piece[2] = weights[3][...]
    (out, proj_o, in_o, back_o, mixed_o, e_o, rl_o, ctx_o, ctxt_o, res_o, act_o, gp_o), rest = rest[:12], rest[12:]
    (w, proj, normed, mixed, skew, mask, e, ctx, ctxt, act, gp, second, load, store, estore, gstore), sems = rest[:16], rest[16:]
    rows, width = tok.shape
    inner = width
    heads = skew.shape[0]
    pairs = heads // 2
    seqs = rows // SEQ
    hidden = act.shape[1]
    if comm:
        me = Place()
        me.barrier(levels)
        g = Gather(me, levels, piece, w, *sems)
        steps = g.events(3)
    else:
        steps = []
    def run(t):
        if t < len(steps):
            for call in steps[t]: call()
    if not comm:
        loads = [pltpu.make_async_copy(weights[0], proj.at[:, : 3 * inner], load.at[0]), pltpu.make_async_copy(weights[1], proj.at[:, 3 * inner :], load.at[1]),
                 pltpu.make_async_copy(weights[2], w.at[1], load.at[2]), pltpu.make_async_copy(weights[3], w.at[2], load.at[3])]
        for l in loads: l.start()
        for l in loads: l.wait()
    run(0)
    def norm_one(i, _):
        at = pl.ds(pl.multiple_of(i * 128, 128), 128)
        v = tok[at, :].astype(F32)
        r = lax.rsqrt(jnp.mean(v * v, axis=1, keepdims=True) + EPSILON)
        normed[at, :] = (v * r * gain1[...]).astype(BF16)
        return 0
    lax.fori_loop(0, rows // 128, norm_one, 0)
    run(1)
    build_bias(table_t[...], skew)
    run(2)
    for s in range(seqs):
        build_mask(seg[s : s + 1, :], mask.at[s])
    for t in range(3, levels + 4): run(t)
    if comm:
        packed = piece.shape[2]
        part = packed * 3 // 4
        blocks = hidden // packed
        def unpack(i, _):
            at = pl.ds(pl.multiple_of(i * 64, 64), 64)
            t = w[0, at, :]
            proj[at, :] = jnp.concatenate([t[:, d * packed : d * packed + part] for d in range(blocks)] + [t[:, d * packed + part : (d + 1) * packed] for d in range(blocks)], axis=1)
            return 0
        lax.fori_loop(0, width // 64, unpack, 0)
    proj_copy = pltpu.make_async_copy(proj, proj_o, store.at[0])
    proj_copy.start()
    def project(i, _):
        r = pl.ds(pl.multiple_of((i // 3) * 256, 256), 256)
        c = pl.ds(pl.multiple_of((i % 3) * inner, 128), inner)
        mixed[r, c] = mm(normed[r, :], proj[:, c]).astype(BF16)
        return 0
    lax.fori_loop(0, rows // 256 * 3, project, 0)
    mixed_copy = pltpu.make_async_copy(mixed, mixed_o, store.at[1])
    mixed_copy.start()
    low_lanes = lax.broadcasted_iota(jnp.int32, (256, 128), 1) < HD
    def attend(i, _):
        s, p = i // pairs, i % pairs
        slot = i % 2
        for t, at in schedule:
            @pl.when(i == at)
            def _():
                run(t)
        ecopy = pltpu.make_async_copy(e.at[slot], e_o.at[i], estore.at[slot])
        @pl.when(i >= 2)
        def _():
            ecopy.wait()
        row = pl.ds(pl.multiple_of(s * SEQ, SEQ), SEQ)
        off = pl.multiple_of(p * 128, 128)
        k = mixed[row, pl.ds(inner + off, 128)]
        v_t = transpose(mixed[row, pl.ds(2 * inner + off, 128)])
        for j in range(SEQ // 256):
            qrow = pl.ds(pl.multiple_of(s * SEQ + j * 256, 256), 256)
            q = mixed[qrow, pl.ds(off, 128)] * jnp.asarray(SCALING, BF16)
            tops = []
            for a in range(2):
                qa = jnp.where(low_lanes == (a == 0), q, jnp.zeros_like(q))
                h = 2 * p + a
                parts = []
                for b in range(SEQ // EDGE):
                    sc = mm(k[b * EDGE : (b + 1) * EDGE], qa, NT)
                    lo = SEQ - EDGE - b * EDGE + j * 256
                    parts.append(sc + (skew[h, :, lo : lo + 256] + mask[s, b * EDGE : (b + 1) * EDGE, j * 256 : (j + 1) * 256]))
                score = jnp.concatenate(parts, axis=0)
                top = jnp.max(score, axis=0, keepdims=True)
                ex = jnp.exp(score - top)
                rl = 1.0 / jnp.sum(ex, axis=0, keepdims=True)
                low = ex.astype(BF16)
                e[slot, a, :, j * 256 : (j + 1) * 256] = low
                rl_o[s * heads + h, :, j * 256 : (j + 1) * 256] = jnp.broadcast_to(rl, (8, 256))
                tops.append((mm(v_t[a * HD : (a + 1) * HD], low) * rl).astype(BF16))
            both = jnp.concatenate(tops, axis=0)
            ctxt[pl.ds(off, 128), qrow] = both
            ctx[qrow, pl.ds(off, 128)] = transpose(both)
        ecopy.start()
        return 0
    n = seqs * pairs
    lax.fori_loop(0, n, attend, 0)
    done = 1 + max([t for t, _ in schedule], default=levels + 3)
    ctx_copies = [pltpu.make_async_copy(ctx, ctx_o, store.at[2]), pltpu.make_async_copy(ctxt, ctxt_o, store.at[3])]
    for c in ctx_copies: c.start()
    def close(i, _):
        r = pl.ds(pl.multiple_of(i * 256, 256), 256)
        res = tok[r, :].astype(F32) + mm(ctx[r, :], proj[:, 3 * inner :], NT)
        res_o[r, :] = res
        scale = lax.rsqrt(jnp.mean(res * res, axis=1, keepdims=True) + EPSILON)
        second[r, :] = (res * scale * gain2[...]).astype(BF16)
        return 0
    lax.fori_loop(0, rows // 256, close, 0)
    for t in range(done, 2 * levels + 5): run(t)
    in_copy = pltpu.make_async_copy(w.at[1], in_o, store.at[4])
    in_copy.start()
    chunk = 512
    per = hidden // chunk
    def widen(i, _):
        slot = i % 2
        r = pl.ds(pl.multiple_of((i // per) * 256, 256), 256)
        c = pl.ds(pl.multiple_of((i % per) * chunk, chunk), chunk)
        gcopy = pltpu.make_async_copy(gp.at[slot], gp_o.at[r, c], gstore.at[slot])
        if comm:
            for t in range(max(done, 2 * levels + 5), len(steps)):
                @pl.when(i == 4 * (t - 2 * levels - 5 + 1))
                def _():
                    run(t)
        @pl.when(i >= 2)
        def _():
            gcopy.wait()
        a, grad = gelu_both(mm(second[r, :], w[1, :, c]))
        act[r, c] = a.astype(BF16)
        gp[slot] = grad.astype(BF16)
        gcopy.start()
        return 0
    lax.fori_loop(0, rows // 256 * per, widen, 0)
    act_copy = pltpu.make_async_copy(act, act_o, store.at[5])
    act_copy.start()
    back_copy = pltpu.make_async_copy(w.at[2], back_o, store.at[6])
    back_copy.start()
    def narrow(i, _):
        r = pl.ds(pl.multiple_of(i * 256, 256), 256)
        out[r, :] = (res_o[r, :] + mm(act[r, :], w[2], NT)).astype(out.dtype)
        return 0
    lax.fori_loop(0, rows // 256, narrow, 0)
    for c in [proj_copy, mixed_copy, *ctx_copies, in_copy, act_copy, back_copy]: c.wait()
    for slot in range(2):
        pltpu.make_async_copy(e.at[slot], e_o.at[0], estore.at[slot]).wait()
        pltpu.make_async_copy(gp.at[slot], gp_o.at[pl.ds(0, 256), pl.ds(0, chunk)], gstore.at[slot]).wait()
    if comm:
        for u in range(3): g.sendwait(u)

def forward(levels, comm, tok, seg, gains, table, weights, schedule=()):
    rows, width = tok.shape
    heads = table.shape[1]
    inner = heads * HD
    hidden = weights[2].shape[1] * (8 if comm else 1)
    seqs, pairs = rows // SEQ, heads // 2
    sds = jax.ShapeDtypeStruct
    vm, hb = pl.BlockSpec(memory_space=pltpu.VMEM), pl.BlockSpec(memory_space=pl.ANY)
    outs = [(sds((rows, width), BF16), vm), (sds((width, 4 * inner), BF16), hb), (sds((width, hidden), BF16), hb), (sds((width, hidden), BF16), hb),
            (sds((rows, 3 * inner), BF16), hb), (sds((seqs * pairs, 2, SEQ, SEQ), BF16), hb), (sds((seqs * heads, 8, SEQ), F32), vm), (sds((rows, inner), BF16), hb), (sds((inner, rows), BF16), hb),
            (sds((rows, width), F32), vm), (sds((rows, hidden), BF16), hb), (sds((rows, hidden), BF16), hb)]
    scratch = [pltpu.VMEM((3, width, hidden), BF16), pltpu.VMEM((width, 4 * inner), BF16), pltpu.VMEM((rows, width), BF16), pltpu.VMEM((rows, 3 * inner), BF16),
               pltpu.VMEM((heads, EDGE, 2 * SEQ - EDGE), F32), pltpu.VMEM((seqs, SEQ, SEQ), F32), pltpu.VMEM((2, 2, SEQ, SEQ), BF16),
               pltpu.VMEM((rows, inner), BF16), pltpu.VMEM((inner, rows), BF16), pltpu.VMEM((rows, hidden), BF16), pltpu.VMEM((2, 256, 512), BF16), pltpu.VMEM((rows, width), BF16),
               pltpu.SemaphoreType.DMA((4,)), pltpu.SemaphoreType.DMA((7,)), pltpu.SemaphoreType.DMA((2,)), pltpu.SemaphoreType.DMA((2,))]
    if comm:
        scratch += gather_sems(3, levels) + [pltpu.VMEM((3, *weights[2].shape), BF16)]
    args = [tok, seg, gains, jnp.pad(table.T, ((0, -heads % 16), (0, 0))), *weights]
    specs = [vm] * 4 + [vm if comm else hb] * 4
    params = dict(collective_id=0, has_side_effects=True) if comm else {}
    return pl.pallas_call(functools.partial(forward_kernel, levels, comm, schedule), out_shape=[o[0] for o in outs], in_specs=specs, out_specs=[o[1] for o in outs],
        scratch_shapes=scratch, compiler_params=pltpu.CompilerParams(vmem_limit_bytes=63 << 20, **params), name="forward")(*args)

def transpose_into(src, dst):
    n, w = src.shape
    def one(i, _):
        r = pl.ds(pl.multiple_of(i * 128, 128), 128)
        for c in range(w // 128):
            dst[c * 128 : (c + 1) * 128, r] = src[r, c * 128 : (c + 1) * 128].T
        return 0
    lax.fori_loop(0, n // 128, one, 0)

def norm_back(v, dy, gain):
    r = lax.rsqrt(jnp.mean(v * v, axis=1, keepdims=True) + EPSILON)
    unit = v * r
    a = dy * gain
    part = r * (a - unit * jnp.mean(a * unit, axis=1, keepdims=True))
    return part, jnp.sum(dy * unit, axis=0, keepdims=True), unit

def backward_kernel(levels, comm, plan, gains, rl, tok_h, cot_h, proj_h, in_h, back_h, mixed_h, e_h, ctx_h, ctxt_h, res_h, act_h, gp_h, *rest):
    if comm:
        (tg_o, small_o, qkv_o, out_o, gin_o, gback_o), rest = rest[:6], rest[6:]
    else:
        (tg_o, small_o, proj_o, gin_o, gback_o), rest = rest[:5], rest[5:]
    (u1, u2, b, t, f, e, qkv, racc, far, own, staged, load, stream, eload, qload, store), rest = rest[:16], rest[16:]
    gain1, gain2 = gains.at[0:1], gains.at[1:2]
    rows, width = f.shape[1], f.shape[2]
    hidden = u1.shape[1]
    inner = width
    heads = racc.shape[0]
    pairs, seqs = heads // 2, rows // SEQ
    small, rest = rest[:5], rest[5:]
    def local(src, dst, sem):
        return pltpu.make_async_copy(src, dst, sem)
    loads = {"cot": local(cot_h, f.at[2], load.at[0]), "back": local(back_h, u1, load.at[1]), "res": local(res_h, f.at[0], load.at[2]), "in": local(in_h, u2, load.at[3])}
    chunk = hidden // 4
    if comm:
        cross, free = rest[:9], rest[9]
        me = Place()
        order = (me.gd, me.xd, me.yd, me.d)
        cols = [pl.ds(pl.multiple_of((o // 2) * chunk, chunk), chunk) for o in order]
    else:
        cols = [pl.ds(q * chunk, chunk) for q in range(4)]
    def act_load(q):
        return local(act_h.at[:, cols[q]], b.at[1 + q % 2], stream.at[0, q % 2])
    def gp_load(q):
        return local(gp_h.at[:, cols[q]], b.at[3 + q % 2], stream.at[1, q % 2])
    loads["cot"].start()
    act_load(0).start()
    loads["res"].start()
    loads["back"].start()
    gp_load(0).start()
    act_load(1).start()
    loads["in"].start()
    gp_load(1).start()
    if comm:
        greet_all(me, levels)
        sc = Scatter(me, levels, width // levels, own.shape[3], own, staged, u2, *cross)
        sm = Small(me, levels, *small)
        mine = sm.mine.at[0]
    else:
        mine = small[0].at[0]
    mine[...] = jnp.zeros(mine.shape, F32)
    racc[...] = jnp.zeros(racc.shape, F32)
    far[...] = jnp.zeros(far.shape, F32)
    loads["cot"].wait()
    def lower(i, _):
        r = pl.ds(pl.multiple_of(i * 128, 128), 128)
        b[0, r, :] = f[2, r, :].astype(BF16)
        return 0
    lax.fori_loop(0, rows // 128, lower, 0)
    transpose_into(b.at[0], t.at[0])
    loads["res"].wait()
    def renorm(i, _):
        r = pl.ds(pl.multiple_of(i * 128, 128), 128)
        v = f[0, r, :]
        s = lax.rsqrt(jnp.mean(v * v, axis=1, keepdims=True) + EPSILON)
        b[5, r, :] = (v * s * gain2[...]).astype(BF16)
        return 0
    lax.fori_loop(0, rows // 128, renorm, 0)
    transpose_into(b.at[5], t.at[1])
    half = chunk // 2
    def weight_grad(u, q, left, right):
        def one(i, _):
            r = pl.ds(pl.multiple_of(i * 256, 256), 256)
            g = mm(left[r, :], right[...]).astype(BF16)
            if comm:
                mine_first = me.c == 0
                own[u, q, r, :] = jnp.where(mine_first, g[:, :half], g[:, half:])
                staged[u, q % 2, r, :] = jnp.where(mine_first, g[:, half:], g[:, :half])
            else:
                own[u, q, r, :] = g[:, :half]
                staged[u, q % 2, r, :] = g[:, half:]
            return 0
        if q >= 2:
            if comm:
                sc.ccopy(u, q - 2).wait_send()
            else:
                put(u, q - 2)[1].wait()
        lax.fori_loop(0, width // 256, one, 0)
        if comm:
            sc.core_start(u, q)
        else:
            for c in put(u, q): c.start()
    def put(u, q):
        dst = (gback_o, gin_o)[u]
        return (local(own.at[u, q], dst.at[:, pl.ds(q * chunk, half)], store.at[u, 0, q]), local(staged.at[u, q % 2], dst.at[:, pl.ds(q * chunk + half, half)], store.at[u, 1, q]))
    def event(name, *a):
        if comm: getattr(sc, name)(*a)
    for q in range(4):
        act, gp = b.at[1 + q % 2], b.at[3 + q % 2]
        act_load(q).wait()
        weight_grad(0, q, t.at[0], act)
        if q + 2 < 4: act_load(q + 2).start()
        if q == 0: loads["back"].wait()
        gp_load(q).wait()
        def widen(i, _):
            r = pl.ds(pl.multiple_of(i * 256, 256), 256)
            b[5, r, :] = (mm(b[0, r, :], u1[:, cols[q]]) * gp[r, :].astype(F32)).astype(BF16)
            return 0
        lax.fori_loop(0, rows // 256, widen, 0)
        if q + 2 < 4: gp_load(q + 2).start()
        if q == 3:
            proj_load = local(proj_h, u1, load.at[4])
            proj_load.start()
        event("core_add", 0, q)
        weight_grad(1, q, t.at[1], b.at[5])
        if q == 0: loads["in"].wait()
        def narrow(i, _):
            r = pl.ds(pl.multiple_of(i * 256, 256), 256)
            g = mm(b[5, r, :], u2[:, cols[q]], NT)
            f[1, r, :] = g if q == 0 else f[1, r, :] + g
            return 0
        lax.fori_loop(0, rows // 256, narrow, 0)
        event("core_add", 1, q)
        if q == 2: event("cross_one", 0)
        if q == 3: event("cross_one", 1)
    ctx_loads = [local(ctx_h, b.at[5], load.at[5]), local(ctxt_h, t.at[2], load.at[6])]
    for c in ctx_loads: c.start()
    def norm_two(i, total):
        r = pl.ds(pl.multiple_of(i * 128, 128), 128)
        part, g, _ = norm_back(f[0, r, :], f[1, r, :], gain2[...])
        grad = f[2, r, :] + part
        f[0, r, :] = grad
        b[0, r, :] = grad.astype(BF16)
        return total + g
    mine[1:2, :] = lax.fori_loop(0, rows // 128, norm_two, jnp.zeros((1, width), F32))
    transpose_into(b.at[0], t.at[0])
    proj_load.wait()
    def context_back(i, _):
        r = pl.ds(pl.multiple_of(i * 256, 256), 256)
        b[4, r, :] = mm(b[0, r, :], u1[:, 3 * inner :]).astype(BF16)
        return 0
    lax.fori_loop(0, rows // 256, context_back, 0)
    for c in ctx_loads: c.wait()
    def out_grad(i, _):
        r = pl.ds(pl.multiple_of(i * 256, 256), 256)
        b[6, r, :] = mm(t[0, r, :], b[5]).astype(BF16)
        return 0
    lax.fori_loop(0, width // 256, out_grad, 0)
    tok_load = local(tok_h, b.at[0], load.at[7])
    tok_load.start()
    tok_load.wait()
    def renorm_one(i, _):
        r = pl.ds(pl.multiple_of(i * 128, 128), 128)
        v = b[0, r, :].astype(F32)
        s = lax.rsqrt(jnp.mean(v * v, axis=1, keepdims=True) + EPSILON)
        b[5, r, :] = (v * s * gain1[...]).astype(BF16)
        return 0
    lax.fori_loop(0, rows // 128, renorm_one, 0)
    transpose_into(b.at[5], t.at[1])
    n = seqs * pairs
    def fetch(i, slot):
        s, p = i // pairs, i % pairs
        row = pl.ds(pl.multiple_of(s * SEQ, SEQ), SEQ)
        return [local(e_h.at[i], e.at[slot], eload.at[slot])] + [
            local(mixed_h.at[row, pl.ds(pl.multiple_of(k * inner + p * 128, 128), 128)], qkv.at[slot, k], qload.at[slot, k]) for k in range(3)]
    for c in fetch(0, 0): c.start()
    low_lanes = lax.broadcasted_iota(jnp.int32, (SEQ, 128), 1) < HD
    blocks = SEQ // EDGE
    def attend_back(i, _):
        s, p = i // pairs, i % pairs
        slot = i % 2
        @pl.when(i + 1 < n)
        def _():
            for c in fetch(i + 1, (i + 1) % 2): c.start()
        for at, name, args in plan:
            @pl.when(i == at)
            def _():
                event(name, *args)
        for c in fetch(i, slot): c.wait()
        row = pl.ds(pl.multiple_of(s * SEQ, SEQ), SEQ)
        off = pl.multiple_of(p * 128, 128)
        q, k, v = qkv[slot, 0] * jnp.asarray(SCALING, BF16), qkv[slot, 1], qkv[slot, 2]
        k_t = k.T
        do_t = b[4, row, pl.ds(off, 128)].T.astype(F32)
        o_t = t[2, pl.ds(off, 128), row].astype(F32)
        scaled = []
        for a in range(2):
            part = do_t[a * HD : (a + 1) * HD] * rl[s * heads + 2 * p + a, :1, :]
            scaled.append(part.astype(BF16))
        dos_t = jnp.concatenate(scaled, axis=0)
        dos = dos_t.T
        prod = dos_t.astype(F32) * o_t
        dq, dk, dv = [], [], []
        for a in range(2):
            h = 2 * p + a
            delta = jnp.sum(prod[a * HD : (a + 1) * HD], axis=0, keepdims=True)
            va = jnp.where(low_lanes == (a == 0), v, jnp.zeros_like(v))
            low = []
            sums = [None] * 3
            fars = [None] * 2
            for kb in range(blocks):
                ek = e[slot, a, kb * EDGE : (kb + 1) * EDGE, :]
                ds = ek.astype(F32) * (mm(va[kb * EDGE : (kb + 1) * EDGE], dos_t) - delta)
                low.append(ds.astype(BF16))
                for qb in range(blocks):
                    piece = ds[:, qb * EDGE : (qb + 1) * EDGE]
                    gap = kb - qb
                    if abs(gap) <= 1:
                        sums[gap + 1] = piece if sums[gap + 1] is None else sums[gap + 1] + piece
                    else:
                        w = 1 if gap > 0 else 0
                        piece = jnp.sum(piece.reshape(EDGE // 8, 8, EDGE), axis=0)
                        fars[w] = piece if fars[w] is None else fars[w] + piece
            for w in range(3):
                racc[h, w] += sums[w]
            for w in range(2):
                far[h, w] += fars[w]
            low = jnp.concatenate(low, axis=0)
            dv.append(mm(e[slot, a], dos))
            dk.append(mm(low, q))
            dq.append(mm(k_t[a * HD : (a + 1) * HD], low))
        b[1, row, pl.ds(off, 128)] = (jnp.concatenate(dq, axis=0) * SCALING).astype(BF16).T
        b[2, row, pl.ds(off, 128)] = jnp.where(low_lanes, dk[0], dk[1]).astype(BF16)
        b[3, row, pl.ds(off, 128)] = jnp.where(low_lanes, dv[0], dv[1]).astype(BF16)
        return 0
    lax.fori_loop(0, n, attend_back, 0)
    if comm:
        for u in range(2):
            (gback_o, gin_o)[u][...] = sc.finish(u)
        for u in range(2): sc.sendwait(u)
        sc.release(free)
    part, packed = own.shape[3] * 3 // 4, own.shape[3]
    def proj_grad(i, _):
        r = pl.ds(pl.multiple_of(i * 256, 256), 256)
        left = t[1, r, :]
        g = jnp.concatenate([mm(left, b[1 + k]).astype(BF16) for k in range(3)], axis=1)
        o = b[6, r, :]
        if comm:
            quarter = packed - part
            for d in range(hidden // packed):
                u2[r, d * packed : (d + 1) * packed] = jnp.concatenate([g[:, d * part : (d + 1) * part], o[:, d * quarter : (d + 1) * quarter]], axis=1)
        else:
            u2[r, : 3 * inner] = g
            u2[r, 3 * inner :] = o
        return 0
    lax.fori_loop(0, width // 256, proj_grad, 0)
    if comm:
        sc.acquire(free)
        for q in range(4): sc.core_start(2, q)
        for q in range(4): sc.core_add(2, q)
    else:
        proj_put = local(u2, proj_o, store.at[0, 0, 4])
        proj_put.start()
    span = 2 * EDGE
    c = lax.broadcasted_iota(jnp.int32, (span, 128), 0)
    offs = EDGE - 1 - c
    bucket_lane = lax.broadcasted_iota(jnp.int32, (span, 128), 1)
    hots = [(bucket_of(offs + EDGE * w) == bucket_lane).astype(F32) for w in (-1, 0, 1)]
    lane = lax.broadcasted_iota(jnp.int32, (1, 128), 1)
    mirror = (lax.broadcasted_iota(jnp.int32, (EDGE, EDGE), 0) + lax.broadcasted_iota(jnp.int32, (EDGE, EDGE), 1) == EDGE - 1).astype(F32)
    at_row = lax.broadcasted_iota(jnp.int32, (16, 128), 0)
    def table_one(h, held):
        total = jnp.zeros((8, 128), F32)
        for w in range(3):
            upended = lax.dot_general(mirror, racc[h, w], NN, precision=lax.Precision.HIGHEST, preferred_element_type=F32)
            wide = jnp.concatenate([upended, jnp.zeros((EDGE, EDGE), F32)], axis=1)
            turned = pltpu.roll(wide, 0, 1, stride=1, stride_axis=0)
            diag = jnp.sum(turned.reshape(EDGE // 8, 8, span), axis=0)
            total = total + lax.dot_general(diag, hots[w], NN, precision=lax.Precision.HIGHEST, preferred_element_type=F32)
        row = jnp.sum(total, axis=0, keepdims=True)
        left = jnp.sum(far[h, 0])
        right = jnp.sum(far[h, 1])
        row = row + jnp.where(lane == BUCKETS // 2 - 1, left, 0.0) + jnp.where(lane == BUCKETS - 1, right, 0.0)
        return held + jnp.where(at_row == 2 + h, row, 0.0)
    mine[:, :128] += lax.fori_loop(0, heads, table_one, jnp.zeros((16, 128), F32))
    if comm: sc.cross_one(2)
    def norm_one(i, total):
        r = pl.ds(pl.multiple_of(i * 256, 256), 256)
        dy = mm(b[1, r, :], u1[:, :inner], NT) + mm(b[2, r, :], u1[:, inner : 2 * inner], NT) + mm(b[3, r, :], u1[:, 2 * inner : 3 * inner], NT)
        part, g, _ = norm_back(b[0, r, :].astype(F32), dy, gain1[...])
        f[1, r, :] = f[0, r, :] + part
        return total + g
    mine[0:1, :] = lax.fori_loop(0, rows // 256, norm_one, jnp.zeros((1, width), F32))
    tg_copy = local(f.at[1], tg_o, load.at[8])
    tg_copy.start()
    if comm:
        sm.start(0)
        sm.add(0); sm.start(1)
        sc.cross_two(2)
        sm.add(1); sm.start(2)
        sc.cross_three(2)
        sc.line_open(2)
        sm.add(2); sm.spread()
        for k in range(1, levels): sc.line_step(2, k)
        total = sc.finish(2)
        qkv_o[...] = total[:, :part]
        out_o[...] = total[:, part:]
        small_o[...] = sm.total()
        sc.sendwait(2)
        sm.sendwait()
    else:
        small_o[...] = mine[...]
        for u in range(2):
            for q in range(4):
                x, y = put(u, q)
                x.wait()
                if q >= 2: y.wait()
        proj_put.wait()
    tg_copy.wait()

def backward(levels, comm, plan, gains, rl, tok, cot, proj, w_in, w_back, mixed, e, ctx, ctxt, res, act, gp, share=None):
    rows, width = tok.shape
    hidden = w_in.shape[1]
    heads = rl.shape[0] // (rows // SEQ)
    sds = jax.ShapeDtypeStruct
    vm, hb = pl.BlockSpec(memory_space=pltpu.VMEM), pl.BlockSpec(memory_space=pl.ANY)
    shape = (16, width)
    half = hidden // 8
    piece_rows = width // levels
    outs = [(sds((rows, width), F32), hb), (sds(shape, F32), vm)]
    if comm:
        outs += [(sds((piece_rows, half * 3 // 4), F32), vm), (sds((piece_rows, half // 4), F32), vm), (sds((piece_rows, half), F32), vm), (sds((piece_rows, half), F32), vm)]
    else:
        outs += [(sds((width, hidden), BF16), hb)] * 3
    D = pltpu.SemaphoreType.DMA
    scratch = [pltpu.VMEM((width, hidden), BF16), pltpu.VMEM((width, hidden), BF16), pltpu.VMEM((7, rows, width), BF16), pltpu.VMEM((3, width, rows), BF16), pltpu.VMEM((3, rows, width), F32),
               pltpu.VMEM((2, 2, SEQ, SEQ), BF16), pltpu.VMEM((2, 3, SEQ, 128), BF16), pltpu.VMEM((heads, 3, EDGE, EDGE), F32), pltpu.VMEM((heads, 2, 8, EDGE), F32),
               pltpu.VMEM((2, 4, width, half), BF16), pltpu.VMEM((2, 2, width, half), BF16), D((9,)), D((2, 2)), D((2,)), D((2, 3)), D((2, 2, 5))] + small_scratch(levels, shape)
    if comm:
        scratch += [pltpu.VMEM((2, 4, width, half), BF16), pltpu.VMEM((2, 2, 3, width // 2, half), BF16), pltpu.VMEM((2, 2, levels - 1, piece_rows, half), BF16),
                    D((3, 4)), D((3, 4)), D((3, 2, 3)), D((3, 2, 3)), D((3, 2, levels - 1)), D((3, 2, levels - 1)), pltpu.SemaphoreType.REGULAR]
    params = dict(collective_id=1, has_side_effects=True) if comm else {}
    return pl.pallas_call(functools.partial(backward_kernel, levels, comm, plan), out_shape=[o[0] for o in outs], in_specs=[vm] * 2 + [hb] * 12, out_specs=[o[1] for o in outs],
        scratch_shapes=scratch, compiler_params=pltpu.CompilerParams(vmem_limit_bytes=63 << 20, **params), name="backward")(gains, rl, tok, cot, proj, w_in, w_back, mixed, e, ctx, ctxt, res, act, gp)

def scatter_plain(grad):
    part = lax.psum_scatter(grad, "dp", scatter_dimension=1, tiled=True)
    return lax.psum_scatter(part, "mp", scatter_dimension=0, tiled=True).astype(F32)


FORWARD_PLAN = ((8, 1), (9, 4), (10, 6), (11, 8), (12, 10))
BACKWARD_PLAN = (
    (0, "cross_two", (0,)), (1, "cross_two", (1,)), (3, "cross_three", (0,)), (3, "line_open", (0,)), (4, "line_step", (0, 1)),
    (5, "cross_three", (1,)), (5, "line_open", (1,)), (6, "line_step", (0, 2)), (7, "line_step", (1, 1)), (8, "line_step", (0, 3)),
    (9, "line_step", (1, 2)), (11, "line_step", (1, 3)),
)


def body(tokens, segment_ids, cotangent, gain_one, w_qkv, w_out, rel_table, gain_two, w_in, w_back):
    axes = ("mp", "dp")
    levels, width = lax.axis_size("mp"), lax.axis_size("dp")
    heads = rel_table.shape[1]
    inner = heads * HD
    segments = segment_ids.reshape(-1, SEQ).astype(F32)
    packed = w_qkv.shape[1] + w_out.shape[1]
    own = width == 8 and levels == 4 and packed == w_in.shape[1] and packed % 128 == 0
    gains = jnp.stack([gain_one, gain_two]).astype(F32)
    weights = [w_qkv, w_out, w_in, w_back]
    if not own:
        weights = [lax.all_gather(lax.all_gather(m, "mp", axis=0, tiled=True), "dp", axis=1, tiled=True) for m in weights]
    held = forward(levels, own, tokens, segments, gains, rel_table, weights, FORWARD_PLAN)
    layer_out, proj, full_in, full_back, mixed, e, rl, ctx, ctxt, res, act, gp = held
    grads = backward(levels, own, BACKWARD_PLAN, gains, rl, tokens, cotangent, proj, full_in, full_back, mixed, e, ctx, ctxt, res, act, gp)
    if own:
        tokens_grad, small, qkv_grad, out_grad, in_grad, back_grad = grads
    else:
        tokens_grad, small, proj_grad, in_grad, back_grad = grads
        small = lax.psum(small, axes)
        qkv_grad, out_grad = scatter_plain(proj_grad[:, : 3 * inner]), scatter_plain(proj_grad[:, 3 * inner :])
        in_grad, back_grad = scatter_plain(in_grad), scatter_plain(back_grad)
    table_grad = small[2 : 2 + heads, :BUCKETS].T
    return layer_out, tokens_grad, small[0], qkv_grad, out_grad, table_grad, small[1], in_grad, back_grad


def solution(mesh):
    both = ("mp", "dp")
    weight = P("mp", "dp")
    return jax.shard_map(
        body,
        mesh=mesh,
        in_specs=(P(both, None), P(both), P(both, None), P(), weight, weight, P(), P(), weight, weight),
        out_specs=(P(both, None), P(both, None), P(), weight, weight, P(), P(), weight, weight),
        check_vma=False,
    )
```
